32 devices in a mesh: grp: 2 (over core), exp: 4 (over y, x), shd: 4 (over z).
Axes of the slice: x: 2, y: 2, z: 4, core: 2. Of those that a mesh axis runs over, the one named last changes fastest.
Arguments:
- tokens_in: bfloat16 [32, 1024, 768], P(('grp', 'exp', 'shd')), may hold values from -6 to 6
- cotangent: bfloat16 [32, 1024, 768], P(('grp', 'exp', 'shd')), may hold values from -6 to 6
- block_ids: int32 [32, 1024], P(('grp', 'exp', 'shd')), may hold values from 0 to 7, never falling along the last dimension, each value on 1 to 256 neighbouring positions
- expert_ids: int32 [32, 1024, 2], P(('grp', 'exp', 'shd')), may hold values from 0 to 3, all different within a row; in each aligned block of 1024 rows (0 to 1023, 1024 to 2047, ..., all dimensions but the last counted through in order) at most 640 rows name the same one
- scales: float32 [2, 768], P(None, ('exp', 'shd')), may hold values from 0.5 to 1.5
- moment_scales: float32 [2, 768], P(None, ('exp', 'shd')), may hold values from -128 to 128
- square_scales: float32 [2, 768], P(None, ('exp', 'shd')), may hold values from 1736.704 to 6881.28
- attend: float32 [3, 768, 768], P(None, ('exp', 'shd')), may hold values from -0.21875 to 0.21875
- moment_attend: float32 [3, 768, 768], P(None, ('exp', 'shd')), may hold values from -64 to 64
- square_attend: float32 [3, 768, 768], P(None, ('exp', 'shd')), may hold values from 425.984 to 1736.704
- output: float32 [768, 768], P(('exp', 'shd')), may hold values from -1.75 to 1.75
- moment_output: float32 [768, 768], P(('exp', 'shd')), may hold values from -7 to 7
- square_output: float32 [768, 768], P(('exp', 'shd')), may hold values from 6.22592 to 24.90368
- router: float32 [768, 4], P(('exp', 'shd')), may hold values from -0.21875 to 0.21875
- moment_router: float32 [768, 4], P(('exp', 'shd')), may hold values from -320 to 320
- square_router: float32 [768, 4], P(('exp', 'shd')), may hold values from 13337.887 to 52848.23
- widener: float32 [2, 768, 2048], P(None, ('exp', 'shd')), may hold values from -0.21875 to 0.21875
- moment_widener: float32 [2, 768, 2048], P(None, ('exp', 'shd')), may hold values from -64 to 64
- square_widener: float32 [2, 768, 2048], P(None, ('exp', 'shd')), may hold values from 425.984 to 1736.704
- reducer: float32 [2048, 768], P(('exp', 'shd')), may hold values from -0.125 to 0.125
- moment_reducer: float32 [2048, 768], P(('exp', 'shd')), may hold values from -64 to 64
- square_reducer: float32 [2048, 768], P(('exp', 'shd')), may hold values from 425.984 to 1736.704
- experts: float32 [4, 2, 768, 2048], P('exp', None, 'shd'), may hold values from -0.21875 to 0.21875
- moment_experts: float32 [4, 2, 768, 2048], P('exp', None, 'shd'), may hold values from -24 to 24
- square_experts: float32 [4, 2, 768, 2048], P('exp', None, 'shd'), may hold values from 68.8128 to 278.528
- narrower: float32 [4, 2048, 768], P('exp', 'shd'), may hold values from -0.125 to 0.125
- moment_narrower: float32 [4, 2048, 768], P('exp', 'shd'), may hold values from -16 to 16
- square_narrower: float32 [4, 2048, 768], P('exp', 'shd'), may hold values from 39.3216 to 157.2864
Outputs:
- block_out: bfloat16 [32, 1024, 768], P(('grp', 'exp', 'shd'))
- input_grad: float32 [32, 1024, 768], P(('grp', 'exp', 'shd'))
- weight_scales: float32 [2, 768], P(None, ('exp', 'shd'))
- first_scales: float32 [2, 768], P(None, ('exp', 'shd'))
- second_scales: float32 [2, 768], P(None, ('exp', 'shd'))
- weight_attend: float32 [3, 768, 768], P(None, ('exp', 'shd'))
- first_attend: float32 [3, 768, 768], P(None, ('exp', 'shd'))
- second_attend: float32 [3, 768, 768], P(None, ('exp', 'shd'))
- weight_output: float32 [768, 768], P(('exp', 'shd'))
- first_output: float32 [768, 768], P(('exp', 'shd'))
- second_output: float32 [768, 768], P(('exp', 'shd'))
- weight_router: float32 [768, 4], P(('exp', 'shd'))
- first_router: float32 [768, 4], P(('exp', 'shd'))
- second_router: float32 [768, 4], P(('exp', 'shd'))
- weight_widener: float32 [2, 768, 2048], P(None, ('exp', 'shd'))
- first_widener: float32 [2, 768, 2048], P(None, ('exp', 'shd'))
- second_widener: float32 [2, 768, 2048], P(None, ('exp', 'shd'))
- weight_reducer: float32 [2048, 768], P(('exp', 'shd'))
- first_reducer: float32 [2048, 768], P(('exp', 'shd'))
- second_reducer: float32 [2048, 768], P(('exp', 'shd'))
- weight_experts: float32 [4, 2, 768, 2048], P('exp', None, 'shd')
- first_experts: float32 [4, 2, 768, 2048], P('exp', None, 'shd')
- second_experts: float32 [4, 2, 768, 2048], P('exp', None, 'shd')
- weight_narrower: float32 [4, 2048, 768], P('exp', 'shd')
- first_narrower: float32 [4, 2048, 768], P('exp', 'shd')
- second_narrower: float32 [4, 2048, 768], P('exp', 'shd')
The draws below stay inside these ranges and needn't reach their ends.
Inputs may be any that keep to these rules, and one draw needn't show every extreme that they name: `expert_ids`: each token names 2 different experts; of the 1024 tokens of one sequence no expert is named by more than 640, a bound that some block reaches. `block_ids`: never falls along a sequence; each block holds 1 to 256 tokens.
All inputs are finite; a program needn't handle non-finite values.
Results may differ from the reference program's by a relative error of at most 0.014.
The reference program's roundings to bfloat16 on the way count: a program that leaves them out, or rounds other values in their place, can miss the bound.
Values may be sent and summed in bfloat16 or wider, within the bound.
A program may use at most 768 MiB of HBM per device.

```python
import math
import jax
import jax.numpy as jnp
import numpy as np
from jax import lax

D = 768
HEADS = 12
HEAD_DIM = 64
FF = 2048
SEQ = 1024
BLK = 256
TOP = 2
EXPERTS = 4
SEQS = 32
CAP = 576
MOST = 640


def block_levels(own_key, extent, pieces, low, top_value):
    def one(position, blocks):
        heights = jax.random.uniform(jax.random.fold_in(jax.random.fold_in(own_key, 6), position), (blocks,), jnp.float32, low / len(pieces), top_value / len(pieces))
        return jnp.repeat(jnp.exp(heights), extent[position] // blocks).reshape((-1,) + (1,) * (len(extent) - position - 1))

    loudness = one(*pieces[0])
    for cut in pieces[1:]:
        loudness = loudness * one(*cut)
    return loudness


def profile(number_of, total, reach, slope):
    portions = [(1 << 20) // math.isqrt(standing ** slope) + 1 for standing in range(2, number_of + 1)]
    surplus, counts = total - reach - (number_of - 1), [1] * (number_of - 1)
    while surplus > 0:
        candidates = [i for i in range(number_of - 1) if counts[i] < reach]
        mass, remaining = sum([portions[i] for i in candidates]), surplus
        for i in candidates:
            addition = min(reach - counts[i], max(1, remaining * portions[i] // mass), surplus)
            counts[i] = counts[i] + addition
            surplus = surplus - addition
    return np.array([reach] + counts)


def uneven_parts(rng, number_of, total, most, lean):
    if number_of == 2:
        one = jax.random.randint(rng, (), max(1, total - most), min(most, total - 1) + 1)
        return jnp.stack([one, total - one])
    sizes = jnp.asarray(profile(number_of, total, most, lean), jnp.int32)
    pairs = (number_of - 1) // 2
    donor, sink = sizes[1:1 + 2 * pairs:2], sizes[2:2 + 2 * pairs:2]
    margin = jnp.minimum(donor - 1, most - sink)
    shifted = jax.random.randint(jax.random.fold_in(rng, 1), (pairs,), 0, 1 << 20) % (margin + 1)
    sizes = sizes.at[1:1 + 2 * pairs:2].set(donor - shifted).at[2:2 + 2 * pairs:2].set(sink + shifted)
    return sizes[jax.random.permutation(jax.random.fold_in(rng, 2), number_of)]


def routed_block(own_key, own, number, rows, count, top, bound, skew):
    ranking = jax.random.permutation(own_key, count)
    heavy_load, usual = portions_of(count, rows * top, bound, skew, True), portions_of(count, rows * top, bound, skew, False)
    places = jnp.arange(count)

    def named(tallies, turn):
        used = int((tallies > 0).sum())
        fixed = max(1, used // 4)
        passed = fixed + (places - fixed + turn * (used - fixed)) % max(1, count - fixed)
        return jnp.zeros((count,), jnp.int32).at[ranking[jnp.where(places < fixed, places, passed)]].set(jnp.asarray(tallies, jnp.int32))

    tallies = jnp.where(number % 4 == 0, named(heavy_load, number // 4), named(usual, number - number // 4 - 1))
    mixed = jax.random.permutation(jax.random.fold_in(own, 3), count)
    donor, taker = mixed[0:count // 2 * 2:2], mixed[1:count // 2 * 2:2]
    margin = jnp.minimum(tallies[donor] - 1, bound - tallies[taker]) // 2
    margin = jnp.where((donor == ranking[0]) | (taker == ranking[0]) | (tallies[taker] == 0), 0, jnp.maximum(margin, 0))
    passed = jax.random.randint(jax.random.fold_in(own, 4), (count // 2,), 0, 1 << 20) % (margin + 1)
    tallies = tallies.at[donor].add(-passed).at[taker].add(passed)
    labels = jnp.searchsorted(jnp.cumsum(tallies), jnp.arange(rows * top), side="right").astype(jnp.int32)
    grid = labels.reshape(top, rows).T
    grid = grid[jax.random.permutation(jax.random.fold_in(own, 1), rows)]
    turn = jax.random.randint(jax.random.fold_in(own, 2), (rows, 1), 0, top)
    return jnp.take_along_axis(grid, (jnp.arange(top)[None, :] + turn) % top, axis=1)


def portions_of(number_of, total, limit, skew, full):
    loads = [(1 << 20) // math.isqrt(rank ** skew) + 1 for rank in range(1, number_of + 1)]
    largest = limit if full else min(limit, max(-(-total // number_of), total * loads[0] // sum(loads)))
    least = 1 if total - largest >= number_of - 1 else 0
    counts, rest = [largest] + [least] * (number_of - 1), total - largest - least * (number_of - 1)
    while rest > 0:
        movable = [i for i in range(1, number_of) if counts[i] < largest] or [i for i in range(1, number_of) if counts[i] < limit]
        mass, remaining = sum([loads[i] for i in movable]), rest
        for i in movable:
            more = min(limit - counts[i], max(1, remaining * loads[i] // mass), rest)
            counts[i] = counts[i] + more
            rest = rest - more
    return np.array(counts)


def gaussian(key, dims, deviation, reach, split=(), kind=jnp.bfloat16):
    values = deviation * jax.random.normal(key, dims, jnp.float32)
    if split:
        values = values * block_levels(key, dims, split, -0.22, 0.18)
    return jnp.clip(values, -reach, reach).astype(kind)


def setup_inputs(seed: int = 0) -> dict:
    key_of = jax.random.split(jax.random.key(seed), 29)
    tokens_in = gaussian(key_of[0], (SEQS, SEQ, D), 1.0, 6.0, ((0, 32),))
    cotangent = gaussian(key_of[1], (SEQS, SEQ, D), 1.0, 6.0, ((0, 32),))
    block_ids = jax.vmap(lambda own: jnp.searchsorted(jnp.cumsum(uneven_parts(own, 2 * SEQ // BLK, SEQ, BLK, 1)), jnp.arange(SEQ), side="right"))(jax.random.split(key_of[2], SEQS)).reshape((SEQS, SEQ)).astype(jnp.int32)
    expert_ids_keys = jax.random.split(jax.random.fold_in(key_of[3], 1), SEQS * SEQ // SEQ)
    expert_ids_turns = jax.random.permutation(jax.random.fold_in(key_of[3], 3), SEQS * SEQ // SEQ)
    expert_ids = jax.vmap(lambda own, number: routed_block(jax.random.fold_in(key_of[3], 2), own, number, SEQ, EXPERTS, TOP, MOST, 1))(expert_ids_keys, expert_ids_turns).reshape((SEQS, SEQ, TOP))
    scales = jnp.clip(1.0 + 0.1 * jax.random.normal(key_of[4], (2, D), jnp.float32), 0.5, 1.5)
    moment_scales = gaussian(key_of[5], (2, D), (0.11 * (SEQS * SEQ) ** 0.5), 128.0, ((1, 16),), jnp.float32)
    square_scales = jnp.clip(jnp.exp(math.log(6881.28) - 1.3768156 * jax.random.uniform(key_of[6], (2, D), jnp.float32) ** block_levels(key_of[6], (2, D), ((1, 16),), -0.2, 0.2)), 1736.704, 6881.28)
    attend = gaussian(key_of[7], (3, D, D), D ** -0.5, 0.21875, ((1, 16),), jnp.float32)
    moment_attend = gaussian(key_of[8], (3, D, D), (0.055 * (SEQS * SEQ) ** 0.5), 64.0, ((1, 16),), jnp.float32)
    square_attend = jnp.clip(jnp.exp(math.log(1736.704) - 1.40534252 * jax.random.uniform(key_of[9], (3, D, D), jnp.float32) ** block_levels(key_of[9], (3, D, D), ((1, 16),), -0.2, 0.2)), 425.984, 1736.704)
    output = gaussian(key_of[10], (D, D), (D // 64) ** -0.5, 1.75, ((0, 16),), jnp.float32)
    moment_output = gaussian(key_of[11], (D, D), (0.0066 * (SEQS * SEQ) ** 0.5), 7.0, ((0, 16),), jnp.float32)
    square_output = jnp.clip(jnp.exp(math.log(24.90368) - 1.3862944 * jax.random.uniform(key_of[12], (D, D), jnp.float32) ** block_levels(key_of[12], (D, D), ((0, 16),), -0.2, 0.2)), 6.22592, 24.90368)
    router = gaussian(key_of[13], (D, EXPERTS), D ** -0.5, 0.21875, ((0, 16),), jnp.float32)
    moment_router = gaussian(key_of[14], (D, EXPERTS), (0.011 * (D * SEQS * SEQ) ** 0.5), 320.0, ((0, 16),), jnp.float32)
    square_router = jnp.clip(jnp.exp(math.log(52848.23) - 1.37681562 * jax.random.uniform(key_of[15], (D, EXPERTS), jnp.float32) ** block_levels(key_of[15], (D, EXPERTS), ((0, 16),), -0.2, 0.2)), 13337.887, 52848.23)
    widener = gaussian(key_of[16], (2, D, FF), D ** -0.5, 0.21875, ((1, 16),), jnp.float32)
    moment_widener = gaussian(key_of[17], (2, D, FF), (0.055 * (SEQS * SEQ) ** 0.5), 64.0, ((1, 16),), jnp.float32)
    square_widener = jnp.clip(jnp.exp(math.log(1736.704) - 1.40534252 * jax.random.uniform(key_of[18], (2, D, FF), jnp.float32) ** block_levels(key_of[18], (2, D, FF), ((1, 16),), -0.2, 0.2)), 425.984, 1736.704)
    reducer = gaussian(key_of[19], (FF, D), FF ** -0.5, 0.125, ((0, 16),), jnp.float32)
    moment_reducer = gaussian(key_of[20], (FF, D), (0.055 * (SEQS * SEQ) ** 0.5), 64.0, ((0, 16),), jnp.float32)
    square_reducer = jnp.clip(jnp.exp(math.log(1736.704) - 1.40534252 * jax.random.uniform(key_of[21], (FF, D), jnp.float32) ** block_levels(key_of[21], (FF, D), ((0, 16),), -0.2, 0.2)), 425.984, 1736.704)
    experts = gaussian(key_of[22], (EXPERTS, 2, D, FF), D ** -0.5, 0.21875, ((0, 4), (2, 4)), jnp.float32)
    moment_experts = gaussian(key_of[23], (EXPERTS, 2, D, FF), (0.022 * (SEQS * SEQ) ** 0.5), 24.0, ((0, 4), (2, 4)), jnp.float32)
    square_experts = jnp.clip(jnp.exp(math.log(278.528) - 1.3981289 * jax.random.uniform(key_of[24], (EXPERTS, 2, D, FF), jnp.float32) ** block_levels(key_of[24], (EXPERTS, 2, D, FF), ((0, 4), (2, 4)), -0.2, 0.2)), 68.8128, 278.528)
    narrower = gaussian(key_of[25], (EXPERTS, FF, D), FF ** -0.5, 0.125, ((0, 4), (1, 4)), jnp.float32)
    moment_narrower = gaussian(key_of[26], (EXPERTS, FF, D), (0.0165 * (SEQS * SEQ) ** 0.5), 16.0, ((0, 4), (1, 4)), jnp.float32)
    square_narrower = jnp.clip(jnp.exp(math.log(157.2864) - 1.3862944 * jax.random.uniform(key_of[27], (EXPERTS, FF, D), jnp.float32) ** block_levels(key_of[27], (EXPERTS, FF, D), ((0, 4), (1, 4)), -0.2, 0.2)), 39.3216, 157.2864)
    return {"tokens_in": tokens_in, "cotangent": cotangent, "block_ids": block_ids, "expert_ids": expert_ids, "scales": scales, "moment_scales": moment_scales, "square_scales": square_scales, "attend": attend, "moment_attend": moment_attend, "square_attend": square_attend, "output": output, "moment_output": moment_output, "square_output": square_output, "router": router, "moment_router": moment_router, "square_router": square_router, "widener": widener, "moment_widener": moment_widener, "square_widener": square_widener, "reducer": reducer, "moment_reducer": moment_reducer, "square_reducer": square_reducer, "experts": experts, "moment_experts": moment_experts, "square_experts": square_experts, "narrower": narrower, "moment_narrower": moment_narrower, "square_narrower": square_narrower}


norm_eps = 1e-06
adam_eps = 1e-08
beta_one = 0.9
beta_two = 0.95
first_fix = 1.0 - 0.9 ** 10
second_fix = 1.0 - 0.95 ** 10
learning_rates = (0.3, 0.02, 0.15, 0.02, 0.02, 0.012, 0.02, 0.012)
decay_rates = (0.0, 0.1, 0.1, 0.1, 0.1, 0.1, 0.1, 0.1)
masked_score = -1e+30
highest = lax.Precision.HIGHEST

@jax.custom_vjp
def low(v):
    return lax.optimization_barrier(v.astype(jnp.bfloat16)).astype(jnp.float32)

@jax.custom_vjp
def low_back(v):
    return v

def low_keep(v):
    return (low(v), None)

def low_pass(kept, grad):
    return (grad,)

def back_keep(v):
    return (v, None)

def back_low(kept, grad):
    return (low(grad),)
low.defvjp(low_keep, low_pass)
low_back.defvjp(back_keep, back_low)

def matmul(matrix_one, matrix_two):
    return jnp.dot(matrix_one, matrix_two, precision=highest, preferred_element_type=jnp.float32)

def slot_tables(choices, experts_all, capacity):
    pair_count = choices.shape[0] * choices.shape[1]
    pair_expert = choices.reshape(pair_count).astype(jnp.int32)
    pair_hot = (pair_expert[:, None] == jnp.arange(experts_all, dtype=jnp.int32)[None, :]).astype(jnp.int32)
    before = jnp.cumsum(pair_hot, axis=0) - pair_hot
    placed = lax.optimization_barrier(jnp.sum(before * pair_hot, axis=1)).astype(jnp.int32)
    slot_id = jnp.where(placed < capacity, pair_expert * capacity + placed, experts_all * capacity).astype(jnp.int32)
    slot_pair = jnp.full((experts_all * capacity + 1,), pair_count, jnp.int32)
    slot_pair = slot_pair.at[slot_id].set(jnp.arange(pair_count, dtype=jnp.int32))
    return (slot_id, slot_pair[:experts_all * capacity])

def sequence_forward(params, tokens, blocks, choices):
    scales, attend, output, router, widener, reducer, experts, narrower = params
    seq_len = tokens.shape[0]
    first = lax.rsqrt(lax.optimization_barrier(jnp.mean(tokens * tokens, axis=1, keepdims=True)) + norm_eps)
    lifted = low(tokens * first * scales[0])
    queries = low(low_back(matmul(lifted, attend[0]))).reshape(seq_len, HEADS, HEAD_DIM)
    keys_all = low(low_back(matmul(lifted, attend[1]))).reshape(seq_len, HEADS, HEAD_DIM)
    values_all = low(low_back(matmul(lifted, attend[2]))).reshape(seq_len, HEADS, HEAD_DIM)
    scores = low_back(jnp.einsum('qhe,khe->hqk', queries, keys_all, precision=highest) * HEAD_DIM ** (-0.5))
    allowed = blocks[None, :] <= blocks[:, None]
    probs = jax.nn.softmax(jnp.where(allowed[None], scores, masked_score), axis=2)
    attended = low(low_back(jnp.einsum('hqk,khe->qhe', low(probs), values_all, precision=highest)))
    middle = tokens + low_back(matmul(attended.reshape(seq_len, D), output))
    second = lax.rsqrt(lax.optimization_barrier(jnp.mean(middle * middle, axis=1, keepdims=True)) + norm_eps)
    lifted_two = low(middle * second * scales[1])
    logits = low_back(matmul(lifted_two, router))
    router_probs = jax.nn.softmax(logits, axis=1)
    picks = (choices[:, :, None] == jnp.arange(EXPERTS, dtype=jnp.int32)[None, None, :]).astype(jnp.float32)
    chosen = lax.optimization_barrier(jnp.sum(router_probs[:, None, :] * picks, axis=2))
    slot_id, slot_pair = slot_tables(choices, EXPERTS, CAP)
    padded = jnp.concatenate([lifted_two, jnp.zeros((1, D), jnp.float32)], axis=0)
    slot_rows = low_back(padded[slot_pair // TOP]).reshape(EXPERTS, CAP, D)
    gate = low_back(jnp.einsum('ecd,edf->ecf', slot_rows, experts[:, 0], precision=highest))
    upward = low_back(jnp.einsum('ecd,edf->ecf', slot_rows, experts[:, 1], precision=highest))
    hidden = low(jax.nn.silu(gate) * upward)
    produced = low(low_back(jnp.einsum('ecf,efd->ecd', hidden, narrower, precision=highest)))
    flat = jnp.concatenate([produced.reshape(EXPERTS * CAP, D), jnp.zeros((1, D), jnp.float32)], axis=0)
    pair_out = flat[slot_id].reshape(seq_len, TOP, D)
    mixture = lax.optimization_barrier(jnp.sum(chosen[:, :, None] * pair_out, axis=1))
    shared_gate = low_back(matmul(lifted_two, widener[0]))
    shared_up = low_back(matmul(lifted_two, widener[1]))
    shared_hidden = low(jax.nn.silu(shared_gate) * shared_up)
    shared_out = low_back(matmul(shared_hidden, reducer))
    return middle + shared_out + mixture

def forward_all(params, tokens, block_ids, expert_ids):
    rounded = tuple((low(weight) for weight in params))

    def one_sequence(items):
        return sequence_forward(rounded, items[0], items[1], items[2])
    return lax.map(jax.checkpoint(one_sequence), (tokens, block_ids, expert_ids))

def adam_update(weight, moment, square, gradient, step_rate, shrink_rate):
    moment_next = beta_one * moment + (1.0 - beta_one) * gradient
    square_next = beta_two * square + (1.0 - beta_two) * gradient * gradient
    direction = moment_next / first_fix / (jnp.sqrt(square_next / second_fix) + adam_eps)
    return (weight - step_rate * (direction + shrink_rate * weight), moment_next, square_next)

def reference(tokens_in, cotangent, block_ids, expert_ids, scales, moment_scales, square_scales, attend, moment_attend, square_attend, output, moment_output, square_output, router, moment_router, square_router, widener, moment_widener, square_widener, reducer, moment_reducer, square_reducer, experts, moment_experts, square_experts, narrower, moment_narrower, square_narrower):
    params = (scales, attend, output, router, widener, reducer, experts, narrower)
    moments = (moment_scales, moment_attend, moment_output, moment_router, moment_widener, moment_reducer, moment_experts, moment_narrower)
    squares = (square_scales, square_attend, square_output, square_router, square_widener, square_reducer, square_experts, square_narrower)

    def wrapped(weights, tokens):
        return forward_all(weights, tokens, block_ids, expert_ids)
    result, pullback = jax.vjp(wrapped, params, tokens_in.astype(jnp.float32))
    weight_grads, input_grad = pullback(cotangent.astype(jnp.float32))
    updated = [adam_update(params[kind], moments[kind], squares[kind], weight_grads[kind], learning_rates[kind], decay_rates[kind]) for kind in range(8)]
    return (result.astype(jnp.bfloat16), input_grad, updated[0][0], updated[0][1], updated[0][2], updated[1][0], updated[1][1], updated[1][2], updated[2][0], updated[2][1], updated[2][2], updated[3][0], updated[3][1], updated[3][2], updated[4][0], updated[4][1], updated[4][2], updated[5][0], updated[5][1], updated[5][2], updated[6][0], updated[6][1], updated[6][2], updated[7][0], updated[7][1], updated[7][2])
```

```python
import functools

import jax
import jax.numpy as jnp
from jax import lax
from jax.experimental import pallas as pl
from jax.experimental.pallas import tpu as pltpu
from jax.sharding import PartitionSpec as P

HEADS = 12
CAP = 576
VMEM_LIMIT = 60 * 1024 * 1024

norm_eps = 1e-06
adam_eps = 1e-08
beta_one = 0.9
beta_two = 0.95
first_fix = 1.0 - 0.9**10
second_fix = 1.0 - 0.95**10
learning_rates = (0.3, 0.02, 0.15, 0.02, 0.02, 0.012, 0.02, 0.012)
decay_rates = (0.0, 0.1, 0.1, 0.1, 0.1, 0.1, 0.1, 0.1)
masked_score = -1e30
bf16 = jnp.bfloat16
f32 = jnp.float32


def mm(a, b):
    return jnp.dot(a, b, preferred_element_type=f32)


def mm_nt(a, b):
    return lax.dot_general(a, b, (((1,), (1,)), ((), ())), preferred_element_type=f32)


def mm_tn(a, b):
    return lax.dot_general(a, b, (((0,), (0,)), ((), ())), preferred_element_type=f32)


def params(semantics=None, **more):
    return pltpu.CompilerParams(
        dimension_semantics=semantics, vmem_limit_bytes=VMEM_LIMIT, **more
    )


def whole_spec(shape, **more):
    zeros = (0,) * len(shape)
    return pl.BlockSpec(shape, lambda *_: zeros, **more)


def once(shape):
    return whole_spec(shape, pipeline_mode=pl.Buffered(1))


def forward_kernel(
    tok_ref, bidr_ref, bidc_ref, gains_ref, wa_ref, wo_ref, wr_ref, wrt_ref,
    qkv_ref, lse_ref, o_ref, mid_ref, h2_ref, probs_ref, probst_ref, h1_ref,
):
    pair = pl.program_id(0)
    seq, width = tok_ref.shape
    tile = 256

    @pl.when(pair == 0)
    def _():
        for row in range(0, seq, tile):
            x = tok_ref[pl.ds(row, tile), :].astype(f32)
            r1 = lax.rsqrt(jnp.mean(x * x, axis=1, keepdims=True) + norm_eps)
            h1_ref[pl.ds(row, tile), :] = (x * r1 * gains_ref[0:1, :]).astype(bf16)

    h1 = h1_ref[...]
    for i in range(3):
        w = wa_ref[0, :, i].reshape(width, 128)
        qkv_ref[i] = mm(h1, w).astype(bf16)
    qs = qkv_ref[0] * jnp.asarray(0.125, bf16)
    k = qkv_ref[1]
    vt = qkv_ref[2].T
    lane = lax.broadcasted_iota(jnp.int32, (tile, 128), 1)
    for q0 in range(0, seq, tile):
        kl = min(seq, q0 + 2 * tile)
        qt = qs[q0 : q0 + tile]
        allowed = bidc_ref[q0:kl, :] <= bidr_ref[0:1, q0 : q0 + tile]
        parts = []
        for head in range(2):
            qm = jnp.where((lane // 64) == head, qt, jnp.zeros_like(qt))
            tail = jnp.where(allowed, mm_nt(k[q0:kl], qm), masked_score)
            top = jnp.max(tail, axis=0, keepdims=True)
            if q0:
                lead = mm_nt(k[:q0], qm)
                top = jnp.maximum(top, jnp.max(lead, axis=0, keepdims=True))
                lead = jnp.exp(lead - top)
            tail = jnp.exp(tail - top)
            total = jnp.sum(tail, axis=0, keepdims=True)
            if q0:
                total = total + jnp.sum(lead, axis=0, keepdims=True)
            inverse = 1.0 / total
            vh = vt[64 * head : 64 * head + 64]
            ot = mm(vh[:, q0:kl], (tail * inverse).astype(bf16))
            if q0:
                ot = ot + mm(vh[:, :q0], (lead * inverse).astype(bf16))
            lse_ref[0, head : head + 1, q0 : q0 + tile] = top + jnp.log(total)
            parts.append(ot)
        out = jnp.concatenate(parts, axis=0).T.astype(bf16)
        o_ref[q0 : q0 + tile, pl.ds(pl.multiple_of(pair * 128, 128), 128)] = out

    @pl.when(pair == pl.num_programs(0) - 1)
    def _():
        half = wo_ref.shape[2]
        for row in range(0, seq, tile):
            rows = pl.ds(row, tile)
            o = o_ref[rows, :]
            add = jnp.concatenate([mm(o, wo_ref[0]), mm(o, wo_ref[1])], axis=1)
            mid = tok_ref[rows, :].astype(f32) + add
            mid_ref[rows, :] = mid
            r2 = lax.rsqrt(jnp.mean(mid * mid, axis=1, keepdims=True) + norm_eps)
            h2 = (mid * r2 * gains_ref[1:2, :]).astype(bf16)
            h2_ref[rows, :] = h2
            logits = mm(h2, wr_ref[...])
            spot = lax.broadcasted_iota(jnp.int32, logits.shape, 1)
            logits = jnp.where(spot < 4, logits, masked_score)
            e = jnp.exp(logits - jnp.max(logits, axis=1, keepdims=True))
            probs_ref[rows, :] = e / jnp.sum(e, axis=1, keepdims=True)
        logits = mm_nt(wrt_ref[...], h2_ref[...])
        spot = lax.broadcasted_iota(jnp.int32, logits.shape, 0)
        logits = jnp.where(spot < 4, logits, masked_score)
        e = jnp.exp(logits - jnp.max(logits, axis=0, keepdims=True))
        probst_ref[...] = e / jnp.sum(e, axis=0, keepdims=True)


def attention_forward(tokens, bid_row, bid_col, gains, wa, wo, wr, wrt):
    seq, width = tokens.shape
    pairs = width // 128
    per_half = pairs // 2
    return pl.pallas_call(
        forward_kernel,
        grid=(pairs,),
        in_specs=[
            once((seq, width)),
            once(bid_row.shape),
            once(bid_col.shape),
            once(gains.shape),
            pl.BlockSpec(
                (1, wa.shape[1], 3, wa.shape[3], 128),
                lambda i: (i // per_half, 0, 0, 0, i % per_half),
            ),
            once(wo.shape),
            once(wr.shape),
            once(wrt.shape),
        ],
        out_specs=[
            pl.BlockSpec((3, seq, 128), lambda i: (0, 0, i)),
            pl.BlockSpec((1, 8, seq), lambda i: (i, 0, 0)),
            whole_spec((seq, width)),
            whole_spec((seq, width)),
            whole_spec((seq, width)),
            whole_spec((seq, 128)),
            whole_spec((16, seq)),
        ],
        out_shape=[
            jax.ShapeDtypeStruct((3, seq, width), bf16),
            jax.ShapeDtypeStruct((pairs, 8, seq), f32),
            jax.ShapeDtypeStruct((seq, width), bf16),
            jax.ShapeDtypeStruct((seq, width), f32),
            jax.ShapeDtypeStruct((seq, width), bf16),
            jax.ShapeDtypeStruct((seq, 128), f32),
            jax.ShapeDtypeStruct((16, seq), f32),
        ],
        scratch_shapes=[pltpu.VMEM((seq, width), bf16)],
        compiler_params=params(("arbitrary",)),
        cost_estimate=pl.CostEstimate(
            flops=30_000_000_000, bytes_accessed=20_000_000, transcendentals=12_000_000
        ),
        name="attention_forward",
    )(tokens, bid_row, bid_col, gains, wa, wo, wr, wrt)


def dispatch_kernel(h2_ref, g_ref, place_ref, probst_ref, rows_ref, grads_ref):
    expert = pl.program_id(0)
    seq = h2_ref.shape[0]
    cap = rows_ref.shape[1]
    slot = lax.broadcasted_iota(jnp.int32, (cap, seq), 0)
    hit = slot == place_ref[pl.ds(expert, 1), :]
    chosen = jnp.sum(
        jnp.where(hit, probst_ref[pl.ds(expert, 1), :], 0.0), axis=1, keepdims=True
    )
    hot = hit.astype(f32).astype(bf16)
    rows_ref[0] = mm(hot, h2_ref[...]).astype(bf16)
    grads_ref[0] = (mm(hot, g_ref[...]) * chosen).astype(bf16)


def dispatch(h2, g, place_row, probst, experts_all, cap):
    seq, width = h2.shape
    return pl.pallas_call(
        dispatch_kernel,
        grid=(experts_all,),
        in_specs=[once(h2.shape), once(g.shape), once(place_row.shape), once(probst.shape)],
        out_specs=[pl.BlockSpec((1, cap, width), lambda e: (e, 0, 0))] * 2,
        out_shape=[jax.ShapeDtypeStruct((experts_all, cap, width), bf16)] * 2,
        compiler_params=params(("arbitrary",)),
        cost_estimate=pl.CostEstimate(
            flops=8_000_000_000, bytes_accessed=10_000_000, transcendentals=0
        ),
        name="dispatch",
    )(h2, g, place_row, probst)


def ffn_kernel(
    x_ref, g_ref, wg_ref, wu_ref, wn_ref,
    out_ref, gin_ref, dwg_ref, dwu_ref, dwn_ref,
    acc_out, acc_gin, hid_s, gg_s, ug_s,
    *, tile,
):
    f = pl.program_id(0)
    last = pl.num_programs(0) - 1
    rows_all = x_ref.shape[0]

    @pl.when(f == 0)
    def _():
        acc_out[...] = jnp.zeros_like(acc_out)
        acc_gin[...] = jnp.zeros_like(acc_gin)

    wg, wu, wn = wg_ref[0], wu_ref[0], wn_ref[...]
    for row in range(0, rows_all, tile):
        rows = pl.ds(row, tile)
        x, g = x_ref[rows, :], g_ref[rows, :]
        gate, up = mm(x, wg), mm(x, wu)
        sig = 1.0 / (1.0 + jnp.exp(-gate))
        active = gate * sig
        slope = sig * (1.0 + gate * (1.0 - sig))
        hidden = (active * up).astype(bf16)
        hgrad = mm_nt(g, wn)
        gg = (hgrad * up * slope).astype(bf16)
        ug = (hgrad * active).astype(bf16)
        hid_s[rows, :], gg_s[rows, :], ug_s[rows, :] = hidden, gg, ug
        acc_out[rows, :] += mm(hidden, wn)
        acc_gin[rows, :] += mm_nt(gg, wg) + mm_nt(ug, wu)
    dwg_ref[0] = mm_tn(x_ref[...], gg_s[...]).astype(dwg_ref.dtype)
    dwu_ref[0] = mm_tn(x_ref[...], ug_s[...]).astype(dwu_ref.dtype)
    dwn_ref[...] = mm_tn(hid_s[...], g_ref[...]).astype(dwn_ref.dtype)

    @pl.when(f == last)
    def _():
        out_ref[...] = acc_out[...].astype(out_ref.dtype)
        gin_ref[...] = acc_gin[...].astype(gin_ref.dtype)


def ffn(x, g, wgu, wn, out_type, tile, name):
    rows, width = x.shape
    hidden = wn.shape[0]
    ft = 512
    return pl.pallas_call(
        functools.partial(ffn_kernel, tile=tile),
        grid=(hidden // ft,),
        in_specs=[
            once((rows, width)),
            once((rows, width)),
            pl.BlockSpec((1, width, ft), lambda f: (0, 0, f)),
            pl.BlockSpec((1, width, ft), lambda f: (1, 0, f)),
            pl.BlockSpec((ft, width), lambda f: (f, 0)),
        ],
        out_specs=[
            once((rows, width)),
            once((rows, width)),
            pl.BlockSpec((1, width, ft), lambda f: (0, 0, f)),
            pl.BlockSpec((1, width, ft), lambda f: (0, 0, f)),
            pl.BlockSpec((ft, width), lambda f: (f, 0)),
        ],
        out_shape=[
            jax.ShapeDtypeStruct((rows, width), out_type),
            jax.ShapeDtypeStruct((rows, width), out_type),
            jax.ShapeDtypeStruct((1, width, hidden), bf16),
            jax.ShapeDtypeStruct((1, width, hidden), bf16),
            jax.ShapeDtypeStruct((hidden, width), bf16),
        ],
        scratch_shapes=[
            pltpu.VMEM((rows, width), f32),
            pltpu.VMEM((rows, width), f32),
            pltpu.VMEM((rows, ft), bf16),
            pltpu.VMEM((rows, ft), bf16),
            pltpu.VMEM((rows, ft), bf16),
        ],
        compiler_params=params(("arbitrary",)),
        cost_estimate=pl.CostEstimate(
            flops=18 * rows * width * hidden,
            bytes_accessed=12 * width * hidden + 8 * rows * width,
            transcendentals=rows * hidden,
        ),
        name=name,
    )(x, g, wgu, wgu, wn)


def combine_kernel(
    mid_ref, sout_ref, sin_ref, g_ref, h2_ref, probs_ref, place_ref, eout_ref, ein_ref,
    gains_ref, wr_ref, wo_ref,
    block_ref, midg_ref, midb_ref, og_ref, gain_ref, rgrad_ref,
):
    step = pl.program_id(0)
    tile, width = mid_ref.shape
    experts_all, cap = eout_ref.shape[0], eout_ref.shape[1]
    slot = lax.broadcasted_iota(jnp.int32, (tile, cap), 1)
    g = g_ref[...].astype(f32)
    probs = probs_ref[...]
    spot = lax.broadcasted_iota(jnp.int32, probs.shape, 1)
    mixture = jnp.zeros((tile, width), f32)
    moe_in = jnp.zeros((tile, width), f32)
    pgrad = jnp.zeros(probs.shape, f32)
    for e in range(experts_all):
        hot = (slot == place_ref[:, e : e + 1]).astype(f32).astype(bf16)
        pair_out = mm(hot, eout_ref[e])
        mixture += probs[:, e : e + 1] * pair_out
        grad = jnp.sum(g * pair_out, axis=1, keepdims=True)
        pgrad = jnp.where(spot == e, grad, pgrad)
        moe_in += mm(hot, ein_ref[e])
    mid = mid_ref[...]
    block_ref[...] = (mid + sout_ref[...] + mixture).astype(bf16)
    inner = jnp.sum(pgrad * probs, axis=1, keepdims=True)
    lgrad = (probs * (pgrad - inner)).astype(bf16)
    h2_grad = moe_in + mm_nt(lgrad, wr_ref[...]) + sin_ref[...]
    r2 = lax.rsqrt(jnp.mean(mid * mid, axis=1, keepdims=True) + norm_eps)
    n2 = mid * r2
    d2 = h2_grad * gains_ref[1:2, :]
    mid_grad = g + r2 * (d2 - n2 * jnp.mean(d2 * n2, axis=1, keepdims=True))
    midb = mid_grad.astype(bf16)
    midg_ref[...] = mid_grad
    midb_ref[...] = midb
    half = wo_ref.shape[2]
    og = mm_nt(midb[:, :half], wo_ref[0]) + mm_nt(midb[:, half:], wo_ref[1])
    og_ref[...] = og.astype(bf16)
    gsum = jnp.sum(h2_grad * n2, axis=0, keepdims=True)
    rsum = mm_tn(lgrad, h2_ref[...])[:16]

    @pl.when(step == 0)
    def _():
        gain_ref[...] = jnp.zeros_like(gain_ref)
        rgrad_ref[...] = jnp.zeros_like(rgrad_ref)

    gain_ref[0:1, :] += gsum
    rgrad_ref[...] += rsum


def combine(mid, sout, sin, g, h2, probs, place_col, eout, ein, gains, wr, wo):
    seq, width = mid.shape
    tile = 256
    by_rows = pl.BlockSpec((tile, width), lambda i: (i, 0))
    lanes = pl.BlockSpec((tile, 128), lambda i: (i, 0))
    return pl.pallas_call(
        combine_kernel,
        grid=(seq // tile,),
        in_specs=[
            by_rows, by_rows, by_rows, by_rows, by_rows, lanes, lanes,
            once(eout.shape), once(ein.shape), once(gains.shape), once(wr.shape), once(wo.shape),
        ],
        out_specs=[by_rows, by_rows, by_rows, by_rows, whole_spec((8, width)), whole_spec((16, width))],
        out_shape=[
            jax.ShapeDtypeStruct((seq, width), bf16),
            jax.ShapeDtypeStruct((seq, width), f32),
            jax.ShapeDtypeStruct((seq, width), bf16),
            jax.ShapeDtypeStruct((seq, width), bf16),
            jax.ShapeDtypeStruct((8, width), f32),
            jax.ShapeDtypeStruct((16, width), f32),
        ],
        compiler_params=params(("arbitrary",)),
        cost_estimate=pl.CostEstimate(
            flops=11_000_000_000, bytes_accessed=30_000_000, transcendentals=0
        ),
        name="combine",
    )(mid, sout, sin, g, h2, probs, place_col, eout, ein, gains, wr, wo)


def backward_kernel(qkv_ref, og_ref, lse_ref, bidr_ref, bidc_ref, grad_ref, dk_s, dv_s):
    seq = og_ref.shape[0]
    tile = 256
    qs = qkv_ref[0] * jnp.asarray(0.125, bf16)
    k = qkv_ref[1]
    v = qkv_ref[2]
    kt = k.T
    og = og_ref[...]
    lane = lax.broadcasted_iota(jnp.int32, (tile, 128), 1)
    dk_s[...] = jnp.zeros_like(dk_s)
    dv_s[...] = jnp.zeros_like(dv_s)
    for q0 in range(0, seq, tile):
        kl = min(seq, q0 + 2 * tile)
        qt, ot = qs[q0 : q0 + tile], og[q0 : q0 + tile]
        allowed = bidc_ref[q0:kl, :] <= bidr_ref[0:1, q0 : q0 + tile]
        parts = []
        for head in range(2):
            own = (lane // 64) == head
            qm = jnp.where(own, qt, jnp.zeros_like(qt))
            om = jnp.where(own, ot, jnp.zeros_like(ot))
            lse = lse_ref[0, head : head + 1, q0 : q0 + tile]
            spans = ([(0, q0)] if q0 else []) + [(q0, kl)]
            kept = []
            delta = jnp.zeros((1, tile), f32)
            for low, high in spans:
                s = mm_nt(k[low:high], qm)
                if low == q0:
                    s = jnp.where(allowed, s, masked_score)
                p = jnp.exp(s - lse)
                dp = mm_nt(v[low:high], om)
                delta = delta + jnp.sum(p * dp, axis=0, keepdims=True)
                kept.append((low, high, p, dp))
            dq = jnp.zeros((64, tile), f32)
            for low, high, p, dp in kept:
                ds = (p * (dp - delta)).astype(bf16)
                dv_s[low:high, :] += mm(p.astype(bf16), om)
                dk_s[low:high, :] += mm(ds, qm)
                dq = dq + mm(kt[64 * head : 64 * head + 64, low:high], ds)
            parts.append(dq)
        dq = jnp.concatenate(parts, axis=0).T * 0.125
        grad_ref[0, q0 : q0 + tile, :] = dq.astype(bf16)
    grad_ref[1] = dk_s[...].astype(bf16)
    grad_ref[2] = dv_s[...].astype(bf16)


def attention_backward(qkv, og, lse, bid_row, bid_col):
    _, seq, width = qkv.shape
    pairs = width // 128
    return pl.pallas_call(
        backward_kernel,
        grid=(pairs,),
        in_specs=[
            pl.BlockSpec((3, seq, 128), lambda i: (0, 0, i)),
            pl.BlockSpec((seq, 128), lambda i: (0, i)),
            pl.BlockSpec((1, 8, seq), lambda i: (i, 0, 0)),
            once(bid_row.shape),
            once(bid_col.shape),
        ],
        out_specs=pl.BlockSpec((3, seq, 128), lambda i: (0, 0, i)),
        out_shape=jax.ShapeDtypeStruct((3, seq, width), bf16),
        scratch_shapes=[pltpu.VMEM((seq, 128), f32), pltpu.VMEM((seq, 128), f32)],
        compiler_params=params(("arbitrary",)),
        cost_estimate=pl.CostEstimate(
            flops=35_000_000_000, bytes_accessed=12_000_000, transcendentals=12_000_000
        ),
        name="attention_backward",
    )(qkv, og, lse, bid_row, bid_col)


def adam_update(weight, moment, square, gradient, step_rate, shrink_rate):
    moment_next = beta_one * moment + (1.0 - beta_one) * gradient
    square_next = beta_two * square + (1.0 - beta_two) * gradient * gradient
    direction = moment_next / first_fix / (jnp.sqrt(square_next / second_fix) + adam_eps)
    return (weight - step_rate * (direction + shrink_rate * weight), moment_next, square_next)


def pick(array, axis, index):
    return lax.dynamic_index_in_dim(array, index, axis, keepdims=False)


def sum_parts(array):
    return jnp.sum(array.astype(f32), axis=0)


def reduce_scatter(stacked, axes, groups, core):
    own, other = pick(stacked, 0, core), pick(stacked, 0, 1 - core)
    swap = [(i, i ^ 1) for i in range(groups)]
    arrived = lax.ppermute(other, "grp", swap)
    part = (own.astype(f32) + arrived.astype(f32)).astype(bf16)
    for axis in axes[:-1]:
        size = lax.axis_size(axis)
        part = part.reshape((size, part.shape[0] // size) + part.shape[1:])
        part = lax.all_to_all(part, axis, 0, 0, tiled=True)
        part = sum_parts(part).astype(bf16)
    part = sum_parts(lax.all_to_all(part, axes[-1], 0, 0, tiled=True))
    both = jnp.zeros((2,) + part.shape, f32)
    both = lax.dynamic_update_index_in_dim(both, part, core, 0)
    if groups > 2:
        return lax.psum(both, "grp")
    return lax.dynamic_update_index_in_dim(both, lax.ppermute(part, "grp", swap), 1 - core, 0)


def on_device(
    tokens_in, cotangent, block_ids, expert_ids,
    scales, moment_scales, square_scales, attend, moment_attend, square_attend,
    output, moment_output, square_output, router, moment_router, square_router,
    widener, moment_widener, square_widener, reducer, moment_reducer, square_reducer,
    experts, moment_experts, square_experts, narrower, moment_narrower, square_narrower,
):
    groups, exps, shds = (lax.axis_size(a) for a in ("grp", "exp", "shd"))
    spread = exps * shds
    core = lax.rem(lax.axis_index("grp"), 2)
    _, seq, width = tokens_in.shape
    hidden = reducer.shape[1 - 1] * spread
    experts_all = exps * experts.shape[0]
    rows = output.shape[0]
    half = width // 2
    tokens, g = tokens_in.reshape(seq, width), cotangent.reshape(seq, width)

    def gather(part, axes, order):
        names = ("grp",) + axes if order == "first" else axes + ("grp",)
        if groups == 2:
            return lax.all_gather(part, names, axis=0, tiled=False).reshape((-1,) + part.shape)
        wide = lax.all_gather(part, names, axis=0, tiled=False)
        shape = (groups, -1) if order == "first" else (-1, groups)
        wide = wide.reshape(shape + part.shape)
        wide = wide[:2] if order == "first" else wide[:, :2]
        return wide.reshape((-1,) + part.shape)

    both = ("exp", "shd")
    small = jnp.concatenate([router.reshape(-1), scales.reshape(-1)])
    small = jnp.pad(small, (0, half - small.shape[0])).reshape(1, half)
    small = jnp.pad(small, ((0, 15), (0, 0))).astype(bf16)
    columns = lambda a, n: pick(a.astype(bf16).reshape(n, 2, half), 1, core)
    payload = jnp.concatenate(
        [columns(attend, 3 * rows), columns(output, rows), small], axis=0
    )
    first = gather(payload, both, "first").reshape(2, spread, payload.shape[0], half)
    w_experts = gather(pick(experts.astype(bf16)[0], 0, core), ("shd",), "first").reshape(2, width, hidden)
    w_narrower = gather(
        pick(narrower.astype(bf16).reshape(2, -1, width), 0, core), ("shd",), "last"
    ).reshape(hidden, width)
    w_widener = gather(pick(widener.astype(bf16), 0, core), both, "first").reshape(2, width, hidden)
    w_reducer = gather(
        pick(reducer.astype(bf16).reshape(2, -1, width), 0, core), both, "last"
    ).reshape(hidden, width)

    wa = first[:, :, : 3 * rows].reshape(2, spread, 3, rows, half)
    wo = first[:, :, 3 * rows : 4 * rows].reshape(2, width, half)
    packed = first[0, :, 4 * rows]
    count = rows * experts_all
    w_router = packed[:, :count].reshape(width, experts_all)
    gains = packed[:, count : count + 2 * rows].reshape(spread, 2, rows)
    gains = gains.transpose(1, 0, 2).reshape(2, width).astype(f32)
    gains = jnp.pad(gains, ((0, 6), (0, 0)))
    wr = jnp.pad(w_router, ((0, 0), (0, 128 - experts_all)))
    wrt = jnp.pad(w_router.T, ((0, 16 - experts_all), (0, 0)))

    ids = expert_ids.reshape(seq, 2)
    every = jnp.arange(128, dtype=jnp.int32)[None, :]
    hot = (ids[:, 0:1] == every) | (ids[:, 1:2] == every)
    order = jnp.arange(seq, dtype=jnp.int32)
    before = (order[:, None] > order[None, :]).astype(bf16)
    placed = mm(before, hot.astype(bf16)).astype(jnp.int32)
    place_col = jnp.where(hot, placed, -1)
    place_row = place_col[:, :16].T
    bid = block_ids.reshape(1, seq)
    bid_row = jnp.broadcast_to(bid, (8, seq))
    bid_col = jnp.broadcast_to(bid.reshape(seq, 1), (seq, 256))

    qkv, lse, o, mid, h2, probs, probst = attention_forward(
        tokens, bid_row, bid_col, gains, wa, wo, wr, wrt
    )
    slot_rows, slot_grad = dispatch(h2, g, place_row, probst, experts_all, CAP)
    swap_rows = functools.partial(lax.all_to_all, axis_name="exp", split_axis=0, concat_axis=0, tiled=True)
    received, back_rows = swap_rows(slot_rows), swap_rows(slot_grad)
    sout, sin, dsg, dsu, dsn = ffn(h2, g, w_widener, w_reducer, f32, 256, "shared")
    eout, ein, dwg, dwu, dwn = ffn(
        received.reshape(-1, width), back_rows.reshape(-1, width), w_experts, w_narrower, bf16, 384, "routed"
    )
    eout = swap_rows(eout.reshape(experts_all, CAP, width))
    ein = swap_rows(ein.reshape(experts_all, CAP, width))
    block_out, mid_grad, midb, og, gain_two, rgrad = combine(
        mid, sout, sin, g, h2, probs, place_col, eout, ein, gains, wr, wo
    )
    dqkv = attention_backward(qkv, og, lse, bid_row, bid_col)

    x = tokens.astype(f32)
    r1 = lax.rsqrt(jnp.mean(x * x, axis=1, keepdims=True) + norm_eps)
    n1 = x * r1
    h1 = (n1 * gains[0:1]).astype(bf16)
    attend_grad = jnp.einsum("nd,tnf->tdf", h1, dqkv, preferred_element_type=f32)
    output_grad = mm_tn(o, midb)
    w_full = wa.transpose(2, 1, 3, 0, 4).reshape(3, width, width)
    h1_grad = jnp.einsum("tnf,tdf->nd", dqkv, w_full, preferred_element_type=f32)
    gain_one = jnp.sum(h1_grad * n1, axis=0)
    d1 = h1_grad * gains[0:1]
    input_grad = mid_grad + r1 * (d1 - n1 * jnp.mean(d1 * n1, axis=1, keepdims=True))

    g_experts = reduce_scatter(
        jnp.concatenate([dwg, dwu], axis=0).reshape(2, shds, width // shds, hidden), ("shd",), groups, core
    )
    g_narrower = reduce_scatter(
        dwn.reshape(shds, 2, -1, width).transpose(1, 0, 2, 3), ("shd",), groups, core
    )
    small = jnp.concatenate(
        [rgrad[:experts_all], gain_one[None, :], gain_two[0:1]], axis=0
    ).reshape(-1, spread, rows).transpose(1, 0, 2).reshape(spread, 1, -1)
    small = jnp.pad(small, ((0, 0), (0, 15), (0, width - small.shape[2])))
    dense = jnp.concatenate(
        [
            attend_grad.astype(bf16).reshape(3, spread, rows, width).transpose(1, 0, 2, 3).reshape(spread, -1, width),
            output_grad.astype(bf16).reshape(spread, rows, width),
            jnp.concatenate([dsg, dsu], axis=0).reshape(2, spread, rows, hidden).transpose(1, 0, 2, 3).reshape(spread, -1, width),
            dsn.reshape(spread, -1, width),
            small.astype(bf16),
        ],
        axis=1,
    )
    total = dense.shape[1]
    dense = dense.reshape(spread, 2, total // 2, width).transpose(1, 0, 2, 3)
    dense = reduce_scatter(dense, both, groups, core).reshape(total, width)
    sizes = (3 * rows, rows, 2 * rows * hidden // width, reducer.shape[0])
    starts = (0, sizes[0], sizes[0] + sizes[1], sum(sizes[:3]))
    cut = lambda i, shape: dense[starts[i] : starts[i] + sizes[i]].reshape(shape)
    tiny = dense[sum(sizes)][: (experts_all + 2) * rows].reshape(experts_all + 2, rows)
    grads = (
        tiny[experts_all:],
        cut(0, attend.shape),
        cut(1, output.shape),
        tiny[:experts_all].T,
        cut(2, widener.shape),
        cut(3, reducer.shape),
        g_experts.reshape(experts.shape),
        g_narrower.reshape(narrower.shape),
    )
    masters = (scales, attend, output, router, widener, reducer, experts, narrower)
    moments = (
        moment_scales, moment_attend, moment_output, moment_router,
        moment_widener, moment_reducer, moment_experts, moment_narrower,
    )
    squares = (
        square_scales, square_attend, square_output, square_router,
        square_widener, square_reducer, square_experts, square_narrower,
    )
    results = [block_out.reshape(tokens_in.shape), input_grad.reshape(tokens_in.shape)]
    for kind in range(8):
        results.extend(
            adam_update(
                masters[kind], moments[kind], squares[kind], grads[kind],
                learning_rates[kind], decay_rates[kind],
            )
        )
    return tuple(results)


def solution(mesh):
    tokens = P(("grp", "exp", "shd"), None, None)
    both = ("exp", "shd")
    kinds = (
        P(None, both), P(None, both, None), P(both, None), P(both, None),
        P(None, both, None), P(both, None), P("exp", None, "shd", None), P("exp", "shd", None),
    )
    thrice = tuple(kind for kind in kinds for _ in range(3))
    return jax.shard_map(
        on_device,
        mesh=mesh,
        in_specs=(tokens, tokens, P(("grp", "exp", "shd"), None), tokens) + thrice,
        out_specs=(tokens, tokens) + thrice,
        check_vma=False,
    )
```

```python
import functools

import jax
import jax.numpy as jnp
from jax import lax
from jax.experimental import pallas as pl
from jax.experimental.pallas import tpu as pltpu
from jax.sharding import PartitionSpec as P

HEADS = 12
CAP = 576
VMEM_LIMIT = 60 * 1024 * 1024

norm_eps = 1e-06
adam_eps = 1e-08
beta_one = 0.9
beta_two = 0.95
first_fix = 1.0 - 0.9**10
second_fix = 1.0 - 0.95**10
learning_rates = (0.3, 0.02, 0.15, 0.02, 0.02, 0.012, 0.02, 0.012)
decay_rates = (0.0, 0.1, 0.1, 0.1, 0.1, 0.1, 0.1, 0.1)
masked_score = -1e30
bf16 = jnp.bfloat16
f32 = jnp.float32


def mm(a, b):
    return jnp.dot(a, b, preferred_element_type=f32)


def mm_nt(a, b):
    return lax.dot_general(a, b, (((1,), (1,)), ((), ())), preferred_element_type=f32)


def mm_tn(a, b):
    return lax.dot_general(a, b, (((0,), (0,)), ((), ())), preferred_element_type=f32)


def params(semantics=None, **more):
    return pltpu.CompilerParams(
        dimension_semantics=semantics, vmem_limit_bytes=VMEM_LIMIT, **more
    )


def whole_spec(shape, **more):
    zeros = (0,) * len(shape)
    return pl.BlockSpec(shape, lambda *_: zeros, **more)


def once(shape):
    return whole_spec(shape, pipeline_mode=pl.Buffered(1))


MESH = pl.DeviceIdType.MESH
ANY = pl.BlockSpec(memory_space=pl.ANY)


def greet(targets):
    barrier = pltpu.get_barrier_semaphore()
    for target in targets:
        pl.semaphore_signal(barrier, inc=1, device_id=target, device_id_type=MESH)
    pl.semaphore_wait(barrier, len(targets))


def send(src, dst, send_sem, recv_sem, target):
    return pltpu.make_async_remote_copy(
        src_ref=src, dst_ref=dst, send_sem=send_sem, recv_sem=recv_sem,
        device_id=target, device_id_type=MESH,
    )


def forward_kernel(
    exps,
    tok_ref, bidr_ref, bidc_ref, gains_ref, wa_ref, wo_ref, wr_ref, wrt_ref, slots_ref,
    qkv_ref, lse_ref, o_ref, mid_ref, h2_ref, probs_ref, probst_ref, landed_ref, h1_ref,
    send_sem, recv_sem,
):
    pair = pl.program_id(0)
    me = lax.axis_index("exp")

    def copies():
        made = [pltpu.make_async_copy(slots_ref.at[me], landed_ref.at[0], send_sem.at[0])]
        for k in range(1, exps):
            peer = lax.bitwise_xor(me, k)
            made.append(
                send(slots_ref.at[peer], landed_ref.at[k], send_sem.at[k], recv_sem.at[k], {"exp": peer})
            )
        return made

    @pl.when(pair == 0)
    def _():
        greet([{"exp": lax.bitwise_xor(me, k)} for k in range(1, exps)])
        for copy in copies():
            copy.start()
    seq, width = tok_ref.shape
    tile = 256

    @pl.when(pair == 0)
    def _():
        for row in range(0, seq, tile):
            x = tok_ref[pl.ds(row, tile), :].astype(f32)
            r1 = lax.rsqrt(jnp.mean(x * x, axis=1, keepdims=True) + norm_eps)
            h1_ref[pl.ds(row, tile), :] = (x * r1 * gains_ref[0:1, :]).astype(bf16)

    h1 = h1_ref[...]
    for i in range(3):
        w = wa_ref[0, :, i].reshape(width, 128)
        qkv_ref[i] = mm(h1, w).astype(bf16)
    qs = qkv_ref[0] * jnp.asarray(0.125, bf16)
    k = qkv_ref[1]
    vt = qkv_ref[2].T
    lane = lax.broadcasted_iota(jnp.int32, (tile, 128), 1)
    for q0 in range(0, seq, tile):
        kl = min(seq, q0 + 2 * tile)
        qt = qs[q0 : q0 + tile]
        allowed = bidc_ref[q0:kl, :] <= bidr_ref[0:1, q0 : q0 + tile]
        parts = []
        for head in range(2):
            qm = jnp.where((lane // 64) == head, qt, jnp.zeros_like(qt))
            tail = jnp.where(allowed, mm_nt(k[q0:kl], qm), masked_score)
            top = jnp.max(tail, axis=0, keepdims=True)
            if q0:
                lead = mm_nt(k[:q0], qm)
                top = jnp.maximum(top, jnp.max(lead, axis=0, keepdims=True))
                lead = jnp.exp(lead - top)
            tail = jnp.exp(tail - top)
            total = jnp.sum(tail, axis=0, keepdims=True)
            if q0:
                total = total + jnp.sum(lead, axis=0, keepdims=True)
            inverse = 1.0 / total
            vh = vt[64 * head : 64 * head + 64]
            ot = mm(vh[:, q0:kl], (tail * inverse).astype(bf16))
            if q0:
                ot = ot + mm(vh[:, :q0], (lead * inverse).astype(bf16))
            lse_ref[0, head : head + 1, q0 : q0 + tile] = top + jnp.log(total)
            parts.append(ot)
        out = jnp.concatenate(parts, axis=0).T.astype(bf16)
        o_ref[q0 : q0 + tile, pl.ds(pl.multiple_of(pair * 128, 128), 128)] = out

    @pl.when(pair == pl.num_programs(0) - 1)
    def _():
        half = wo_ref.shape[2]
        for row in range(0, seq, tile):
            rows = pl.ds(row, tile)
            o = o_ref[rows, :]
            add = jnp.concatenate([mm(o, wo_ref[0]), mm(o, wo_ref[1])], axis=1)
            mid = tok_ref[rows, :].astype(f32) + add
            mid_ref[rows, :] = mid
            r2 = lax.rsqrt(jnp.mean(mid * mid, axis=1, keepdims=True) + norm_eps)
            h2 = (mid * r2 * gains_ref[1:2, :]).astype(bf16)
            h2_ref[rows, :] = h2
            logits = mm(h2, wr_ref[...])
            spot = lax.broadcasted_iota(jnp.int32, logits.shape, 1)
            logits = jnp.where(spot < 4, logits, masked_score)
            e = jnp.exp(logits - jnp.max(logits, axis=1, keepdims=True))
            probs_ref[rows, :] = e / jnp.sum(e, axis=1, keepdims=True)
        logits = mm_nt(wrt_ref[...], h2_ref[...])
        spot = lax.broadcasted_iota(jnp.int32, logits.shape, 0)
        logits = jnp.where(spot < 4, logits, masked_score)
        e = jnp.exp(logits - jnp.max(logits, axis=0, keepdims=True))
        probst_ref[...] = e / jnp.sum(e, axis=0, keepdims=True)
        for copy in copies():
            copy.wait()


def attention_forward(tokens, bid_row, bid_col, gains, wa, wo, wr, wrt, slots):
    exps = slots.shape[0]
    seq, width = tokens.shape
    pairs = width // 128
    per_half = pairs // 2
    return pl.pallas_call(
        functools.partial(forward_kernel, exps),
        grid=(pairs,),
        in_specs=[
            once((seq, width)),
            once(bid_row.shape),
            once(bid_col.shape),
            once(gains.shape),
            pl.BlockSpec(
                (1, wa.shape[1], 3, wa.shape[3], 128),
                lambda i: (i // per_half, 0, 0, 0, i % per_half),
            ),
            once(wo.shape),
            once(wr.shape),
            once(wrt.shape),
            ANY,
        ],
        out_specs=[
            pl.BlockSpec((3, seq, 128), lambda i: (0, 0, i)),
            pl.BlockSpec((1, 8, seq), lambda i: (i, 0, 0)),
            whole_spec((seq, width)),
            whole_spec((seq, width)),
            whole_spec((seq, width)),
            whole_spec((seq, 128)),
            whole_spec((16, seq)),
            ANY,
        ],
        out_shape=[
            jax.ShapeDtypeStruct((3, seq, width), bf16),
            jax.ShapeDtypeStruct((pairs, 8, seq), f32),
            jax.ShapeDtypeStruct((seq, width), bf16),
            jax.ShapeDtypeStruct((seq, width), f32),
            jax.ShapeDtypeStruct((seq, width), bf16),
            jax.ShapeDtypeStruct((seq, 128), f32),
            jax.ShapeDtypeStruct((16, seq), f32),
            jax.ShapeDtypeStruct(slots.shape, bf16),
        ],
        scratch_shapes=[
            pltpu.VMEM((seq, width), bf16),
            pltpu.SemaphoreType.DMA((exps,)),
            pltpu.SemaphoreType.DMA((exps,)),
        ],
        compiler_params=params(("arbitrary",), collective_id=1, has_side_effects=True),
        cost_estimate=pl.CostEstimate(
            flops=30_000_000_000, bytes_accessed=20_000_000, transcendentals=12_000_000
        ),
        name="attention_forward",
    )(tokens, bid_row, bid_col, gains, wa, wo, wr, wrt, slots)


def slots_of(place_row, cap):
    slot = lax.broadcasted_iota(jnp.int32, (cap, place_row.shape[1]), 0)
    return (slot == place_row).astype(f32).astype(bf16)


def place_kernel(g_ref, place_ref, rows_ref):
    hot = slots_of(place_ref[pl.ds(pl.program_id(0), 1), :], rows_ref.shape[1])
    rows_ref[0] = mm(hot, g_ref[...]).astype(bf16)


def place_gradients(g, place_row, experts_all, cap):
    return pl.pallas_call(
        place_kernel,
        grid=(experts_all,),
        in_specs=[once(g.shape), once(place_row.shape)],
        out_specs=pl.BlockSpec((1, cap, g.shape[1]), lambda e: (e, 0, 0)),
        out_shape=jax.ShapeDtypeStruct((experts_all, cap, g.shape[1]), bf16),
        compiler_params=params(("arbitrary",)),
        cost_estimate=pl.CostEstimate(
            flops=4_000_000_000, bytes_accessed=6_000_000, transcendentals=0
        ),
        name="place_gradients",
    )(g, place_row)


def dispatch_kernel(h2_ref, place_ref, probst_ref, rows_ref, chosen_ref):
    expert = pl.program_id(0)
    cap = rows_ref.shape[1]
    lanes = chosen_ref.shape[2]
    row = place_ref[pl.ds(expert, 1), :]
    rows_ref[0] = mm(slots_of(row, cap), h2_ref[...]).astype(bf16)
    value = probst_ref[pl.ds(expert, 1), :]
    high = value.astype(bf16)
    rest = value - high.astype(f32)
    middle = rest.astype(bf16)
    low = (rest - middle.astype(f32)).astype(bf16)
    eight = lambda a: jnp.broadcast_to(a.astype(f32), (8, row.shape[1])).astype(bf16)
    hot = slots_of(row, lanes)
    chosen = mm_nt(eight(high), hot) + mm_nt(eight(middle), hot) + mm_nt(eight(low), hot)
    chosen_ref[0] = chosen


def dispatch(h2, place_row, probst, experts_all, cap, lanes):
    seq, width = h2.shape
    return pl.pallas_call(
        dispatch_kernel,
        grid=(experts_all,),
        in_specs=[once(h2.shape), once(place_row.shape), once(probst.shape)],
        out_specs=[
            pl.BlockSpec((1, cap, width), lambda e: (e, 0, 0)),
            pl.BlockSpec((1, 8, lanes), lambda e: (e, 0, 0)),
        ],
        out_shape=[
            jax.ShapeDtypeStruct((experts_all, cap, width), bf16),
            jax.ShapeDtypeStruct((experts_all, 8, lanes), f32),
        ],
        compiler_params=params(("arbitrary",)),
        cost_estimate=pl.CostEstimate(
            flops=5_000_000_000, bytes_accessed=6_000_000, transcendentals=0
        ),
        name="dispatch",
    )(h2, place_row, probst)


def gated(x, g, wg, wu, wn):
    gate, up = mm(x, wg), mm(x, wu)
    sig = 1.0 / (1.0 + jnp.exp(-gate))
    active = gate * sig
    slope = sig * (1.0 + gate * (1.0 - sig))
    hidden = (active * up).astype(bf16)
    hgrad = mm_nt(g, wn)
    return hidden, (hgrad * up * slope).astype(bf16), (hgrad * active).astype(bf16)


def routed_kernel(
    exps, shds,
    rows_ref, chosen_ref, grads_ref, we_ref, wn_ref,
    eout_ref, ein_ref, sums_ref,
    x_s, g_s, c_s, w_s, n_s, hid_s, gg_s, ug_s, out_s, gin_s, acc_o, acc_i,
    load_sem, x_send, x_recv, c_send, c_recv, o_send, o_recv, i_send, i_recv, w_sem,
):
    me = lax.axis_index("exp")
    _, cap, width = x_s.shape
    hidden = hid_s.shape[1]
    rows_all = exps * cap
    peers = [lax.bitwise_xor(me, k) for k in range(exps)]
    greet([{"exp": peer} for peer in peers[1:]])

    chosen, arriving = [], []
    for k in range(1, exps):
        target = {"exp": peers[k]}
        chosen.append(send(chosen_ref.at[peers[k]], c_s.at[k], c_send.at[k], c_recv.at[k], target))
        arriving.append(send(rows_ref.at[peers[k]], x_s.at[k], x_send.at[k], x_recv.at[k], target))
    for copy in chosen + arriving:
        copy.start()
    loads = [
        pltpu.make_async_copy(rows_ref.at[me], x_s.at[0], load_sem.at[0]),
        pltpu.make_async_copy(chosen_ref.at[me], c_s.at[0], load_sem.at[1]),
        pltpu.make_async_copy(grads_ref, g_s, load_sem.at[2]),
        pltpu.make_async_copy(we_ref, w_s, load_sem.at[3]),
        pltpu.make_async_copy(wn_ref, n_s, load_sem.at[4]),
    ]
    for copy in loads:
        copy.start()
    for copy in loads:
        copy.wait()

    ft = 256
    returns = []
    for k in range(exps):
        if k:
            chosen[k - 1].wait()
            arriving[k - 1].wait()
        scale = c_s[k].T[:cap, 0:1]
        g_s[k] = (g_s[k].astype(f32) * scale).astype(bf16)
        acc_o[...] = jnp.zeros_like(acc_o)
        acc_i[...] = jnp.zeros_like(acc_i)

        @pl.loop(0, hidden // ft)
        def _(f):
            columns = pl.ds(pl.multiple_of(f * ft, ft), ft)
            wg = w_s[0, :, :, columns].reshape(width, ft)
            wu = w_s[1, :, :, columns].reshape(width, ft)
            wn = n_s[f // 2, f % 2]
            hid, gg, ug = gated(x_s[k], g_s[k], wg, wu, wn)
            hid_s[pl.ds(k * cap, cap), columns] = hid
            gg_s[pl.ds(k * cap, cap), columns] = gg
            ug_s[pl.ds(k * cap, cap), columns] = ug
            acc_o[...] += mm(hid, wn)
            acc_i[...] += mm_nt(gg, wg) + mm_nt(ug, wu)

        out_s[k] = acc_o[...].astype(bf16)
        gin_s[k] = acc_i[...].astype(bf16)
        if k:
            target = {"exp": peers[k]}
            made = [
                send(out_s.at[k], eout_ref.at[me], o_send.at[k], o_recv.at[k], target),
                send(gin_s.at[k], ein_ref.at[me], i_send.at[k], i_recv.at[k], target),
            ]
        else:
            made = [
                pltpu.make_async_copy(out_s.at[0], eout_ref.at[me], o_send.at[0]),
                pltpu.make_async_copy(gin_s.at[0], ein_ref.at[me], i_send.at[0]),
            ]
        for copy in made:
            copy.start()
        returns.extend(made)

    wide = hidden // shds

    @pl.loop(0, shds)
    def _(f):
        columns = pl.ds(pl.multiple_of(f * wide, wide), wide)
        x = x_s[...].reshape(rows_all, width)
        g = g_s[...].reshape(rows_all, width)
        part = w_s.shape[1:3] + (wide,)
        w_s[0, :, :, columns] = mm_tn(x, gg_s[:, columns]).astype(bf16).reshape(part)
        w_s[1, :, :, columns] = mm_tn(x, ug_s[:, columns]).astype(bf16).reshape(part)
        n_s[f] = mm_tn(hid_s[:, columns], g).astype(bf16).reshape(n_s.shape[1:])

    stores = []
    deep = w_s.shape[2]
    base = hidden // 256 * deep
    tall = n_s.shape[2]
    for c in range(2):
        for b in range(hidden // 256):
            stores.append((w_s.at[c, :, :, pl.ds(256 * b, 256)], sums_ref.at[c, :, pl.ds(b * deep, deep), :]))
        for b in range(width // 256):
            stores.append((n_s.at[:, c, :, pl.ds(256 * b, 256)], sums_ref.at[c, :, pl.ds(base + b * tall, tall), :]))
    stores = [pltpu.make_async_copy(a, b, w_sem.at[i]) for i, (a, b) in enumerate(stores)]
    for copy in stores:
        copy.start()
    for copy in stores + returns:
        copy.wait()


def routed(slot_rows, chosen, grads, w_experts, w_narrower, shds):
    exps, cap, width = slot_rows.shape
    hidden = w_experts.shape[2]
    deep, tall = width // shds, hidden // shds // 2
    height = hidden // 256 * deep + width // 256 * tall
    big = lambda *shape: pltpu.VMEM(shape, bf16)
    sems = lambda n: pltpu.SemaphoreType.DMA((n,))
    return pl.pallas_call(
        functools.partial(routed_kernel, exps, shds),
        in_specs=[ANY] * 5,
        out_specs=[ANY] * 3,
        out_shape=[
            jax.ShapeDtypeStruct((exps, cap, width), bf16),
            jax.ShapeDtypeStruct((exps, cap, width), bf16),
            jax.ShapeDtypeStruct((2, shds, height, 256), bf16),
        ],
        scratch_shapes=[
            big(exps, cap, width),
            big(exps, cap, width),
            pltpu.VMEM(chosen.shape, f32),
            big(2, shds, deep, hidden),
            big(shds, 2, tall, width),
            big(exps * cap, hidden),
            big(exps * cap, hidden),
            big(exps * cap, hidden),
            big(exps, cap, width),
            big(exps, cap, width),
            pltpu.VMEM((cap, width), f32),
            pltpu.VMEM((cap, width), f32),
            sems(5), sems(exps), sems(exps), sems(exps), sems(exps),
            sems(exps), sems(exps), sems(exps), sems(exps),
            sems(2 * (hidden // 256 + width // 256)),
        ],
        compiler_params=params(collective_id=2, has_side_effects=True),
        cost_estimate=pl.CostEstimate(
            flops=18 * exps * cap * width * hidden,
            bytes_accessed=40_000_000,
            transcendentals=exps * cap * hidden,
        ),
        name="routed",
    )(
        slot_rows, chosen, grads,
        w_experts.reshape(2, shds, deep, hidden),
        w_narrower.reshape(shds, 2, tall, width),
    )


def ffn_kernel(
    x_ref, g_ref, wg_ref, wu_ref, wn_ref, sums_ref,
    out_ref, gin_ref, dwg_ref, dwu_ref, dwn_ref, swapped_ref,
    acc_out, acc_gin, hid_s, gg_s, ug_s, send_sem, recv_sem,
    *, tile,
):
    f = pl.program_id(0)
    last = pl.num_programs(0) - 1
    rows_all = x_ref.shape[0]
    group = lax.axis_index("grp")
    partner = {"grp": lax.bitwise_xor(group, 1)}
    swap = lambda: send(
        sums_ref.at[1 - lax.rem(group, 2)], swapped_ref, send_sem, recv_sem, partner
    )

    @pl.when(f == 0)
    def _():
        greet([partner])
        swap().start()
        acc_out[...] = jnp.zeros_like(acc_out)
        acc_gin[...] = jnp.zeros_like(acc_gin)

    wg, wu, wn = wg_ref[0], wu_ref[0], wn_ref[...]
    for row in range(0, rows_all, tile):
        rows = pl.ds(row, tile)
        x, g = x_ref[rows, :], g_ref[rows, :]
        hidden, gg, ug = gated(x, g, wg, wu, wn)
        hid_s[rows, :], gg_s[rows, :], ug_s[rows, :] = hidden, gg, ug
        acc_out[rows, :] += mm(hidden, wn)
        acc_gin[rows, :] += mm_nt(gg, wg) + mm_nt(ug, wu)
    dwg_ref[0] = mm_tn(x_ref[...], gg_s[...]).astype(dwg_ref.dtype)
    dwu_ref[0] = mm_tn(x_ref[...], ug_s[...]).astype(dwu_ref.dtype)
    dwn_ref[...] = mm_tn(hid_s[...], g_ref[...]).astype(dwn_ref.dtype)

    @pl.when(f == last)
    def _():
        out_ref[...] = acc_out[...].astype(out_ref.dtype)
        gin_ref[...] = acc_gin[...].astype(gin_ref.dtype)
        swap().wait()


def ffn(x, g, wgu, wn, sums, out_type, tile, name):
    rows, width = x.shape
    hidden = wn.shape[0]
    ft = 512
    return pl.pallas_call(
        functools.partial(ffn_kernel, tile=tile),
        grid=(hidden // ft,),
        in_specs=[
            once((rows, width)),
            once((rows, width)),
            pl.BlockSpec((1, width, ft), lambda f: (0, 0, f)),
            pl.BlockSpec((1, width, ft), lambda f: (1, 0, f)),
            pl.BlockSpec((ft, width), lambda f: (f, 0)),
            ANY,
        ],
        out_specs=[
            once((rows, width)),
            once((rows, width)),
            pl.BlockSpec((1, width, ft), lambda f: (0, 0, f)),
            pl.BlockSpec((1, width, ft), lambda f: (0, 0, f)),
            pl.BlockSpec((ft, width), lambda f: (f, 0)),
            ANY,
        ],
        out_shape=[
            jax.ShapeDtypeStruct((rows, width), out_type),
            jax.ShapeDtypeStruct((rows, width), out_type),
            jax.ShapeDtypeStruct((1, width, hidden), bf16),
            jax.ShapeDtypeStruct((1, width, hidden), bf16),
            jax.ShapeDtypeStruct((hidden, width), bf16),
            jax.ShapeDtypeStruct(sums.shape[1:], bf16),
        ],
        scratch_shapes=[
            pltpu.VMEM((rows, width), f32),
            pltpu.VMEM((rows, width), f32),
            pltpu.VMEM((rows, ft), bf16),
            pltpu.VMEM((rows, ft), bf16),
            pltpu.VMEM((rows, ft), bf16),
            pltpu.SemaphoreType.DMA,
            pltpu.SemaphoreType.DMA,
        ],
        compiler_params=params(("arbitrary",), collective_id=3, has_side_effects=True),
        cost_estimate=pl.CostEstimate(
            flops=18 * rows * width * hidden,
            bytes_accessed=12 * width * hidden + 8 * rows * width,
            transcendentals=rows * hidden,
        ),
        name=name,
    )(x, g, wgu, wgu, wn, sums)


def combine_kernel(
    mid_ref, sout_ref, sin_ref, g_ref, h2_ref, probs_ref, place_ref, eout_ref, ein_ref,
    gains_ref, wr_ref, wo_ref,
    block_ref, midg_ref, midb_ref, og_ref, gain_ref, rgrad_ref,
):
    step = pl.program_id(0)
    tile, width = mid_ref.shape
    experts_all, cap = eout_ref.shape[0], eout_ref.shape[1]
    slot = lax.broadcasted_iota(jnp.int32, (tile, cap), 1)
    g = g_ref[...].astype(f32)
    probs = probs_ref[...]
    spot = lax.broadcasted_iota(jnp.int32, probs.shape, 1)
    mixture = jnp.zeros((tile, width), f32)
    moe_in = jnp.zeros((tile, width), f32)
    pgrad = jnp.zeros(probs.shape, f32)
    for e in range(experts_all):
        hot = (slot == place_ref[:, e : e + 1]).astype(f32).astype(bf16)
        pair_out = mm(hot, eout_ref[e])
        mixture += probs[:, e : e + 1] * pair_out
        grad = jnp.sum(g * pair_out, axis=1, keepdims=True)
        pgrad = jnp.where(spot == e, grad, pgrad)
        moe_in += mm(hot, ein_ref[e])
    mid = mid_ref[...]
    block_ref[...] = (mid + sout_ref[...] + mixture).astype(bf16)
    inner = jnp.sum(pgrad * probs, axis=1, keepdims=True)
    lgrad = (probs * (pgrad - inner)).astype(bf16)
    h2_grad = moe_in + mm_nt(lgrad, wr_ref[...]) + sin_ref[...]
    r2 = lax.rsqrt(jnp.mean(mid * mid, axis=1, keepdims=True) + norm_eps)
    n2 = mid * r2
    d2 = h2_grad * gains_ref[1:2, :]
    mid_grad = g + r2 * (d2 - n2 * jnp.mean(d2 * n2, axis=1, keepdims=True))
    midb = mid_grad.astype(bf16)
    midg_ref[...] = mid_grad
    midb_ref[...] = midb
    half = wo_ref.shape[2]
    og = mm_nt(midb[:, :half], wo_ref[0]) + mm_nt(midb[:, half:], wo_ref[1])
    og_ref[...] = og.astype(bf16)
    gsum = jnp.sum(h2_grad * n2, axis=0, keepdims=True)
    rsum = mm_tn(lgrad, h2_ref[...])[:16]

    @pl.when(step == 0)
    def _():
        gain_ref[...] = jnp.zeros_like(gain_ref)
        rgrad_ref[...] = jnp.zeros_like(rgrad_ref)

    gain_ref[0:1, :] += gsum
    rgrad_ref[...] += rsum


def combine(mid, sout, sin, g, h2, probs, place_col, eout, ein, gains, wr, wo):
    seq, width = mid.shape
    tile = 256
    by_rows = pl.BlockSpec((tile, width), lambda i: (i, 0))
    lanes = pl.BlockSpec((tile, 128), lambda i: (i, 0))
    return pl.pallas_call(
        combine_kernel,
        grid=(seq // tile,),
        in_specs=[
            by_rows, by_rows, by_rows, by_rows, by_rows, lanes, lanes,
            once(eout.shape), once(ein.shape), once(gains.shape), once(wr.shape), once(wo.shape),
        ],
        out_specs=[by_rows, by_rows, by_rows, by_rows, whole_spec((8, width)), whole_spec((16, width))],
        out_shape=[
            jax.ShapeDtypeStruct((seq, width), bf16),
            jax.ShapeDtypeStruct((seq, width), f32),
            jax.ShapeDtypeStruct((seq, width), bf16),
            jax.ShapeDtypeStruct((seq, width), bf16),
            jax.ShapeDtypeStruct((8, width), f32),
            jax.ShapeDtypeStruct((16, width), f32),
        ],
        compiler_params=params(("arbitrary",)),
        cost_estimate=pl.CostEstimate(
            flops=11_000_000_000, bytes_accessed=30_000_000, transcendentals=0
        ),
        name="combine",
    )(mid, sout, sin, g, h2, probs, place_col, eout, ein, gains, wr, wo)


def backward_kernel(qkv_ref, og_ref, lse_ref, bidr_ref, bidc_ref, grad_ref, dk_s, dv_s):
    seq = og_ref.shape[0]
    tile = 256
    qs = qkv_ref[0] * jnp.asarray(0.125, bf16)
    k = qkv_ref[1]
    v = qkv_ref[2]
    kt = k.T
    og = og_ref[...]
    lane = lax.broadcasted_iota(jnp.int32, (tile, 128), 1)
    dk_s[...] = jnp.zeros_like(dk_s)
    dv_s[...] = jnp.zeros_like(dv_s)
    for q0 in range(0, seq, tile):
        kl = min(seq, q0 + 2 * tile)
        qt, ot = qs[q0 : q0 + tile], og[q0 : q0 + tile]
        allowed = bidc_ref[q0:kl, :] <= bidr_ref[0:1, q0 : q0 + tile]
        parts = []
        for head in range(2):
            own = (lane // 64) == head
            qm = jnp.where(own, qt, jnp.zeros_like(qt))
            om = jnp.where(own, ot, jnp.zeros_like(ot))
            lse = lse_ref[0, head : head + 1, q0 : q0 + tile]
            spans = ([(0, q0)] if q0 else []) + [(q0, kl)]
            kept = []
            delta = jnp.zeros((1, tile), f32)
            for low, high in spans:
                s = mm_nt(k[low:high], qm)
                if low == q0:
                    s = jnp.where(allowed, s, masked_score)
                p = jnp.exp(s - lse)
                dp = mm_nt(v[low:high], om)
                delta = delta + jnp.sum(p * dp, axis=0, keepdims=True)
                kept.append((low, high, p, dp))
            dq = jnp.zeros((64, tile), f32)
            for low, high, p, dp in kept:
                ds = (p * (dp - delta)).astype(bf16)
                dv_s[low:high, :] += mm(p.astype(bf16), om)
                dk_s[low:high, :] += mm(ds, qm)
                dq = dq + mm(kt[64 * head : 64 * head + 64, low:high], ds)
            parts.append(dq)
        dq = jnp.concatenate(parts, axis=0).T * 0.125
        grad_ref[0, q0 : q0 + tile, :] = dq.astype(bf16)
    grad_ref[1] = dk_s[...].astype(bf16)
    grad_ref[2] = dv_s[...].astype(bf16)


def attention_backward(qkv, og, lse, bid_row, bid_col):
    _, seq, width = qkv.shape
    pairs = width // 128
    return pl.pallas_call(
        backward_kernel,
        grid=(pairs,),
        in_specs=[
            pl.BlockSpec((3, seq, 128), lambda i: (0, 0, i)),
            pl.BlockSpec((seq, 128), lambda i: (0, i)),
            pl.BlockSpec((1, 8, seq), lambda i: (i, 0, 0)),
            once(bid_row.shape),
            once(bid_col.shape),
        ],
        out_specs=pl.BlockSpec((3, seq, 128), lambda i: (0, 0, i)),
        out_shape=jax.ShapeDtypeStruct((3, seq, width), bf16),
        scratch_shapes=[pltpu.VMEM((seq, 128), f32), pltpu.VMEM((seq, 128), f32)],
        compiler_params=params(("arbitrary",)),
        cost_estimate=pl.CostEstimate(
            flops=35_000_000_000, bytes_accessed=12_000_000, transcendentals=12_000_000
        ),
        name="attention_backward",
    )(qkv, og, lse, bid_row, bid_col)


def adam_update(weight, moment, square, gradient, step_rate, shrink_rate):
    moment_next = beta_one * moment + (1.0 - beta_one) * gradient
    square_next = beta_two * square + (1.0 - beta_two) * gradient * gradient
    direction = moment_next / first_fix / (jnp.sqrt(square_next / second_fix) + adam_eps)
    return (weight - step_rate * (direction + shrink_rate * weight), moment_next, square_next)


def pick(array, axis, index):
    return lax.dynamic_index_in_dim(array, index, axis, keepdims=False)


def sum_parts(array):
    return jnp.sum(array.astype(f32), axis=0)


def reduce_scatter(stacked, axes, groups, core):
    own, other = pick(stacked, 0, core), pick(stacked, 0, 1 - core)
    swap = [(i, i ^ 1) for i in range(groups)]
    arrived = lax.ppermute(other, "grp", swap)
    part = (own.astype(f32) + arrived.astype(f32)).astype(bf16)
    for axis in axes[:-1]:
        size = lax.axis_size(axis)
        part = part.reshape((size, part.shape[0] // size) + part.shape[1:])
        part = lax.all_to_all(part, axis, 0, 0, tiled=True)
        part = sum_parts(part).astype(bf16)
    return share(sum_parts(lax.all_to_all(part, axes[-1], 0, 0, tiled=True)), groups, core)


def share(part, groups, core):
    swap = [(i, i ^ 1) for i in range(groups)]
    both = jnp.zeros((2,) + part.shape, part.dtype)
    both = lax.dynamic_update_index_in_dim(both, part, core, 0)
    if groups > 2:
        return lax.psum(both, "grp")
    return lax.dynamic_update_index_in_dim(both, lax.ppermute(part, "grp", swap), 1 - core, 0)


def on_device(
    tokens_in, cotangent, block_ids, expert_ids,
    scales, moment_scales, square_scales, attend, moment_attend, square_attend,
    output, moment_output, square_output, router, moment_router, square_router,
    widener, moment_widener, square_widener, reducer, moment_reducer, square_reducer,
    experts, moment_experts, square_experts, narrower, moment_narrower, square_narrower,
):
    groups, exps, shds = (lax.axis_size(a) for a in ("grp", "exp", "shd"))
    spread = exps * shds
    core = lax.rem(lax.axis_index("grp"), 2)
    _, seq, width = tokens_in.shape
    hidden = reducer.shape[1 - 1] * spread
    experts_all = exps * experts.shape[0]
    rows = output.shape[0]
    half = width // 2
    tokens, g = tokens_in.reshape(seq, width), cotangent.reshape(seq, width)

    def gather(part, axes, order):
        names = ("grp",) + axes if order == "first" else axes + ("grp",)
        if groups == 2:
            return lax.all_gather(part, names, axis=0, tiled=False).reshape((-1,) + part.shape)
        wide = lax.all_gather(part, names, axis=0, tiled=False)
        shape = (groups, -1) if order == "first" else (-1, groups)
        wide = wide.reshape(shape + part.shape)
        wide = wide[:2] if order == "first" else wide[:, :2]
        return wide.reshape((-1,) + part.shape)

    both = ("exp", "shd")
    small = jnp.concatenate([router.reshape(-1), scales.reshape(-1)])
    small = jnp.pad(small, (0, half - small.shape[0])).reshape(1, half)
    small = jnp.pad(small, ((0, 15), (0, 0))).astype(bf16)
    columns = lambda a, n: pick(a.astype(bf16).reshape(n, 2, half), 1, core)
    payload = jnp.concatenate(
        [columns(attend, 3 * rows), columns(output, rows), small], axis=0
    )
    first = gather(payload, both, "first").reshape(2, spread, payload.shape[0], half)
    w_experts = gather(pick(experts.astype(bf16)[0], 0, core), ("shd",), "first").reshape(2, width, hidden)
    w_narrower = gather(
        pick(narrower.astype(bf16).reshape(2, -1, width), 0, core), ("shd",), "last"
    ).reshape(hidden, width)
    w_widener = gather(pick(widener.astype(bf16), 0, core), both, "first").reshape(2, width, hidden)
    w_reducer = gather(
        pick(reducer.astype(bf16).reshape(2, -1, width), 0, core), both, "last"
    ).reshape(hidden, width)

    wa = first[:, :, : 3 * rows].reshape(2, spread, 3, rows, half)
    wo = first[:, :, 3 * rows : 4 * rows].reshape(2, width, half)
    packed = first[0, :, 4 * rows]
    count = rows * experts_all
    w_router = packed[:, :count].reshape(width, experts_all)
    gains = packed[:, count : count + 2 * rows].reshape(spread, 2, rows)
    gains = gains.transpose(1, 0, 2).reshape(2, width).astype(f32)
    gains = jnp.pad(gains, ((0, 6), (0, 0)))
    wr = jnp.pad(w_router, ((0, 0), (0, 128 - experts_all)))
    wrt = jnp.pad(w_router.T, ((0, 16 - experts_all), (0, 0)))

    ids = expert_ids.reshape(seq, 2)
    every = jnp.arange(128, dtype=jnp.int32)[None, :]
    hot = (ids[:, 0:1] == every) | (ids[:, 1:2] == every)
    order = jnp.arange(seq, dtype=jnp.int32)
    before = (order[:, None] > order[None, :]).astype(bf16)
    placed = mm(before, hot.astype(bf16)).astype(jnp.int32)
    place_col = jnp.where(hot, placed, -1)
    place_row = place_col[:, :16].T
    bid = block_ids.reshape(1, seq)
    bid_row = jnp.broadcast_to(bid, (8, seq))
    bid_col = jnp.broadcast_to(bid.reshape(seq, 1), (seq, 256))

    lanes = -(-CAP // 128) * 128
    g_slots = place_gradients(g, place_row, experts_all, CAP)
    qkv, lse, o, mid, h2, probs, probst, g_landed = attention_forward(
        tokens, bid_row, bid_col, gains, wa, wo, wr, wrt, g_slots
    )
    slot_rows, chosen = dispatch(h2, place_row, probst, experts_all, CAP, lanes)
    eout, ein, sums = routed(slot_rows, chosen, g_landed, w_experts, w_narrower, shds)
    sout, sin, dsg, dsu, dsn, swapped = ffn(h2, g, w_widener, w_reducer, sums, f32, 256, "shared")
    part = (pick(sums, 0, core).astype(f32) + swapped.astype(f32)).astype(bf16)
    part = lax.psum_scatter(part, "shd", scatter_dimension=0, tiled=False)
    block_out, mid_grad, midb, og, gain_two, rgrad = combine(
        mid, sout, sin, g, h2, probs, place_col, eout, ein, gains, wr, wo
    )
    dqkv = attention_backward(qkv, og, lse, bid_row, bid_col)

    x = tokens.astype(f32)
    r1 = lax.rsqrt(jnp.mean(x * x, axis=1, keepdims=True) + norm_eps)
    n1 = x * r1
    h1 = (n1 * gains[0:1]).astype(bf16)
    attend_grad = jnp.einsum("nd,tnf->tdf", h1, dqkv, preferred_element_type=f32)
    output_grad = mm_tn(o, midb)
    w_full = wa.transpose(2, 1, 3, 0, 4).reshape(3, width, width)
    h1_grad = jnp.einsum("tnf,tdf->nd", dqkv, w_full, preferred_element_type=f32)
    gain_one = jnp.sum(h1_grad * n1, axis=0)
    d1 = h1_grad * gains[0:1]
    input_grad = mid_grad + r1 * (d1 - n1 * jnp.mean(d1 * n1, axis=1, keepdims=True))

    expert_sums = share(part, groups, core)
    deep = width // shds
    cut_at = hidden // 256 * deep
    g_experts = expert_sums[:, :cut_at].reshape(2, hidden // 256, deep, 256)
    g_experts = g_experts.transpose(0, 2, 1, 3).reshape(2, deep, hidden)
    g_narrower = expert_sums[:, cut_at:].reshape(2, width // 256, -1, 256)
    g_narrower = g_narrower.transpose(0, 2, 1, 3)
    small = jnp.concatenate(
        [rgrad[:experts_all], gain_one[None, :], gain_two[0:1]], axis=0
    ).reshape(-1, spread, rows).transpose(1, 0, 2).reshape(spread, 1, -1)
    small = jnp.pad(small, ((0, 0), (0, 15), (0, width - small.shape[2])))
    dense = jnp.concatenate(
        [
            attend_grad.astype(bf16).reshape(3, spread, rows, width).transpose(1, 0, 2, 3).reshape(spread, -1, width),
            output_grad.astype(bf16).reshape(spread, rows, width),
            jnp.concatenate([dsg, dsu], axis=0).reshape(2, spread, rows, hidden).transpose(1, 0, 2, 3).reshape(spread, -1, width),
            dsn.reshape(spread, -1, width),
            small.astype(bf16),
        ],
        axis=1,
    )
    total = dense.shape[1]
    dense = dense.reshape(spread, 2, total // 2, width).transpose(1, 0, 2, 3)
    dense = reduce_scatter(dense, both, groups, core).reshape(total, width)
    sizes = (3 * rows, rows, 2 * rows * hidden // width, reducer.shape[0])
    starts = (0, sizes[0], sizes[0] + sizes[1], sum(sizes[:3]))
    cut = lambda i, shape: dense[starts[i] : starts[i] + sizes[i]].reshape(shape)
    tiny = dense[sum(sizes)][: (experts_all + 2) * rows].reshape(experts_all + 2, rows)
    grads = (
        tiny[experts_all:],
        cut(0, attend.shape),
        cut(1, output.shape),
        tiny[:experts_all].T,
        cut(2, widener.shape),
        cut(3, reducer.shape),
        g_experts.reshape(experts.shape),
        g_narrower.reshape(narrower.shape),
    )
    masters = (scales, attend, output, router, widener, reducer, experts, narrower)
    moments = (
        moment_scales, moment_attend, moment_output, moment_router,
        moment_widener, moment_reducer, moment_experts, moment_narrower,
    )
    squares = (
        square_scales, square_attend, square_output, square_router,
        square_widener, square_reducer, square_experts, square_narrower,
    )
    results = [block_out.reshape(tokens_in.shape), input_grad.reshape(tokens_in.shape)]
    for kind in range(8):
        results.extend(
            adam_update(
                masters[kind], moments[kind], squares[kind], grads[kind],
                learning_rates[kind], decay_rates[kind],
            )
        )
    return tuple(results)


def solution(mesh):
    tokens = P(("grp", "exp", "shd"), None, None)
    both = ("exp", "shd")
    kinds = (
        P(None, both), P(None, both, None), P(both, None), P(both, None),
        P(None, both, None), P(both, None), P("exp", None, "shd", None), P("exp", "shd", None),
    )
    thrice = tuple(kind for kind in kinds for _ in range(3))
    return jax.shard_map(
        on_device,
        mesh=mesh,
        in_specs=(tokens, tokens, P(("grp", "exp", "shd"), None), tokens) + thrice,
        out_specs=(tokens, tokens) + thrice,
        check_vma=False,
    )
```

```python
import functools

import jax
import jax.numpy as jnp
from jax import lax
from jax.experimental import pallas as pl
from jax.experimental.pallas import tpu as pltpu
from jax.sharding import PartitionSpec as P

HEADS = 12
CAP = 576
VMEM_LIMIT = 60 * 1024 * 1024

norm_eps = 1e-06
adam_eps = 1e-08
beta_one = 0.9
beta_two = 0.95
first_fix = 1.0 - 0.9**10
second_fix = 1.0 - 0.95**10
learning_rates = (0.3, 0.02, 0.15, 0.02, 0.02, 0.012, 0.02, 0.012)
decay_rates = (0.0, 0.1, 0.1, 0.1, 0.1, 0.1, 0.1, 0.1)
masked_score = -1e30
bf16 = jnp.bfloat16
f32 = jnp.float32


def mm(a, b):
    return jnp.dot(a, b, preferred_element_type=f32)


def mm_nt(a, b):
    return lax.dot_general(a, b, (((1,), (1,)), ((), ())), preferred_element_type=f32)


def mm_tn(a, b):
    return lax.dot_general(a, b, (((0,), (0,)), ((), ())), preferred_element_type=f32)


def params(semantics=None, **more):
    return pltpu.CompilerParams(
        dimension_semantics=semantics, vmem_limit_bytes=VMEM_LIMIT, **more
    )


def whole_spec(shape, **more):
    zeros = (0,) * len(shape)
    return pl.BlockSpec(shape, lambda *_: zeros, **more)


def once(shape):
    return whole_spec(shape, pipeline_mode=pl.Buffered(1))


MESH = pl.DeviceIdType.MESH
ANY = pl.BlockSpec(memory_space=pl.ANY)


def greet(targets):
    barrier = pltpu.get_barrier_semaphore()
    for target in targets:
        pl.semaphore_signal(barrier, inc=1, device_id=target, device_id_type=MESH)
    pl.semaphore_wait(barrier, len(targets))


def send(src, dst, send_sem, recv_sem, target):
    return pltpu.make_async_remote_copy(
        src_ref=src, dst_ref=dst, send_sem=send_sem, recv_sem=recv_sem,
        device_id=target, device_id_type=MESH,
    )


def others(axis, count):
    me = lax.axis_index(axis)
    return [lax.bitwise_xor(me, k) for k in range(count)]


def gather_kernel(
    exps, shds,
    mine_ref, tiny_ref, g_ref, place_ref, full_ref, every_ref, slots_ref,
    own_sem, z_send, z_recv, p_send, p_recv, c_send, c_recv,
):
    columns, layers = others("exp", exps), others("shd", shds)
    group = lax.axis_index("grp")
    core = lax.rem(group, 2)
    partner = {"grp": lax.bitwise_xor(group, 1)}
    rows = mine_ref.shape[1]

    def spots(kz, kx):
        at = pl.ds(pl.multiple_of((columns[kx] * shds + layers[kz]) * rows, 16), rows)
        return full_ref.at[pl.ds(2 * core, 2), at, :], every_ref.at[at, :]

    greet(
        [{"shd": layer} for layer in layers[1:]]
        + [{"exp": column} for column in columns[1:]]
        + [partner]
    )
    started = []

    def begin(copies):
        for copy in copies:
            copy.start()
        started.extend(copies)
        return copies

    def both(sources, kz, kx, sem, far, index, target):
        return [
            send(a, b, sem.at[index + (i,)], far.at[index + (i,)], target)
            for i, (a, b) in enumerate(zip(sources, spots(kz, kx)))
        ]

    mine = (mine_ref, tiny_ref)
    local = [
        pltpu.make_async_copy(a, b, own_sem.at[i])
        for i, (a, b) in enumerate(zip(mine, spots(0, 0)))
    ]
    for copy in local:
        copy.start()
    down = [both(mine, 0, 0, z_send, z_recv, (k,), {"shd": layers[k]}) for k in range(1, shds)]
    for copies in down:
        begin(copies)
    across = {}
    for kx in range(1, exps):
        across[0, kx] = begin(both(mine, 0, 0, p_send, p_recv, (0, kx), {"exp": columns[kx]}))
    swaps = [send(mine_ref, spots(0, 0)[0], c_send.at[0, 0], c_recv.at[0, 0], partner)]
    swaps[0].start()
    for e in range(slots_ref.shape[0]):
        hot = slots_of(place_ref[e : e + 1, :], slots_ref.shape[1])
        slots_ref[e] = mm(hot, g_ref[...]).astype(bf16)

    def swap(kz, kx):
        here = spots(kz, kx)[0]
        copy = send(here, here, c_send.at[kz, kx], c_recv.at[kz, kx], partner)
        copy.start()
        swaps.append(copy)

    for kz in range(1, shds):
        for copy in down[kz - 1]:
            copy.wait_recv()
        for kx in range(1, exps):
            across[kz, kx] = begin(both(spots(kz, 0), kz, 0, p_send, p_recv, (kz, kx), {"exp": columns[kx]}))
        swap(kz, 0)
    for kz in range(shds):
        for kx in range(1, exps):
            for copy in across[kz, kx]:
                copy.wait_recv()
            swap(kz, kx)
    for copy in started:
        copy.wait_send()
    for copy in swaps + local:
        copy.wait()


def gather_first(mine, tiny, g, place_row, exps, shds, experts_all, cap):
    _, rows, width = mine.shape
    tall = exps * shds * rows
    sems = lambda *shape: pltpu.SemaphoreType.DMA(shape)
    return pl.pallas_call(
        functools.partial(gather_kernel, exps, shds),
        in_specs=[ANY, ANY, pl.BlockSpec(memory_space=pltpu.VMEM), pl.BlockSpec(memory_space=pltpu.VMEM)],
        out_specs=[ANY, ANY, pl.BlockSpec(memory_space=pltpu.VMEM)],
        out_shape=[
            jax.ShapeDtypeStruct((4, tall, width), bf16),
            jax.ShapeDtypeStruct((tall, 128), bf16),
            jax.ShapeDtypeStruct((experts_all, cap, width), bf16),
        ],
        scratch_shapes=[
            sems(2), sems(shds, 2), sems(shds, 2), sems(shds, exps, 2), sems(shds, exps, 2),
            sems(shds, exps), sems(shds, exps),
        ],
        compiler_params=params(collective_id=4, has_side_effects=True),
        cost_estimate=pl.CostEstimate(
            flops=40_000_000_000, bytes_accessed=10_000_000, transcendentals=0
        ),
        name="gather_first",
    )(mine, tiny, g, place_row)


def forward_kernel(
    exps,
    tok_ref, bidr_ref, bidc_ref, wa_ref, wo_ref, wr_ref, slots_ref,
    qkv_ref, lse_ref, o_ref, mid_ref, h2_ref, probs_ref, probst_ref, gains_ref, landed_ref, h1_ref,
    send_sem, recv_sem,
):
    pair = pl.program_id(0)
    me = lax.axis_index("exp")

    def copies():
        made = [pltpu.make_async_copy(slots_ref.at[me], landed_ref.at[0], send_sem.at[0])]
        for k in range(1, exps):
            peer = lax.bitwise_xor(me, k)
            made.append(
                send(slots_ref.at[peer], landed_ref.at[k], send_sem.at[k], recv_sem.at[k], {"exp": peer})
            )
        return made

    @pl.when(pair == 0)
    def _():
        greet([{"exp": lax.bitwise_xor(me, k)} for k in range(1, exps)])
        for copy in copies():
            copy.start()
    seq, width = tok_ref.shape
    tile = 256

    @pl.when(pair == 0)
    def _():
        gains_ref[...] = wr_ref[...].astype(f32).T[:8]
        for row in range(0, seq, tile):
            x = tok_ref[pl.ds(row, tile), :].astype(f32)
            r1 = lax.rsqrt(jnp.mean(x * x, axis=1, keepdims=True) + norm_eps)
            h1_ref[pl.ds(row, tile), :] = (x * r1 * gains_ref[4:5, :]).astype(bf16)

    h1 = h1_ref[...]
    for i in range(3):
        qkv_ref[i] = mm(h1, wa_ref[i]).astype(bf16)
    qs = qkv_ref[0] * jnp.asarray(0.125, bf16)
    k = qkv_ref[1]
    vt = qkv_ref[2].T
    lane = lax.broadcasted_iota(jnp.int32, (tile, 128), 1)
    for q0 in range(0, seq, tile):
        kl = min(seq, q0 + 2 * tile)
        qt = qs[q0 : q0 + tile]
        allowed = bidc_ref[q0:kl, :] <= bidr_ref[0:1, q0 : q0 + tile]
        parts = []
        for head in range(2):
            qm = jnp.where((lane // 64) == head, qt, jnp.zeros_like(qt))
            tail = jnp.where(allowed, mm_nt(k[q0:kl], qm), masked_score)
            top = jnp.max(tail, axis=0, keepdims=True)
            if q0:
                lead = mm_nt(k[:q0], qm)
                top = jnp.maximum(top, jnp.max(lead, axis=0, keepdims=True))
                lead = jnp.exp(lead - top)
            tail = jnp.exp(tail - top)
            total = jnp.sum(tail, axis=0, keepdims=True)
            if q0:
                total = total + jnp.sum(lead, axis=0, keepdims=True)
            inverse = 1.0 / total
            vh = vt[64 * head : 64 * head + 64]
            ot = mm(vh[:, q0:kl], (tail * inverse).astype(bf16))
            if q0:
                ot = ot + mm(vh[:, :q0], (lead * inverse).astype(bf16))
            lse_ref[0, head : head + 1, q0 : q0 + tile] = top + jnp.log(total)
            parts.append(ot)
        out = jnp.concatenate(parts, axis=0).T.astype(bf16)
        o_ref[q0 : q0 + tile, pl.ds(pl.multiple_of(pair * 128, 128), 128)] = out

    @pl.when(pair == pl.num_programs(0) - 1)
    def _():
        for row in range(0, seq, tile):
            rows = pl.ds(row, tile)
            mid = tok_ref[rows, :].astype(f32) + mm(o_ref[rows, :], wo_ref[0])
            mid_ref[rows, :] = mid
            r2 = lax.rsqrt(jnp.mean(mid * mid, axis=1, keepdims=True) + norm_eps)
            h2 = (mid * r2 * gains_ref[5:6, :]).astype(bf16)
            h2_ref[rows, :] = h2
            logits = mm(h2, wr_ref[...])
            spot = lax.broadcasted_iota(jnp.int32, logits.shape, 1)
            logits = jnp.where(spot < 4, logits, masked_score)
            e = jnp.exp(logits - jnp.max(logits, axis=1, keepdims=True))
            probs_ref[rows, :] = e / jnp.sum(e, axis=1, keepdims=True)
        routers = gains_ref[...].astype(bf16)
        logits = mm_nt(jnp.concatenate([routers, routers], axis=0), h2_ref[...])
        spot = lax.broadcasted_iota(jnp.int32, logits.shape, 0)
        logits = jnp.where(spot < 4, logits, masked_score)
        e = jnp.exp(logits - jnp.max(logits, axis=0, keepdims=True))
        probst_ref[...] = e / jnp.sum(e, axis=0, keepdims=True)
        for copy in copies():
            copy.wait()


def attention_forward(tokens, bid_row, bid_col, full, wr, slots):
    exps = slots.shape[0]
    seq, width = tokens.shape
    pairs = width // 128
    return pl.pallas_call(
        functools.partial(forward_kernel, exps),
        grid=(pairs,),
        in_specs=[
            once((seq, width)),
            once(bid_row.shape),
            once(bid_col.shape),
            pl.BlockSpec((3, width, 128), lambda i: (0, 0, i)),
            pl.BlockSpec((1, width, width), lambda i: (3, 0, 0), pipeline_mode=pl.Buffered(1)),
            once(wr.shape),
            ANY,
        ],
        out_specs=[
            pl.BlockSpec((3, seq, 128), lambda i: (0, 0, i)),
            pl.BlockSpec((1, 8, seq), lambda i: (i, 0, 0)),
            whole_spec((seq, width)),
            whole_spec((seq, width)),
            whole_spec((seq, width)),
            whole_spec((seq, 128)),
            whole_spec((16, seq)),
            whole_spec((8, width)),
            ANY,
        ],
        out_shape=[
            jax.ShapeDtypeStruct((3, seq, width), bf16),
            jax.ShapeDtypeStruct((pairs, 8, seq), f32),
            jax.ShapeDtypeStruct((seq, width), bf16),
            jax.ShapeDtypeStruct((seq, width), f32),
            jax.ShapeDtypeStruct((seq, width), bf16),
            jax.ShapeDtypeStruct((seq, 128), f32),
            jax.ShapeDtypeStruct((16, seq), f32),
            jax.ShapeDtypeStruct((8, width), f32),
            jax.ShapeDtypeStruct(slots.shape, bf16),
        ],
        scratch_shapes=[
            pltpu.VMEM((seq, width), bf16),
            pltpu.SemaphoreType.DMA((exps,)),
            pltpu.SemaphoreType.DMA((exps,)),
        ],
        compiler_params=params(("arbitrary",), collective_id=1, has_side_effects=True),
        cost_estimate=pl.CostEstimate(
            flops=30_000_000_000, bytes_accessed=20_000_000, transcendentals=12_000_000
        ),
        name="attention_forward",
    )(tokens, bid_row, bid_col, full, full, wr, slots)


def slots_of(place_row, cap):
    slot = lax.broadcasted_iota(jnp.int32, (cap, place_row.shape[1]), 0)
    return (slot == place_row).astype(f32).astype(bf16)


def dispatch_kernel(h2_ref, place_ref, probst_ref, rows_ref, chosen_ref):
    expert = pl.program_id(0)
    cap = rows_ref.shape[1]
    lanes = chosen_ref.shape[2]
    row = place_ref[pl.ds(expert, 1), :]
    rows_ref[0] = mm(slots_of(row, cap), h2_ref[...]).astype(bf16)
    value = probst_ref[pl.ds(expert, 1), :]
    high = value.astype(bf16)
    rest = value - high.astype(f32)
    middle = rest.astype(bf16)
    low = (rest - middle.astype(f32)).astype(bf16)
    eight = lambda a: jnp.broadcast_to(a.astype(f32), (8, row.shape[1])).astype(bf16)
    hot = slots_of(row, lanes)
    chosen = mm_nt(eight(high), hot) + mm_nt(eight(middle), hot) + mm_nt(eight(low), hot)
    chosen_ref[0] = chosen


def dispatch(h2, place_row, probst, experts_all, cap, lanes):
    seq, width = h2.shape
    return pl.pallas_call(
        dispatch_kernel,
        grid=(experts_all,),
        in_specs=[once(h2.shape), once(place_row.shape), once(probst.shape)],
        out_specs=[
            pl.BlockSpec((1, cap, width), lambda e: (e, 0, 0)),
            pl.BlockSpec((1, 8, lanes), lambda e: (e, 0, 0)),
        ],
        out_shape=[
            jax.ShapeDtypeStruct((experts_all, cap, width), bf16),
            jax.ShapeDtypeStruct((experts_all, 8, lanes), f32),
        ],
        compiler_params=params(("arbitrary",)),
        cost_estimate=pl.CostEstimate(
            flops=5_000_000_000, bytes_accessed=6_000_000, transcendentals=0
        ),
        name="dispatch",
    )(h2, place_row, probst)


def gated(x, g, wg, wu, wn):
    gate, up = mm(x, wg), mm(x, wu)
    sig = 1.0 / (1.0 + jnp.exp(-gate))
    active = gate * sig
    slope = sig * (1.0 + gate * (1.0 - sig))
    hidden = (active * up).astype(bf16)
    hgrad = mm_nt(g, wn)
    return hidden, (hgrad * up * slope).astype(bf16), (hgrad * active).astype(bf16)


def routed_kernel(
    exps, shds,
    rows_ref, chosen_ref, grads_ref, packed_ref,
    eout_ref, ein_ref, own_ref, swapped_ref,
    x_s, g_s, c_s, w_s, n_s, hid_s, gg_s, ug_s, out_s, gin_s, acc_o, acc_i,
    load_sem, x_send, x_recv, c_send, c_recv, o_send, o_recv, i_send, i_recv, w_sem, s_send, s_recv,
):
    me = lax.axis_index("exp")
    _, cap, width = x_s.shape
    hidden = hid_s.shape[1]
    rows_all = exps * cap
    peers = [lax.bitwise_xor(me, k) for k in range(exps)]
    group = lax.axis_index("grp")
    core = lax.rem(group, 2)
    partner = {"grp": lax.bitwise_xor(group, 1)}
    greet([{"exp": peer} for peer in peers[1:]] + [partner])
    deep, tall = w_s.shape[2], n_s.shape[2]
    base = hidden // 256 * deep
    wide_at = lambda b: pl.ds(pl.multiple_of(b * deep, 16), deep)
    narrow_at = lambda b: pl.ds(base + b * tall, tall)
    lanes_at = lambda b: pl.ds(pl.multiple_of(256 * b, 256), 256)

    chosen, arriving = [], []
    for k in range(1, exps):
        target = {"exp": peers[k]}
        chosen.append(send(chosen_ref.at[peers[k]], c_s.at[k], c_send.at[k], c_recv.at[k], target))
        arriving.append(send(rows_ref.at[peers[k]], x_s.at[k], x_send.at[k], x_recv.at[k], target))
    for copy in chosen + arriving:
        copy.start()
    loads = [
        pltpu.make_async_copy(rows_ref.at[me], x_s.at[0], load_sem.at[0]),
        pltpu.make_async_copy(chosen_ref.at[me], c_s.at[0], load_sem.at[1]),
        pltpu.make_async_copy(grads_ref, g_s, load_sem.at[2]),
    ]
    for c in range(2):
        for b in range(hidden // 256):
            loads.append(
                pltpu.make_async_copy(
                    packed_ref.at[c, :, wide_at(b), :], w_s.at[c, :, :, lanes_at(b)], load_sem.at[len(loads)]
                )
            )
        for b in range(width // 256):
            loads.append(
                pltpu.make_async_copy(
                    packed_ref.at[c, :, narrow_at(b), :], n_s.at[:, c, :, lanes_at(b)], load_sem.at[len(loads)]
                )
            )
    for copy in loads:
        copy.start()
    for copy in loads:
        copy.wait()

    ft = 256
    returns = []
    for k in range(exps):
        if k:
            chosen[k - 1].wait()
            arriving[k - 1].wait()
        scale = c_s[k].T[:cap, 0:1]
        g_s[k] = (g_s[k].astype(f32) * scale).astype(bf16)
        acc_o[...] = jnp.zeros_like(acc_o)
        acc_i[...] = jnp.zeros_like(acc_i)

        @pl.loop(0, hidden // ft)
        def _(f):
            columns = pl.ds(pl.multiple_of(f * ft, ft), ft)
            wg = w_s[0, :, :, columns].reshape(width, ft)
            wu = w_s[1, :, :, columns].reshape(width, ft)
            wn = n_s[f // 2, f % 2]
            hid, gg, ug = gated(x_s[k], g_s[k], wg, wu, wn)
            hid_s[pl.ds(k * cap, cap), columns] = hid
            gg_s[pl.ds(k * cap, cap), columns] = gg
            ug_s[pl.ds(k * cap, cap), columns] = ug
            acc_o[...] += mm(hid, wn)
            acc_i[...] += mm_nt(gg, wg) + mm_nt(ug, wu)

        out_s[k] = acc_o[...].astype(bf16)
        gin_s[k] = acc_i[...].astype(bf16)
        if k:
            target = {"exp": peers[k]}
            made = [
                send(out_s.at[k], eout_ref.at[me], o_send.at[k], o_recv.at[k], target),
                send(gin_s.at[k], ein_ref.at[me], i_send.at[k], i_recv.at[k], target),
            ]
        else:
            made = [
                pltpu.make_async_copy(out_s.at[0], eout_ref.at[me], o_send.at[0]),
                pltpu.make_async_copy(gin_s.at[0], ein_ref.at[me], i_send.at[0]),
            ]
        for copy in made:
            copy.start()
        returns.extend(made)

    wide = hidden // shds
    per = wide // 256

    def stores(f):
        made = []
        for b in range(per):
            block = per * f + b
            here = (slice(None), wide_at(block), slice(None))
            made.append((w_s.at[core, :, :, lanes_at(block)], own_ref.at[here]))
            made.append((w_s.at[1 - core, :, :, lanes_at(block)], swapped_ref.at[here]))
        for b in range(width // 256):
            made.append((n_s.at[f, core, :, lanes_at(b)], own_ref.at[f, narrow_at(b), :]))
            made.append((n_s.at[f, 1 - core, :, lanes_at(b)], swapped_ref.at[f, narrow_at(b), :]))
        copies = []
        for i, (a, b) in enumerate(made):
            if i % 2:
                copies.append(send(a, b, s_send.at[f, i // 2], s_recv.at[f, i // 2], partner))
            else:
                copies.append(pltpu.make_async_copy(a, b, w_sem.at[f, i // 2]))
        return copies

    @pl.loop(0, shds)
    def _(f):
        columns = pl.ds(pl.multiple_of(f * wide, wide), wide)
        x = x_s[...].reshape(rows_all, width)
        g = g_s[...].reshape(rows_all, width)
        part = w_s.shape[1:3] + (wide,)
        w_s[0, :, :, columns] = mm_tn(x, gg_s[:, columns]).astype(bf16).reshape(part)
        w_s[1, :, :, columns] = mm_tn(x, ug_s[:, columns]).astype(bf16).reshape(part)
        n_s[f] = mm_tn(hid_s[:, columns], g).astype(bf16).reshape(n_s.shape[1:])
        for copy in stores(f):
            copy.start()

    for copy in returns:
        copy.wait()

    @pl.loop(0, shds)
    def _(f):
        for copy in stores(f):
            copy.wait()


def routed(slot_rows, chosen, grads, packed, hidden):
    exps, cap, width = slot_rows.shape
    shds, height = packed.shape[1:3]
    deep, tall = width // shds, hidden // shds // 2
    pieces = hidden // shds // 256 + width // 256
    big = lambda *shape: pltpu.VMEM(shape, bf16)
    sems = lambda *n: pltpu.SemaphoreType.DMA(n)
    return pl.pallas_call(
        functools.partial(routed_kernel, exps, shds),
        in_specs=[ANY] * 4,
        out_specs=[ANY] * 4,
        out_shape=[
            jax.ShapeDtypeStruct((exps, cap, width), bf16),
            jax.ShapeDtypeStruct((exps, cap, width), bf16),
            jax.ShapeDtypeStruct((shds, height, 256), bf16),
            jax.ShapeDtypeStruct((shds, height, 256), bf16),
        ],
        scratch_shapes=[
            big(exps, cap, width),
            big(exps, cap, width),
            pltpu.VMEM(chosen.shape, f32),
            big(2, shds, deep, hidden),
            big(shds, 2, tall, width),
            big(exps * cap, hidden),
            big(exps * cap, hidden),
            big(exps * cap, hidden),
            big(exps, cap, width),
            big(exps, cap, width),
            pltpu.VMEM((cap, width), f32),
            pltpu.VMEM((cap, width), f32),
            sems(3 + 2 * (hidden // 256 + width // 256)),
            sems(exps), sems(exps), sems(exps), sems(exps),
            sems(exps), sems(exps), sems(exps), sems(exps),
            sems(shds, pieces), sems(shds, pieces), sems(shds, pieces),
        ],
        compiler_params=params(collective_id=2, has_side_effects=True),
        cost_estimate=pl.CostEstimate(
            flops=18 * exps * cap * width * hidden,
            bytes_accessed=40_000_000,
            transcendentals=exps * cap * hidden,
        ),
        name="routed",
    )(slot_rows, chosen, grads, packed)


def ffn_kernel(
    x_ref, g_ref, wg_ref, wu_ref, wn_ref,
    out_ref, gin_ref, own_a, swapped_a, own_b, swapped_b,
    acc_out, acc_gin, hid_s, gg_s, ug_s, wide_s, narrow_s, own_sem, send_sem, recv_sem,
    *, tile,
):
    f = pl.program_id(0)
    last = pl.num_programs(0) - 1
    rows_all, width = x_ref.shape
    group = lax.axis_index("grp")
    core = lax.rem(group, 2)
    partner = {"grp": lax.bitwise_xor(group, 1)}
    _, _, _, ft = wide_s.shape
    _, shards, _, tall, _ = narrow_s.shape

    def stores(step):
        columns = pl.ds(pl.multiple_of(step * ft, ft), ft)
        at = pl.ds(step * shards, shards)
        return [
            pltpu.make_async_copy(wide_s.at[step, core], own_a.at[:, columns], own_sem.at[step, 0]),
            pltpu.make_async_copy(narrow_s.at[step, :, core], own_b.at[at], own_sem.at[step, 1]),
            send(
                wide_s.at[step, 1 - core], swapped_a.at[:, columns],
                send_sem.at[step, 0], recv_sem.at[step, 0], partner,
            ),
            send(
                narrow_s.at[step, :, 1 - core], swapped_b.at[at],
                send_sem.at[step, 1], recv_sem.at[step, 1], partner,
            ),
        ]

    @pl.when(f == 0)
    def _():
        greet([partner])
        acc_out[...] = jnp.zeros_like(acc_out)
        acc_gin[...] = jnp.zeros_like(acc_gin)

    deep = wg_ref.shape[2] // 2
    wide = lambda ref: jnp.concatenate(
        [ref[0, :, :deep].reshape(width, 256), ref[0, :, deep:].reshape(width, 256)], axis=1
    )
    wg, wu = wide(wg_ref), wide(wu_ref)
    narrow = [
        jnp.concatenate([wn_ref[c, s, tall * b : tall * (b + 1)] for b in range(width // 256)], axis=1)
        for s in range(shards)
        for c in range(2)
    ]
    wn = jnp.concatenate(narrow, axis=0)
    for row in range(0, rows_all, tile):
        rows = pl.ds(row, tile)
        x, g = x_ref[rows, :], g_ref[rows, :]
        hidden, gg, ug = gated(x, g, wg, wu, wn)
        hid_s[rows, :], gg_s[rows, :], ug_s[rows, :] = hidden, gg, ug
        acc_out[rows, :] += mm(hidden, wn)
        acc_gin[rows, :] += mm_nt(gg, wg) + mm_nt(ug, wu)
    wide_s[f, 0] = mm_tn(x_ref[...], gg_s[...]).astype(bf16)
    wide_s[f, 1] = mm_tn(x_ref[...], ug_s[...]).astype(bf16)
    narrow_s[f] = mm_tn(hid_s[...], g_ref[...]).astype(bf16).reshape(narrow_s.shape[1:])
    for copy in stores(f):
        copy.start()

    @pl.when(f == last)
    def _():
        out_ref[...] = acc_out[...].astype(out_ref.dtype)
        gin_ref[...] = acc_gin[...].astype(gin_ref.dtype)

        @pl.loop(0, pl.num_programs(0))
        def _(step):
            for copy in stores(step):
                copy.wait()


def ffn(x, g, packed, hidden, out_type, tile, name):
    rows, width = x.shape
    _, spread, height, _ = packed.shape
    ft = 512
    steps = hidden // ft
    deep, tall = width // spread, hidden // spread // 2
    shards = spread // steps
    base = hidden // 256 * deep
    narrow_high = height - base
    sems = pltpu.SemaphoreType.DMA((steps, 2))
    return pl.pallas_call(
        functools.partial(ffn_kernel, tile=tile),
        grid=(steps,),
        in_specs=[
            once((rows, width)),
            once((rows, width)),
            pl.BlockSpec((1, spread, 2 * deep, 256), lambda f: (0, 0, f, 0)),
            pl.BlockSpec((1, spread, 2 * deep, 256), lambda f: (1, 0, f, 0)),
            pl.BlockSpec((2, shards, narrow_high, 256), lambda f: (0, f, base // narrow_high, 0)),
        ],
        out_specs=[once((rows, width)), once((rows, width)), ANY, ANY, ANY, ANY],
        out_shape=[
            jax.ShapeDtypeStruct((rows, width), out_type),
            jax.ShapeDtypeStruct((rows, width), out_type),
            jax.ShapeDtypeStruct((width, hidden), bf16),
            jax.ShapeDtypeStruct((width, hidden), bf16),
            jax.ShapeDtypeStruct((spread, tall, width), bf16),
            jax.ShapeDtypeStruct((spread, tall, width), bf16),
        ],
        scratch_shapes=[
            pltpu.VMEM((rows, width), f32),
            pltpu.VMEM((rows, width), f32),
            pltpu.VMEM((rows, ft), bf16),
            pltpu.VMEM((rows, ft), bf16),
            pltpu.VMEM((rows, ft), bf16),
            pltpu.VMEM((steps, 2, width, ft), bf16),
            pltpu.VMEM((steps, shards, 2, tall, width), bf16),
            sems, sems, sems,
        ],
        compiler_params=params(("arbitrary",), collective_id=3, has_side_effects=True),
        cost_estimate=pl.CostEstimate(
            flops=18 * rows * width * hidden,
            bytes_accessed=12 * width * hidden + 8 * rows * width,
            transcendentals=rows * hidden,
        ),
        name=name,
    )(x, g, packed, packed, packed)


def plane_copies(exps, part_ref, landed_ref, send_sem, recv_sem):
    columns = others("exp", exps)
    made = [pltpu.make_async_copy(part_ref.at[columns[0]], landed_ref.at[0], send_sem.at[0])]
    for k in range(1, exps):
        made.append(
            send(
                part_ref.at[columns[k]], landed_ref.at[k],
                send_sem.at[k], recv_sem.at[k], {"exp": columns[k]},
            )
        )
    return made


def plane_begin(exps, *refs):
    greet([{"exp": column} for column in others("exp", exps)[1:]])
    for copy in plane_copies(exps, *refs):
        copy.start()


def plane_end(exps, *refs):
    for copy in plane_copies(exps, *refs):
        copy.wait()


def pair_sems(count):
    return [pltpu.SemaphoreType.DMA((count,)), pltpu.SemaphoreType.DMA((count,))]


def combine_kernel(
    mid_ref, sout_ref, sin_ref, g_ref, h2_ref, probs_ref, place_ref, eout_ref, ein_ref,
    gains_ref, wr_ref, wo_ref, part_ref,
    block_ref, midg_ref, midb_ref, og_ref, gain_ref, rgrad_ref, landed_ref,
    send_sem, recv_sem,
):
    step = pl.program_id(0)
    exps = part_ref.shape[0]
    exchange = (exps, part_ref, landed_ref, send_sem, recv_sem)

    @pl.when(step == 0)
    def _():
        plane_begin(*exchange)

    tile, width = mid_ref.shape
    experts_all, cap = eout_ref.shape[0], eout_ref.shape[1]
    slot = lax.broadcasted_iota(jnp.int32, (tile, cap), 1)
    g = g_ref[...].astype(f32)
    probs = probs_ref[...]
    spot = lax.broadcasted_iota(jnp.int32, probs.shape, 1)
    mixture = jnp.zeros((tile, width), f32)
    moe_in = jnp.zeros((tile, width), f32)
    pgrad = jnp.zeros(probs.shape, f32)
    for e in range(experts_all):
        hot = (slot == place_ref[:, e : e + 1]).astype(f32).astype(bf16)
        pair_out = mm(hot, eout_ref[e])
        mixture += probs[:, e : e + 1] * pair_out
        grad = jnp.sum(g * pair_out, axis=1, keepdims=True)
        pgrad = jnp.where(spot == e, grad, pgrad)
        moe_in += mm(hot, ein_ref[e])
    mid = mid_ref[...]
    block_ref[...] = (mid + sout_ref[...] + mixture).astype(bf16)
    inner = jnp.sum(pgrad * probs, axis=1, keepdims=True)
    lgrad = (probs * (pgrad - inner)).astype(bf16)
    h2_grad = moe_in + mm_nt(lgrad, wr_ref[...]) + sin_ref[...]
    r2 = lax.rsqrt(jnp.mean(mid * mid, axis=1, keepdims=True) + norm_eps)
    n2 = mid * r2
    d2 = h2_grad * gains_ref[5:6, :]
    mid_grad = g + r2 * (d2 - n2 * jnp.mean(d2 * n2, axis=1, keepdims=True))
    midb = mid_grad.astype(bf16)
    midg_ref[...] = mid_grad
    midb_ref[...] = midb
    og_ref[...] = mm_nt(midb, wo_ref[0]).astype(bf16)
    gsum = jnp.sum(h2_grad * n2, axis=0, keepdims=True)
    rsum = mm_tn(lgrad, h2_ref[...])[:8]

    @pl.when(step == 0)
    def _():
        gain_ref[...] = jnp.zeros_like(gain_ref)
        rgrad_ref[...] = jnp.zeros_like(rgrad_ref)

    gain_ref[0:1, :] += gsum
    rgrad_ref[...] += rsum

    @pl.when(step == pl.num_programs(0) - 1)
    def _():
        plane_end(*exchange)


def combine(mid, sout, sin, g, h2, probs, place_col, eout, ein, gains, wr, full, part):
    seq, width = mid.shape
    tile = 256
    by_rows = pl.BlockSpec((tile, width), lambda i: (i, 0))
    lanes = pl.BlockSpec((tile, 128), lambda i: (i, 0))
    return pl.pallas_call(
        combine_kernel,
        grid=(seq // tile,),
        in_specs=[
            by_rows, by_rows, by_rows, by_rows, by_rows, lanes, lanes,
            once(eout.shape), once(ein.shape), once(gains.shape), once(wr.shape),
            pl.BlockSpec((1, width, width), lambda i: (3, 0, 0), pipeline_mode=pl.Buffered(1)),
            ANY,
        ],
        out_specs=[by_rows, by_rows, by_rows, by_rows, whole_spec((8, width)), whole_spec((8, width)), ANY],
        out_shape=[
            jax.ShapeDtypeStruct((seq, width), bf16),
            jax.ShapeDtypeStruct((seq, width), f32),
            jax.ShapeDtypeStruct((seq, width), bf16),
            jax.ShapeDtypeStruct((seq, width), bf16),
            jax.ShapeDtypeStruct((8, width), f32),
            jax.ShapeDtypeStruct((8, width), f32),
            jax.ShapeDtypeStruct(part.shape, bf16),
        ],
        scratch_shapes=pair_sems(part.shape[0]),
        compiler_params=params(("arbitrary",), collective_id=5, has_side_effects=True),
        cost_estimate=pl.CostEstimate(
            flops=11_000_000_000, bytes_accessed=30_000_000, transcendentals=0
        ),
        name="combine",
    )(mid, sout, sin, g, h2, probs, place_col, eout, ein, gains, wr, full, part)


def backward_kernel(
    qkv_ref, og_ref, lse_ref, bidr_ref, bidc_ref, part_ref,
    grad_ref, landed_ref, dk_s, dv_s, send_sem, recv_sem,
):
    step = pl.program_id(0)
    exps = part_ref.shape[0]
    exchange = (exps, part_ref, landed_ref, send_sem, recv_sem)

    @pl.when(step == 0)
    def _():
        plane_begin(*exchange)

    seq = og_ref.shape[0]
    tile = 256
    qs = qkv_ref[0] * jnp.asarray(0.125, bf16)
    k = qkv_ref[1]
    v = qkv_ref[2]
    kt = k.T
    og = og_ref[...]
    lane = lax.broadcasted_iota(jnp.int32, (tile, 128), 1)
    dk_s[...] = jnp.zeros_like(dk_s)
    dv_s[...] = jnp.zeros_like(dv_s)
    for q0 in range(0, seq, tile):
        kl = min(seq, q0 + 2 * tile)
        qt, ot = qs[q0 : q0 + tile], og[q0 : q0 + tile]
        allowed = bidc_ref[q0:kl, :] <= bidr_ref[0:1, q0 : q0 + tile]
        parts = []
        for head in range(2):
            own = (lane // 64) == head
            qm = jnp.where(own, qt, jnp.zeros_like(qt))
            om = jnp.where(own, ot, jnp.zeros_like(ot))
            lse = lse_ref[0, head : head + 1, q0 : q0 + tile]
            spans = ([(0, q0)] if q0 else []) + [(q0, kl)]
            kept = []
            delta = jnp.zeros((1, tile), f32)
            for low, high in spans:
                s = mm_nt(k[low:high], qm)
                if low == q0:
                    s = jnp.where(allowed, s, masked_score)
                p = jnp.exp(s - lse)
                dp = mm_nt(v[low:high], om)
                delta = delta + jnp.sum(p * dp, axis=0, keepdims=True)
                kept.append((low, high, p, dp))
            dq = jnp.zeros((64, tile), f32)
            for low, high, p, dp in kept:
                ds = (p * (dp - delta)).astype(bf16)
                dv_s[low:high, :] += mm(p.astype(bf16), om)
                dk_s[low:high, :] += mm(ds, qm)
                dq = dq + mm(kt[64 * head : 64 * head + 64, low:high], ds)
            parts.append(dq)
        dq = jnp.concatenate(parts, axis=0).T * 0.125
        grad_ref[0, q0 : q0 + tile, :] = dq.astype(bf16)
    grad_ref[1] = dk_s[...].astype(bf16)
    grad_ref[2] = dv_s[...].astype(bf16)

    @pl.when(step == pl.num_programs(0) - 1)
    def _():
        plane_end(*exchange)


def attention_backward(qkv, og, lse, bid_row, bid_col, part):
    _, seq, width = qkv.shape
    pairs = width // 128
    return pl.pallas_call(
        backward_kernel,
        grid=(pairs,),
        in_specs=[
            pl.BlockSpec((3, seq, 128), lambda i: (0, 0, i)),
            pl.BlockSpec((seq, 128), lambda i: (0, i)),
            pl.BlockSpec((1, 8, seq), lambda i: (i, 0, 0)),
            once(bid_row.shape),
            once(bid_col.shape),
            ANY,
        ],
        out_specs=[pl.BlockSpec((3, seq, 128), lambda i: (0, 0, i)), ANY],
        out_shape=[
            jax.ShapeDtypeStruct((3, seq, width), bf16),
            jax.ShapeDtypeStruct(part.shape, bf16),
        ],
        scratch_shapes=[pltpu.VMEM((seq, 128), f32), pltpu.VMEM((seq, 128), f32)]
        + pair_sems(part.shape[0]),
        compiler_params=params(("arbitrary",), collective_id=6, has_side_effects=True),
        cost_estimate=pl.CostEstimate(
            flops=35_000_000_000, bytes_accessed=12_000_000, transcendentals=12_000_000
        ),
        name="attention_backward",
    )(qkv, og, lse, bid_row, bid_col, part)


def finish_kernel(
    exps, shds,
    dqkv_ref, tok_ref, midg_ref, o_ref, midb_ref, w_ref, gains_ref, gain2_ref, rgrad_ref, la_ref, lb_ref,
    igrad_ref, sw_ref, sa_ref, sb_ref, st_ref,
    h1_s, stack_s, pair_s, tiny_s, tpair_s, plane_s, tplane_s, qa_s, qb_s, za_s, zb_s, r_s, zr_s, tr_s, tz_s,
    fw_s, fa_s, fb_s,
    pair_send, pair_recv, plane_send, plane_recv, line_send, line_recv, last_send, last_recv, own_sem,
):
    columns, layers = others("exp", exps), others("shd", shds)
    group = lax.axis_index("grp")
    core = lax.rem(group, 2)
    partner = {"grp": lax.bitwise_xor(group, 1)}
    seq, width = tok_ref.shape
    tile = 256
    greet(
        [{"shd": layer} for layer in layers[1:]]
        + [{"exp": column} for column in columns[1:]]
        + [partner]
    )

    def total(ref):
        value = ref[0].astype(f32)
        for k in range(1, ref.shape[0]):
            value = value + ref[k].astype(f32)
        return value

    waits = []

    def begin(copy):
        copy.start()
        waits.append(copy)
        return copy

    def line(part_s, landed_s, kind):
        return [
            begin(
                send(
                    part_s.at[layers[k]], landed_s.at[k],
                    line_send.at[kind, k], line_recv.at[kind, k], {"shd": layers[k]},
                )
            )
            for k in range(1, shds)
        ]

    for z in range(shds):
        qa_s[z] = sum([la_ref[k, z].astype(f32) for k in range(1, exps)], la_ref[0, z].astype(f32)).astype(bf16)
        qb_s[z] = sum([lb_ref[k, z].astype(f32) for k in range(1, exps)], lb_ref[0, z].astype(f32)).astype(bf16)
    line_a, line_b = line(qa_s, za_s, 0), line(qb_s, zb_s, 1)

    for row in range(0, seq, tile):
        rows = pl.ds(row, tile)
        x = tok_ref[rows, :].astype(f32)
        r1 = lax.rsqrt(jnp.mean(x * x, axis=1, keepdims=True) + norm_eps)
        h1_s[rows, :] = (x * r1 * gains_ref[4:5, :]).astype(bf16)
    shape = stack_s.shape[2:]
    stack_s[0, 0] = mm_tn(h1_s[...], dqkv_ref[0]).astype(bf16).reshape(shape)
    stack_s[0, 1] = mm_tn(h1_s[...], dqkv_ref[1]).astype(bf16).reshape(shape)
    stack_s[1, 0] = mm_tn(h1_s[...], dqkv_ref[2]).astype(bf16).reshape(shape)
    stack_s[1, 1] = mm_tn(o_ref[...], midb_ref[...]).astype(bf16).reshape(shape)
    swap = send(stack_s.at[1 - core], pair_s, pair_send.at[0], pair_recv.at[0], partner)
    swap.start()

    gain = jnp.zeros((1, width), f32)
    for row in range(0, seq, tile):
        rows = pl.ds(row, tile)
        x = tok_ref[rows, :].astype(f32)
        r1 = lax.rsqrt(jnp.mean(x * x, axis=1, keepdims=True) + norm_eps)
        n1 = x * r1
        grad = mm_nt(dqkv_ref[0, rows, :], w_ref[0])
        grad = grad + mm_nt(dqkv_ref[1, rows, :], w_ref[1])
        grad = grad + mm_nt(dqkv_ref[2, rows, :], w_ref[2])
        gain = gain + jnp.sum(grad * n1, axis=0, keepdims=True)
        d1 = grad * gains_ref[4:5, :]
        igrad_ref[rows, :] = midg_ref[rows, :] + r1 * (d1 - n1 * jnp.mean(d1 * n1, axis=1, keepdims=True))
    spot = lax.broadcasted_iota(jnp.int32, (8, width), 0)
    small = jnp.where(spot < 4, rgrad_ref[...], jnp.where(spot == 4, gain, gain2_ref[0:1, :]))
    small = jnp.concatenate([small, jnp.zeros((120, width), f32)], axis=0)
    tiny_s[...] = small.T.reshape(tiny_s.shape)
    tswap = send(tiny_s, tpair_s, pair_send.at[1], pair_recv.at[1], partner)
    tswap.start()

    swap.wait()
    for i in range(2):
        for e in range(exps):
            stack_s[core, i, e] = (stack_s[core, i, e].astype(f32) + pair_s[i, e].astype(f32)).astype(bf16)
    plane = [
        begin(
            send(
                stack_s.at[core, :, columns[k]], plane_s.at[k],
                plane_send.at[0, k], plane_recv.at[0, k], {"exp": columns[k]},
            )
        )
        for k in range(1, exps)
    ]
    tswap.wait()
    tpair_s[...] += tiny_s[...]
    plane += [
        begin(
            send(
                tpair_s.at[columns[k]], tplane_s.at[k],
                plane_send.at[1, k], plane_recv.at[1, k], {"exp": columns[k]},
            )
        )
        for k in range(1, exps)
    ]

    def finals(kind, part_s, out_ref, at):
        return [
            pltpu.make_async_copy(part_s, out_ref.at[at], own_sem.at[kind]),
            send(part_s, out_ref.at[at], last_send.at[kind], last_recv.at[kind], partner),
        ]

    for copy in line_a + line_b:
        copy.wait_recv()
    mine = layers[0]
    fa_s[...] = sum([za_s[k].astype(f32) for k in range(1, shds)], qa_s[mine].astype(f32))
    fb_s[...] = sum([zb_s[k].astype(f32) for k in range(1, shds)], qb_s[mine].astype(f32))
    last = finals(0, fa_s, sa_ref, core) + finals(1, fb_s, sb_ref, core)
    for copy in last:
        copy.start()

    for copy in plane:
        copy.wait_recv()
    own = columns[0]
    for i in range(2):
        for z in range(shds):
            value = stack_s[core, i, own, z].astype(f32)
            for k in range(1, exps):
                value = value + plane_s[k, i, z].astype(f32)
            r_s[z, i] = value.astype(bf16)
    line_r = line(r_s, zr_s, 2)
    tr_s[...] = sum([tplane_s[k] for k in range(1, exps)], tpair_s[own])
    line_r += line(tr_s, tz_s, 3)
    for copy in line_r:
        copy.wait_recv()
    fw_s[...] = sum([zr_s[k].astype(f32) for k in range(1, shds)], r_s[mine].astype(f32))
    ends = finals(2, fw_s, sw_ref, core)
    for copy in ends:
        copy.start()
    st_ref[...] = sum([tz_s[k] for k in range(1, shds)], tr_s[mine])
    for copy in waits:
        copy.wait_send()
    for copy in last + ends:
        copy.wait()


def finish(dqkv, tokens, midg, o, midb, full, gains, gain2, rgrad, la, lb):
    exps, shds = la.shape[:2]
    seq, width = tokens.shape
    rows = la.shape[2]
    vmem = pl.BlockSpec(memory_space=pltpu.VMEM)
    big = lambda *shape: pltpu.VMEM(shape, bf16)
    wide = lambda *shape: pltpu.VMEM(shape, f32)
    sems = lambda *n: pltpu.SemaphoreType.DMA(n)
    a, b = la.shape[2:], lb.shape[2:]
    tiny = (exps, shds, rows, 128)
    weights = pl.BlockSpec((3, width, width), lambda i: (0, 0, 0), pipeline_mode=pl.Buffered(1))
    given = [dqkv, tokens, midg, o, midb, full, gains, gain2, rgrad, la, lb]
    return pl.pallas_call(
        functools.partial(finish_kernel, exps, shds),
        grid=(1,),
        in_specs=[weights if v is full else once(v.shape) for v in given],
        out_specs=[once((seq, width)), ANY, ANY, ANY, once((rows, 128))],
        out_shape=[
            jax.ShapeDtypeStruct((seq, width), f32),
            jax.ShapeDtypeStruct((2, 2, rows, width), f32),
            jax.ShapeDtypeStruct((2,) + a, f32),
            jax.ShapeDtypeStruct((2,) + b, f32),
            jax.ShapeDtypeStruct((rows, 128), f32),
        ],
        scratch_shapes=[
            big(seq, width),
            big(2, 2, exps, shds, rows, width),
            big(2, exps, shds, rows, width),
            wide(*tiny),
            wide(*tiny),
            big(exps, 2, shds, rows, width),
            wide(exps, shds, rows, 128),
            big(shds, *a),
            big(shds, *b),
            big(shds, *a),
            big(shds, *b),
            big(shds, 2, rows, width),
            big(shds, 2, rows, width),
            wide(shds, rows, 128),
            wide(shds, rows, 128),
            wide(2, rows, width),
            wide(*a),
            wide(*b),
            sems(2), sems(2), sems(2, exps), sems(2, exps), sems(4, shds), sems(4, shds),
            sems(3), sems(3), sems(3),
        ],
        compiler_params=params(("arbitrary",), collective_id=7, has_side_effects=True),
        cost_estimate=pl.CostEstimate(
            flops=60_000_000_000, bytes_accessed=30_000_000, transcendentals=0
        ),
        name="finish",
    )(*given)


def adam_update(weight, moment, square, gradient, step_rate, shrink_rate):
    moment_next = beta_one * moment + (1.0 - beta_one) * gradient
    square_next = beta_two * square + (1.0 - beta_two) * gradient * gradient
    direction = moment_next / first_fix / (jnp.sqrt(square_next / second_fix) + adam_eps)
    return (weight - step_rate * (direction + shrink_rate * weight), moment_next, square_next)


def pick(array, axis, index):
    return lax.dynamic_index_in_dim(array, index, axis, keepdims=False)


def share(part, groups, core):
    swap = [(i, i ^ 1) for i in range(groups)]
    both = jnp.zeros((2,) + part.shape, part.dtype)
    both = lax.dynamic_update_index_in_dim(both, part, core, 0)
    if groups > 2:
        return lax.psum(both, "grp")
    return lax.dynamic_update_index_in_dim(both, lax.ppermute(part, "grp", swap), 1 - core, 0)


def on_device(
    tokens_in, cotangent, block_ids, expert_ids,
    scales, moment_scales, square_scales, attend, moment_attend, square_attend,
    output, moment_output, square_output, router, moment_router, square_router,
    widener, moment_widener, square_widener, reducer, moment_reducer, square_reducer,
    experts, moment_experts, square_experts, narrower, moment_narrower, square_narrower,
):
    groups, exps, shds = (lax.axis_size(a) for a in ("grp", "exp", "shd"))
    spread = exps * shds
    core = lax.rem(lax.axis_index("grp"), 2)
    _, seq, width = tokens_in.shape
    hidden = reducer.shape[0] * spread
    experts_all = exps * experts.shape[0]
    rows, tall = output.shape[0], reducer.shape[0] // 2
    deep = width // shds
    tokens, g = tokens_in.reshape(seq, width), cotangent.reshape(seq, width)

    def packed(wide, narrow):
        wide = pick(wide.astype(bf16), 0, core)
        narrow = pick(narrow.astype(bf16).reshape(2, -1, width), 0, core)
        blocks = [
            a.reshape(a.shape[0], -1, 256).transpose(1, 0, 2).reshape(-1, 256) for a in (wide, narrow)
        ]
        return jnp.concatenate(blocks, axis=0)

    def gather(part, axes):
        wide = lax.all_gather(part, ("grp",) + axes, axis=0, tiled=False)
        return wide.reshape((groups, -1) + part.shape)[:2]

    mine = jnp.where(
        core == 0,
        attend[:2].astype(bf16),
        jnp.stack([attend[2].astype(bf16), output.astype(bf16)]),
    )
    tiny = jnp.concatenate([router, scales.T], axis=1).astype(bf16)
    tiny = jnp.pad(tiny, ((0, 0), (0, 128 - tiny.shape[1])))
    expert_weights = gather(packed(experts[0], narrower[0]), ("shd",))
    shared_weights = gather(packed(widener, reducer), ("exp", "shd"))

    ids = expert_ids.reshape(seq, 2)
    every = jnp.arange(128, dtype=jnp.int32)[None, :]
    hot = (ids[:, 0:1] == every) | (ids[:, 1:2] == every)
    order = jnp.arange(seq, dtype=jnp.int32)
    before = (order[:, None] > order[None, :]).astype(bf16)
    placed = mm(before, hot.astype(bf16)).astype(jnp.int32)
    place_col = jnp.where(hot, placed, -1)
    place_row = place_col[:, :16].T
    bid = block_ids.reshape(1, seq)
    bid_row = jnp.broadcast_to(bid, (8, seq))
    bid_col = jnp.broadcast_to(bid.reshape(seq, 1), (seq, 256))

    lanes = -(-CAP // 128) * 128
    full, wr, g_slots = gather_first(mine, tiny, g, place_row, exps, shds, experts_all, CAP)
    qkv, lse, o, mid, h2, probs, probst, gains, g_landed = attention_forward(
        tokens, bid_row, bid_col, full, wr, g_slots
    )
    slot_rows, chosen = dispatch(h2, place_row, probst, experts_all, CAP, lanes)
    eout, ein, own, swapped = routed(slot_rows, chosen, g_landed, expert_weights, hidden)
    add = lambda a, b: (a.astype(f32) + b.astype(f32)).astype(bf16)
    part = add(own, swapped)
    part, h2_later = lax.optimization_barrier((part, h2))
    part = lax.psum_scatter(part, "shd", scatter_dimension=0, tiled=False)
    sout, sin, own_a, swapped_a, own_b, swapped_b = ffn(
        h2_later, g, shared_weights, hidden, f32, 256, "shared"
    )
    part_a = add(own_a, swapped_a).reshape(exps, shds, rows, hidden)
    part_b = add(own_b, swapped_b).reshape(exps, shds, tall, width)
    block_out, mid_grad, midb, og, gain_two, rgrad, landed_b = combine(
        mid, sout, sin, g, h2, probs, place_col, eout, ein, gains, wr, full, part_b
    )
    dqkv, landed_a = attention_backward(qkv, og, lse, bid_row, bid_col, part_a)
    input_grad, sum_w, sum_a, sum_b, sum_t = finish(
        dqkv, tokens, mid_grad, o, midb, full, gains, gain_two, rgrad, landed_a, landed_b
    )
    if groups > 2:
        sum_w, sum_a, sum_b, sum_t = (
            0.5 * lax.psum(v, "grp") for v in (sum_w, sum_a, sum_b, sum_t)
        )
    expert_sums = share(part, groups, core).astype(f32)
    cut_at = hidden // 256 * deep
    g_experts = expert_sums[:, :cut_at].reshape(2, hidden // 256, deep, 256)
    g_experts = g_experts.transpose(0, 2, 1, 3).reshape(2, deep, hidden)
    g_narrower = expert_sums[:, cut_at:].reshape(2, width // 256, -1, 256)
    g_narrower = g_narrower.transpose(0, 2, 1, 3)
    sum_w = sum_w.reshape(4, rows, width)
    grads = (
        sum_t[:, 4:6].T,
        sum_w[:3],
        sum_w[3],
        sum_t[:, :experts_all],
        sum_a,
        sum_b.reshape(reducer.shape),
        g_experts.reshape(experts.shape),
        g_narrower.reshape(narrower.shape),
    )
    masters = (scales, attend, output, router, widener, reducer, experts, narrower)
    moments = (
        moment_scales, moment_attend, moment_output, moment_router,
        moment_widener, moment_reducer, moment_experts, moment_narrower,
    )
    squares = (
        square_scales, square_attend, square_output, square_router,
        square_widener, square_reducer, square_experts, square_narrower,
    )
    results = [block_out.reshape(tokens_in.shape), input_grad.reshape(tokens_in.shape)]
    for kind in range(8):
        results.extend(
            adam_update(
                masters[kind], moments[kind], squares[kind], grads[kind],
                learning_rates[kind], decay_rates[kind],
            )
        )
    return tuple(results)


def solution(mesh):
    tokens = P(("grp", "exp", "shd"), None, None)
    both = ("exp", "shd")
    kinds = (
        P(None, both), P(None, both, None), P(both, None), P(both, None),
        P(None, both, None), P(both, None), P("exp", None, "shd", None), P("exp", "shd", None),
    )
    thrice = tuple(kind for kind in kinds for _ in range(3))
    return jax.shard_map(
        on_device,
        mesh=mesh,
        in_specs=(tokens, tokens, P(("grp", "exp", "shd"), None), tokens) + thrice,
        out_specs=(tokens, tokens) + thrice,
        check_vma=False,
    )
```

```python
import functools

import jax
import jax.numpy as jnp
from jax import lax
from jax.experimental import pallas as pl
from jax.experimental.pallas import tpu as pltpu
from jax.sharding import PartitionSpec as P

HEADS = 12
CAP = 576
VMEM_LIMIT = 60 * 1024 * 1024

norm_eps = 1e-06
adam_eps = 1e-08
beta_one = 0.9
beta_two = 0.95
first_fix = 1.0 - 0.9**10
second_fix = 1.0 - 0.95**10
learning_rates = (0.3, 0.02, 0.15, 0.02, 0.02, 0.012, 0.02, 0.012)
decay_rates = (0.0, 0.1, 0.1, 0.1, 0.1, 0.1, 0.1, 0.1)
masked_score = -1e30
bf16 = jnp.bfloat16
f32 = jnp.float32


def mm(a, b):
    return jnp.dot(a, b, preferred_element_type=f32)


def mm_nt(a, b):
    return lax.dot_general(a, b, (((1,), (1,)), ((), ())), preferred_element_type=f32)


def mm_tn(a, b):
    return lax.dot_general(a, b, (((0,), (0,)), ((), ())), preferred_element_type=f32)


def params(semantics=None, **more):
    return pltpu.CompilerParams(
        dimension_semantics=semantics, vmem_limit_bytes=VMEM_LIMIT, **more
    )


def whole_spec(shape, **more):
    zeros = (0,) * len(shape)
    return pl.BlockSpec(shape, lambda *_: zeros, **more)


def once(shape):
    return whole_spec(shape, pipeline_mode=pl.Buffered(1))


MESH = pl.DeviceIdType.MESH
ANY = pl.BlockSpec(memory_space=pl.ANY)


def greet(targets):
    barrier = pltpu.get_barrier_semaphore()
    for target in targets:
        pl.semaphore_signal(barrier, inc=1, device_id=target, device_id_type=MESH)
    pl.semaphore_wait(barrier, len(targets))


def send(src, dst, send_sem, recv_sem, target):
    return pltpu.make_async_remote_copy(
        src_ref=src, dst_ref=dst, send_sem=send_sem, recv_sem=recv_sem,
        device_id=target, device_id_type=MESH,
    )


def others(axis, count):
    me = lax.axis_index(axis)
    return [lax.bitwise_xor(me, k) for k in range(count)]


def gather_kernel(
    exps, shds,
    mine_ref, tiny_ref, g_ref, place_ref, full_ref, every_ref, slots_ref,
    own_sem, z_send, z_recv, p_send, p_recv, c_send, c_recv,
):
    columns, layers = others("exp", exps), others("shd", shds)
    group = lax.axis_index("grp")
    core = lax.rem(group, 2)
    partner = {"grp": lax.bitwise_xor(group, 1)}
    rows = mine_ref.shape[1]

    def spots(kz, kx):
        at = pl.ds(pl.multiple_of((columns[kx] * shds + layers[kz]) * rows, 16), rows)
        return full_ref.at[pl.ds(2 * core, 2), at, :], every_ref.at[at, :]

    greet(
        [{"shd": layer} for layer in layers[1:]]
        + [{"exp": column} for column in columns[1:]]
        + [partner]
    )
    started = []

    def begin(copies):
        for copy in copies:
            copy.start()
        started.extend(copies)
        return copies

    def both(sources, kz, kx, sem, far, index, target):
        return [
            send(a, b, sem.at[index + (i,)], far.at[index + (i,)], target)
            for i, (a, b) in enumerate(zip(sources, spots(kz, kx)))
        ]

    mine = (mine_ref, tiny_ref)
    local = [
        pltpu.make_async_copy(a, b, own_sem.at[i])
        for i, (a, b) in enumerate(zip(mine, spots(0, 0)))
    ]
    for copy in local:
        copy.start()
    down = [both(mine, 0, 0, z_send, z_recv, (k,), {"shd": layers[k]}) for k in range(1, shds)]
    for copies in down:
        begin(copies)
    across = {}
    for kx in range(1, exps):
        across[0, kx] = begin(both(mine, 0, 0, p_send, p_recv, (0, kx), {"exp": columns[kx]}))
    swaps = [send(mine_ref, spots(0, 0)[0], c_send.at[0, 0], c_recv.at[0, 0], partner)]
    swaps[0].start()
    for e in range(slots_ref.shape[0]):
        hot = slots_of(place_ref[e : e + 1, :], slots_ref.shape[1])
        slots_ref[e] = mm(hot, g_ref[...]).astype(bf16)

    def swap(kz, kx):
        here = spots(kz, kx)[0]
        copy = send(here, here, c_send.at[kz, kx], c_recv.at[kz, kx], partner)
        copy.start()
        swaps.append(copy)

    for kz in range(1, shds):
        for copy in down[kz - 1]:
            copy.wait_recv()
        for kx in range(1, exps):
            across[kz, kx] = begin(both(spots(kz, 0), kz, 0, p_send, p_recv, (kz, kx), {"exp": columns[kx]}))
        swap(kz, 0)
    for kz in range(shds):
        for kx in range(1, exps):
            for copy in across[kz, kx]:
                copy.wait_recv()
            swap(kz, kx)
    for copy in started:
        copy.wait_send()
    for copy in swaps + local:
        copy.wait()


def gather_first(mine, tiny, g, place_row, exps, shds, experts_all, cap):
    _, rows, width = mine.shape
    tall = exps * shds * rows
    sems = lambda *shape: pltpu.SemaphoreType.DMA(shape)
    return pl.pallas_call(
        functools.partial(gather_kernel, exps, shds),
        in_specs=[ANY, ANY, pl.BlockSpec(memory_space=pltpu.VMEM), pl.BlockSpec(memory_space=pltpu.VMEM)],
        out_specs=[ANY, ANY, pl.BlockSpec(memory_space=pltpu.VMEM)],
        out_shape=[
            jax.ShapeDtypeStruct((4, tall, width), bf16),
            jax.ShapeDtypeStruct((tall, 128), bf16),
            jax.ShapeDtypeStruct((experts_all, cap, width), bf16),
        ],
        scratch_shapes=[
            sems(2), sems(shds, 2), sems(shds, 2), sems(shds, exps, 2), sems(shds, exps, 2),
            sems(shds, exps), sems(shds, exps),
        ],
        compiler_params=params(collective_id=4, has_side_effects=True),
        cost_estimate=pl.CostEstimate(
            flops=40_000_000_000, bytes_accessed=10_000_000, transcendentals=0
        ),
        name="gather_first",
    )(mine, tiny, g, place_row)


def forward_kernel(
    exps,
    tok_ref, bidr_ref, bidc_ref, wa_ref, wo_ref, wr_ref, slots_ref,
    qkv_ref, lse_ref, o_ref, mid_ref, h2_ref, probs_ref, probst_ref, gains_ref, landed_ref, h1_ref,
    send_sem, recv_sem,
):
    pair = pl.program_id(0)
    me = lax.axis_index("exp")

    def copies():
        made = [pltpu.make_async_copy(slots_ref.at[me], landed_ref.at[0], send_sem.at[0])]
        for k in range(1, exps):
            peer = lax.bitwise_xor(me, k)
            made.append(
                send(slots_ref.at[peer], landed_ref.at[k], send_sem.at[k], recv_sem.at[k], {"exp": peer})
            )
        return made

    @pl.when(pair == 0)
    def _():
        greet([{"exp": lax.bitwise_xor(me, k)} for k in range(1, exps)])
        for copy in copies():
            copy.start()
    seq, width = tok_ref.shape
    tile = 256

    @pl.when(pair == 0)
    def _():
        gains_ref[...] = wr_ref[...].astype(f32).T[:8]
        for row in range(0, seq, tile):
            x = tok_ref[pl.ds(row, tile), :].astype(f32)
            r1 = lax.rsqrt(jnp.mean(x * x, axis=1, keepdims=True) + norm_eps)
            h1_ref[pl.ds(row, tile), :] = (x * r1 * gains_ref[4:5, :]).astype(bf16)

    h1 = h1_ref[...]
    for i in range(3):
        qkv_ref[i] = mm(h1, wa_ref[i]).astype(bf16)
    qs = qkv_ref[0] * jnp.asarray(0.125, bf16)
    k = qkv_ref[1]
    vt = qkv_ref[2].T
    lane = lax.broadcasted_iota(jnp.int32, (tile, 128), 1)
    for q0 in range(0, seq, tile):
        kl = min(seq, q0 + 2 * tile)
        qt = qs[q0 : q0 + tile]
        allowed = bidc_ref[q0:kl, :] <= bidr_ref[0:1, q0 : q0 + tile]
        parts = []
        for head in range(2):
            qm = jnp.where((lane // 64) == head, qt, jnp.zeros_like(qt))
            tail = jnp.where(allowed, mm_nt(k[q0:kl], qm), masked_score)
            top = jnp.max(tail, axis=0, keepdims=True)
            if q0:
                lead = mm_nt(k[:q0], qm)
                top = jnp.maximum(top, jnp.max(lead, axis=0, keepdims=True))
                lead = jnp.exp(lead - top)
            tail = jnp.exp(tail - top)
            total = jnp.sum(tail, axis=0, keepdims=True)
            if q0:
                total = total + jnp.sum(lead, axis=0, keepdims=True)
            inverse = 1.0 / total
            vh = vt[64 * head : 64 * head + 64]
            ot = mm(vh[:, q0:kl], (tail * inverse).astype(bf16))
            if q0:
                ot = ot + mm(vh[:, :q0], (lead * inverse).astype(bf16))
            lse_ref[0, head : head + 1, q0 : q0 + tile] = top + jnp.log(total)
            parts.append(ot)
        out = jnp.concatenate(parts, axis=0).T.astype(bf16)
        o_ref[q0 : q0 + tile, pl.ds(pl.multiple_of(pair * 128, 128), 128)] = out

    @pl.when(pair == pl.num_programs(0) - 1)
    def _():
        for row in range(0, seq, tile):
            rows = pl.ds(row, tile)
            mid = tok_ref[rows, :].astype(f32) + mm(o_ref[rows, :], wo_ref[0])
            mid_ref[rows, :] = mid
            r2 = lax.rsqrt(jnp.mean(mid * mid, axis=1, keepdims=True) + norm_eps)
            h2 = (mid * r2 * gains_ref[5:6, :]).astype(bf16)
            h2_ref[rows, :] = h2
            logits = mm(h2, wr_ref[...])
            spot = lax.broadcasted_iota(jnp.int32, logits.shape, 1)
            logits = jnp.where(spot < 4, logits, masked_score)
            e = jnp.exp(logits - jnp.max(logits, axis=1, keepdims=True))
            probs_ref[rows, :] = e / jnp.sum(e, axis=1, keepdims=True)
        routers = gains_ref[...].astype(bf16)
        logits = mm_nt(jnp.concatenate([routers, routers], axis=0), h2_ref[...])
        spot = lax.broadcasted_iota(jnp.int32, logits.shape, 0)
        logits = jnp.where(spot < 4, logits, masked_score)
        e = jnp.exp(logits - jnp.max(logits, axis=0, keepdims=True))
        probst_ref[...] = e / jnp.sum(e, axis=0, keepdims=True)
        for copy in copies():
            copy.wait()


def attention_forward(tokens, bid_row, bid_col, full, wr, slots):
    exps = slots.shape[0]
    seq, width = tokens.shape
    pairs = width // 128
    return pl.pallas_call(
        functools.partial(forward_kernel, exps),
        grid=(pairs,),
        in_specs=[
            once((seq, width)),
            once(bid_row.shape),
            once(bid_col.shape),
            pl.BlockSpec((3, width, 128), lambda i: (0, 0, i)),
            pl.BlockSpec((1, width, width), lambda i: (3, 0, 0), pipeline_mode=pl.Buffered(1)),
            once(wr.shape),
            ANY,
        ],
        out_specs=[
            pl.BlockSpec((3, seq, 128), lambda i: (0, 0, i)),
            pl.BlockSpec((1, 8, seq), lambda i: (i, 0, 0)),
            whole_spec((seq, width)),
            whole_spec((seq, width)),
            whole_spec((seq, width)),
            whole_spec((seq, 128)),
            whole_spec((16, seq)),
            whole_spec((8, width)),
            ANY,
        ],
        out_shape=[
            jax.ShapeDtypeStruct((3, seq, width), bf16),
            jax.ShapeDtypeStruct((pairs, 8, seq), f32),
            jax.ShapeDtypeStruct((seq, width), bf16),
            jax.ShapeDtypeStruct((seq, width), f32),
            jax.ShapeDtypeStruct((seq, width), bf16),
            jax.ShapeDtypeStruct((seq, 128), f32),
            jax.ShapeDtypeStruct((16, seq), f32),
            jax.ShapeDtypeStruct((8, width), f32),
            jax.ShapeDtypeStruct(slots.shape, bf16),
        ],
        scratch_shapes=[
            pltpu.VMEM((seq, width), bf16),
            pltpu.SemaphoreType.DMA((exps,)),
            pltpu.SemaphoreType.DMA((exps,)),
        ],
        compiler_params=params(("arbitrary",), collective_id=1, has_side_effects=True),
        cost_estimate=pl.CostEstimate(
            flops=30_000_000_000, bytes_accessed=20_000_000, transcendentals=12_000_000
        ),
        name="attention_forward",
    )(tokens, bid_row, bid_col, full, full, wr, slots)


def slots_of(place_row, cap):
    slot = lax.broadcasted_iota(jnp.int32, (cap, place_row.shape[1]), 0)
    return (slot == place_row).astype(f32).astype(bf16)


def dispatch_kernel(h2_ref, place_ref, probst_ref, rows_ref, chosen_ref):
    expert = pl.program_id(0)
    cap = rows_ref.shape[1]
    lanes = chosen_ref.shape[2]
    row = place_ref[pl.ds(expert, 1), :]
    rows_ref[0] = mm(slots_of(row, cap), h2_ref[...]).astype(bf16)
    value = probst_ref[pl.ds(expert, 1), :]
    high = value.astype(bf16)
    rest = value - high.astype(f32)
    middle = rest.astype(bf16)
    low = (rest - middle.astype(f32)).astype(bf16)
    spot = lax.broadcasted_iota(jnp.int32, (16, row.shape[1]), 0)
    pieces = jnp.where(
        spot == 0, high.astype(f32), jnp.where(spot == 1, middle.astype(f32), jnp.where(spot == 2, low.astype(f32), 0.0))
    )
    chosen = jnp.sum(mm_nt(pieces.astype(bf16), slots_of(row, lanes)), axis=0, keepdims=True)
    chosen_ref[0] = jnp.broadcast_to(chosen, chosen_ref.shape[1:])


def dispatch(h2, place_row, probst, experts_all, cap, lanes):
    seq, width = h2.shape
    return pl.pallas_call(
        dispatch_kernel,
        grid=(experts_all,),
        in_specs=[once(h2.shape), once(place_row.shape), once(probst.shape)],
        out_specs=[
            pl.BlockSpec((1, cap, width), lambda e: (e, 0, 0)),
            pl.BlockSpec((1, 8, lanes), lambda e: (e, 0, 0)),
        ],
        out_shape=[
            jax.ShapeDtypeStruct((experts_all, cap, width), bf16),
            jax.ShapeDtypeStruct((experts_all, 8, lanes), f32),
        ],
        compiler_params=params(("arbitrary",)),
        cost_estimate=pl.CostEstimate(
            flops=5_000_000_000, bytes_accessed=6_000_000, transcendentals=0
        ),
        name="dispatch",
    )(h2, place_row, probst)


def gated(x, g, wg, wu, wn):
    gate, up = mm(x, wg), mm(x, wu)
    hgrad = mm_nt(g, wn)
    sig = lax.logistic(gate)
    active = gate * sig
    slope = sig * (1.0 + gate * (1.0 - sig))
    hidden = (active * up).astype(bf16)
    return hidden, (hgrad * up * slope).astype(bf16), (hgrad * active).astype(bf16)


def routed_kernel(
    exps, shds,
    rows_ref, chosen_ref, grads_ref, packed_ref,
    eout_ref, gin_ref, sum_ref,
    x_s, g_s, c_s, w_s, n_s, hid_s, gg_s, ug_s, out_s, gin_s, wide_l, narrow_l,
    load_sem, x_send, x_recv, c_send, c_recv, o_send, o_recv, i_send, w_sem, s_send, s_recv,
):
    me = lax.axis_index("exp")
    _, cap, width = x_s.shape
    hidden = hid_s.shape[1]
    rows_all = exps * cap
    peers = [lax.bitwise_xor(me, k) for k in range(exps)]
    group = lax.axis_index("grp")
    core = lax.rem(group, 2)
    partner = {"grp": lax.bitwise_xor(group, 1)}
    greet([{"exp": peer} for peer in peers[1:]] + [partner])
    deep, tall = w_s.shape[2], n_s.shape[2]
    base = hidden // 256 * deep
    wide_at = lambda b: pl.ds(pl.multiple_of(b * deep, 16), deep)
    narrow_at = lambda b: pl.ds(base + b * tall, tall)
    lanes_at = lambda b: pl.ds(pl.multiple_of(256 * b, 256), 256)

    chosen, arriving = [], []
    for k in range(1, exps):
        target = {"exp": peers[k]}
        chosen.append(send(chosen_ref.at[peers[k]], c_s.at[k], c_send.at[k], c_recv.at[k], target))
        arriving.append(send(rows_ref.at[peers[k]], x_s.at[k], x_send.at[k], x_recv.at[k], target))
    for copy in chosen + arriving[:2]:
        copy.start()
    loads = [
        pltpu.make_async_copy(rows_ref.at[me], x_s.at[0], load_sem.at[0]),
        pltpu.make_async_copy(chosen_ref.at[me], c_s.at[0], load_sem.at[1]),
        pltpu.make_async_copy(grads_ref, g_s, load_sem.at[2]),
    ]
    for c in range(2):
        for b in range(hidden // 256):
            loads.append(
                pltpu.make_async_copy(
                    packed_ref.at[c, :, wide_at(b), :], w_s.at[c, :, :, lanes_at(b)], load_sem.at[len(loads)]
                )
            )
        for b in range(width // 256):
            loads.append(
                pltpu.make_async_copy(
                    packed_ref.at[c, :, narrow_at(b), :], n_s.at[:, c, :, lanes_at(b)], load_sem.at[len(loads)]
                )
            )
    for copy in loads:
        copy.start()
    for copy in loads:
        copy.wait()

    ft = 512
    returns, kept = [], []
    for k in range(exps):
        if k:
            chosen[k - 1].wait()
            arriving[k - 1].wait()
        scale = c_s[k].T[:cap, 0:1]
        g_s[k] = (g_s[k].astype(f32) * scale).astype(bf16)

        @pl.loop(0, hidden // ft)
        def _(f):
            columns = pl.ds(pl.multiple_of(f * ft, ft), ft)
            wg = w_s[0, :, :, columns].reshape(width, ft)
            wu = w_s[1, :, :, columns].reshape(width, ft)
            hid, gg, ug = gated(x_s[k], g_s[k], wg, wu, n_s[f].reshape(ft, width))
            hid_s[pl.ds(k * cap, cap), columns] = hid
            gg_s[pl.ds(k * cap, cap), columns] = gg
            ug_s[pl.ds(k * cap, cap), columns] = ug

        mine = pl.ds(k * cap, cap)
        if k >= 2:
            kept[k - 2].wait()
        for b in range(width // 256):
            part = slice(256 * b, 256 * b + 256)
            out_s[k, :, part] = mm(hid_s[mine, :], n_s[:, :, :, part].reshape(hidden, 256)).astype(bf16)
            wg = w_s[0].reshape(width, hidden)[part]
            wu = w_s[1].reshape(width, hidden)[part]
            gin_s[k % 2, :, part] = (mm_nt(gg_s[mine, :], wg) + mm_nt(ug_s[mine, :], wu)).astype(bf16)

        if k:
            back = send(
                out_s.at[k], eout_ref.at[me], o_send.at[k], o_recv.at[k], {"exp": peers[k]}
            )
        else:
            back = pltpu.make_async_copy(out_s.at[0], eout_ref.at[me], o_send.at[0])
            for copy in arriving[2:]:
                copy.start()
        kept.append(pltpu.make_async_copy(gin_s.at[k % 2], gin_ref.at[peers[k]], i_send.at[k]))
        for copy in (back, kept[k]):
            copy.start()
        returns.append(back)

    wide = hidden // shds
    per = wide // 256

    across = lambda f: pl.ds(pl.multiple_of(f * wide, wide), wide)

    def swaps(f):
        return [
            send(w_s.at[1 - core, :, :, across(f)], wide_l.at[f], s_send.at[f, 0], s_recv.at[f, 0], partner),
            send(n_s.at[f, 1 - core], narrow_l.at[f], s_send.at[f, 1], s_recv.at[f, 1], partner),
        ]

    def stores(f):
        made = []
        for b in range(per):
            block = per * f + b
            made.append((w_s.at[core, :, :, lanes_at(block)], sum_ref.at[:, wide_at(block), :]))
        for b in range(width // 256):
            made.append((n_s.at[f, core, :, lanes_at(b)], sum_ref.at[f, narrow_at(b), :]))
        return [pltpu.make_async_copy(a, b, w_sem.at[f, i]) for i, (a, b) in enumerate(made)]

    def add(f):
        for copy in swaps(f):
            copy.wait_recv()
        for z in range(shds):
            own = w_s[core, z, :, across(f)].astype(f32)
            w_s[core, z, :, across(f)] = (own + wide_l[f, z].astype(f32)).astype(bf16)
        n_s[f, core] = (n_s[f, core].astype(f32) + narrow_l[f].astype(f32)).astype(bf16)
        for copy in stores(f):
            copy.start()

    @pl.loop(0, shds)
    def _(f):
        columns = pl.ds(pl.multiple_of(f * wide, wide), wide)
        x = x_s[...].reshape(rows_all, width)
        g = g_s[...].reshape(rows_all, width)
        part = w_s.shape[1:3] + (wide,)
        w_s[0, :, :, columns] = mm_tn(x, gg_s[:, columns]).astype(bf16).reshape(part)
        w_s[1, :, :, columns] = mm_tn(x, ug_s[:, columns]).astype(bf16).reshape(part)
        n_s[f] = mm_tn(hid_s[:, columns], g).astype(bf16).reshape(n_s.shape[1:])
        for copy in swaps(f):
            copy.start()

        @pl.when(f > 0)
        def _():
            add(f - 1)

    add(shds - 1)
    for copy in returns + kept[-2:]:
        copy.wait()

    @pl.loop(0, shds)
    def _(f):
        for copy in swaps(f):
            copy.wait_send()
        for copy in stores(f):
            copy.wait()


def routed(slot_rows, chosen, grads, packed, hidden):
    exps, cap, width = slot_rows.shape
    shds, height = packed.shape[1:3]
    deep, tall = width // shds, hidden // shds // 2
    pieces = hidden // shds // 256 + width // 256
    big = lambda *shape: pltpu.VMEM(shape, bf16)
    sems = lambda *n: pltpu.SemaphoreType.DMA(n)
    return pl.pallas_call(
        functools.partial(routed_kernel, exps, shds),
        in_specs=[ANY] * 4,
        out_specs=[ANY] * 3,
        out_shape=[
            jax.ShapeDtypeStruct((exps, cap, width), bf16),
            jax.ShapeDtypeStruct((exps, cap, width), bf16),
            jax.ShapeDtypeStruct((shds, height, 256), bf16),
        ],
        scratch_shapes=[
            big(exps, cap, width),
            big(exps, cap, width),
            pltpu.VMEM(chosen.shape, f32),
            big(2, shds, deep, hidden),
            big(shds, 2, tall, width),
            big(exps * cap, hidden),
            big(exps * cap, hidden),
            big(exps * cap, hidden),
            big(exps, cap, width),
            big(2, cap, width),
            big(shds, shds, deep, hidden // shds),
            big(shds, tall, width),
            sems(3 + 2 * (hidden // 256 + width // 256)),
            sems(exps), sems(exps), sems(exps), sems(exps), sems(exps), sems(exps), sems(exps),
            sems(shds, pieces), sems(shds, 2), sems(shds, 2),
        ],
        compiler_params=params(collective_id=2, has_side_effects=True),
        cost_estimate=pl.CostEstimate(
            flops=18 * exps * cap * width * hidden,
            bytes_accessed=40_000_000,
            transcendentals=exps * cap * hidden,
        ),
        name="routed",
    )(slot_rows, chosen, grads, packed)


def ffn_kernel(
    x_ref, g_ref, wg_ref, wu_ref, wn_ref, back_ref,
    out_ref, gin_ref, part_a, part_b, ein_ref,
    acc_out, acc_gin, hid_s, gg_s, ug_s, wide_s, narrow_s, wide_l, narrow_l,
    own_sem, send_sem, recv_sem, b_send, b_recv,
    *, tile,
):
    f = pl.program_id(0)
    last = pl.num_programs(0) - 1
    rows_all, width = x_ref.shape
    group = lax.axis_index("grp")
    core = lax.rem(group, 2)
    partner = {"grp": lax.bitwise_xor(group, 1)}
    ft = wide_s.shape[3]
    shards, tall = narrow_s.shape[2:4]

    def swaps(step):
        return [
            send(a.at[step, b], c.at[step], send_sem.at[step, i], recv_sem.at[step, i], partner)
            for i, (a, b, c) in enumerate(
                [(wide_s, 1 - core, wide_l), (narrow_s, 1 - core, narrow_l)]
            )
        ]

    def stores(step):
        columns = pl.ds(pl.multiple_of(step * ft, ft), ft)
        at = pl.ds(step * shards, shards)
        return [
            pltpu.make_async_copy(wide_s.at[step, core], part_a.at[:, columns], own_sem.at[step, 0]),
            pltpu.make_async_copy(narrow_s.at[step, core], part_b.at[at], own_sem.at[step, 1]),
        ]

    def add(step):
        for copy in swaps(step):
            copy.wait_recv()
        wide_s[step, core] = (wide_s[step, core].astype(f32) + wide_l[step].astype(f32)).astype(bf16)
        narrow_s[step, core] = (narrow_s[step, core].astype(f32) + narrow_l[step].astype(f32)).astype(bf16)
        for copy in stores(step):
            copy.start()

    exps = back_ref.shape[0]
    columns = others("exp", exps)

    def returns():
        me = columns[0]
        made = [pltpu.make_async_copy(back_ref.at[me], ein_ref.at[me], b_send.at[0])]
        for k in range(1, exps):
            made.append(
                send(
                    back_ref.at[columns[k]], ein_ref.at[me],
                    b_send.at[k], b_recv.at[k], {"exp": columns[k]},
                )
            )
        return made

    @pl.when(f == 0)
    def _():
        greet([{"exp": column} for column in columns[1:]] + [partner])
        for copy in returns():
            copy.start()
        acc_out[...] = jnp.zeros_like(acc_out)
        acc_gin[...] = jnp.zeros_like(acc_gin)

    deep = wg_ref.shape[2] // 2
    wide = lambda ref: jnp.concatenate(
        [ref[0, :, :deep].reshape(width, 256), ref[0, :, deep:].reshape(width, 256)], axis=1
    )
    wg, wu = wide(wg_ref), wide(wu_ref)
    narrow = [
        jnp.concatenate([wn_ref[c, s, tall * b : tall * (b + 1)] for b in range(width // 256)], axis=1)
        for s in range(shards)
        for c in range(2)
    ]
    wn = jnp.concatenate(narrow, axis=0)
    for row in range(0, rows_all, tile):
        rows = pl.ds(row, tile)
        x, g = x_ref[rows, :], g_ref[rows, :]
        hidden, gg, ug = gated(x, g, wg, wu, wn)
        hid_s[rows, :], gg_s[rows, :], ug_s[rows, :] = hidden, gg, ug
        acc_out[rows, :] += mm(hidden, wn)
        acc_gin[rows, :] += mm_nt(gg, wg) + mm_nt(ug, wu)
    wide_s[f, 0] = mm_tn(x_ref[...], gg_s[...]).astype(bf16)
    wide_s[f, 1] = mm_tn(x_ref[...], ug_s[...]).astype(bf16)
    narrow = mm_tn(hid_s[...], g_ref[...]).astype(bf16).reshape(shards, 2, tall, width)
    for c in range(2):
        narrow_s[f, c] = narrow[:, c]
    for copy in swaps(f):
        copy.start()

    @pl.when(f > 0)
    def _():
        add(f - 1)

    @pl.when(f == last)
    def _():
        out_ref[...] = acc_out[...].astype(out_ref.dtype)
        gin_ref[...] = acc_gin[...].astype(gin_ref.dtype)

        add(last)

        @pl.loop(0, pl.num_programs(0))
        def _(step):
            for copy in swaps(step):
                copy.wait_send()
            for copy in stores(step):
                copy.wait()

        for copy in returns():
            copy.wait()


def ffn(x, g, packed, back, hidden, out_type, tile, name):
    rows, width = x.shape
    _, spread, height, _ = packed.shape
    ft = 512
    steps = hidden // ft
    deep, tall = width // spread, hidden // spread // 2
    shards = spread // steps
    base = hidden // 256 * deep
    narrow_high = height - base
    sems = pltpu.SemaphoreType.DMA((steps, 2))
    return pl.pallas_call(
        functools.partial(ffn_kernel, tile=tile),
        grid=(steps,),
        in_specs=[
            once((rows, width)),
            once((rows, width)),
            pl.BlockSpec((1, spread, 2 * deep, 256), lambda f: (0, 0, f, 0)),
            pl.BlockSpec((1, spread, 2 * deep, 256), lambda f: (1, 0, f, 0)),
            pl.BlockSpec((2, shards, narrow_high, 256), lambda f: (0, f, base // narrow_high, 0)),
            ANY,
        ],
        out_specs=[once((rows, width)), once((rows, width)), ANY, ANY, ANY],
        out_shape=[
            jax.ShapeDtypeStruct((rows, width), out_type),
            jax.ShapeDtypeStruct((rows, width), out_type),
            jax.ShapeDtypeStruct((width, hidden), bf16),
            jax.ShapeDtypeStruct((spread, tall, width), bf16),
            jax.ShapeDtypeStruct(back.shape, bf16),
        ],
        scratch_shapes=[
            pltpu.VMEM((rows, width), f32),
            pltpu.VMEM((rows, width), f32),
            pltpu.VMEM((rows, ft), bf16),
            pltpu.VMEM((rows, ft), bf16),
            pltpu.VMEM((rows, ft), bf16),
            pltpu.VMEM((steps, 2, width, ft), bf16),
            pltpu.VMEM((steps, 2, shards, tall, width), bf16),
            pltpu.VMEM((steps, width, ft), bf16),
            pltpu.VMEM((steps, shards, tall, width), bf16),
            sems, sems, sems,
        ]
        + pair_sems(back.shape[0]),
        compiler_params=params(("arbitrary",), collective_id=3, has_side_effects=True),
        cost_estimate=pl.CostEstimate(
            flops=18 * rows * width * hidden,
            bytes_accessed=12 * width * hidden + 8 * rows * width,
            transcendentals=rows * hidden,
        ),
        name=name,
    )(x, g, packed, packed, packed, back)


def plane_copies(exps, block_for, landed_ref, send_sem, recv_sem):
    columns = others("exp", exps)
    made = [pltpu.make_async_copy(block_for(columns[0]), landed_ref.at[0], send_sem.at[0])]
    for k in range(1, exps):
        made.append(
            send(
                block_for(columns[k]), landed_ref.at[k],
                send_sem.at[k], recv_sem.at[k], {"exp": columns[k]},
            )
        )
    return made


def pair_sems(count):
    return [pltpu.SemaphoreType.DMA((count,)), pltpu.SemaphoreType.DMA((count,))]


def combine_kernel(
    mid_ref, sout_ref, sin_ref, g_ref, h2_ref, probs_ref, place_ref, eout_ref, ein_ref,
    gains_ref, wr_ref, wo_ref, part_ref,
    block_ref, midg_ref, midb_ref, og_ref, gain_ref, rgrad_ref, landed_ref,
    send_sem, recv_sem,
):
    step = pl.program_id(0)
    exps = part_ref.shape[0]
    exchange = lambda: plane_copies(exps, lambda c: part_ref.at[c], landed_ref, send_sem, recv_sem)

    @pl.when(step == 0)
    def _():
        greet([{"exp": column} for column in others("exp", exps)[1:]])
        for copy in exchange():
            copy.start()

    tile, width = mid_ref.shape
    experts_all, cap = eout_ref.shape[0], eout_ref.shape[1]
    slot = lax.broadcasted_iota(jnp.int32, (tile, cap), 1)
    g = g_ref[...].astype(f32)
    probs = probs_ref[...]
    spot = lax.broadcasted_iota(jnp.int32, probs.shape, 1)
    mixture = jnp.zeros((tile, width), f32)
    moe_in = jnp.zeros((tile, width), f32)
    pgrad = jnp.zeros(probs.shape, f32)
    for e in range(experts_all):
        hot = (slot == place_ref[:, e : e + 1]).astype(f32).astype(bf16)
        pair_out = mm(hot, eout_ref[e])
        mixture += probs[:, e : e + 1] * pair_out
        grad = jnp.sum(g * pair_out, axis=1, keepdims=True)
        pgrad = jnp.where(spot == e, grad, pgrad)
        moe_in += mm(hot, ein_ref[e])
    mid = mid_ref[...]
    block_ref[...] = (mid + sout_ref[...] + mixture).astype(bf16)
    inner = jnp.sum(pgrad * probs, axis=1, keepdims=True)
    lgrad = (probs * (pgrad - inner)).astype(bf16)
    h2_grad = moe_in + mm_nt(lgrad, wr_ref[...]) + sin_ref[...]
    r2 = lax.rsqrt(jnp.mean(mid * mid, axis=1, keepdims=True) + norm_eps)
    n2 = mid * r2
    d2 = h2_grad * gains_ref[5:6, :]
    mid_grad = g + r2 * (d2 - n2 * jnp.mean(d2 * n2, axis=1, keepdims=True))
    midb = mid_grad.astype(bf16)
    midg_ref[...] = mid_grad
    midb_ref[...] = midb
    og_ref[...] = mm_nt(midb, wo_ref[0]).astype(bf16)
    gsum = jnp.sum(h2_grad * n2, axis=0, keepdims=True)
    rsum = mm_tn(lgrad, h2_ref[...])[:8]

    @pl.when(step == 0)
    def _():
        gain_ref[...] = jnp.zeros_like(gain_ref)
        rgrad_ref[...] = jnp.zeros_like(rgrad_ref)

    gain_ref[0:1, :] += gsum
    rgrad_ref[...] += rsum

    @pl.when(step == pl.num_programs(0) - 1)
    def _():
        for copy in exchange():
            copy.wait()


def combine(mid, sout, sin, g, h2, probs, place_col, eout, ein, gains, wr, full, part):
    seq, width = mid.shape
    tile = 256
    by_rows = pl.BlockSpec((tile, width), lambda i: (i, 0))
    lanes = pl.BlockSpec((tile, 128), lambda i: (i, 0))
    return pl.pallas_call(
        combine_kernel,
        grid=(seq // tile,),
        in_specs=[
            by_rows, by_rows, by_rows, by_rows, by_rows, lanes, lanes,
            once(eout.shape), once(ein.shape), once(gains.shape), once(wr.shape),
            pl.BlockSpec((1, width, width), lambda i: (3, 0, 0), pipeline_mode=pl.Buffered(1)),
            ANY,
        ],
        out_specs=[
            by_rows, by_rows, by_rows, by_rows, whole_spec((8, width)), whole_spec((8, width)), ANY,
        ],
        out_shape=[
            jax.ShapeDtypeStruct((seq, width), bf16),
            jax.ShapeDtypeStruct((seq, width), f32),
            jax.ShapeDtypeStruct((seq, width), bf16),
            jax.ShapeDtypeStruct((seq, width), bf16),
            jax.ShapeDtypeStruct((8, width), f32),
            jax.ShapeDtypeStruct((8, width), f32),
            jax.ShapeDtypeStruct(part.shape, bf16),
        ],
        scratch_shapes=pair_sems(part.shape[0]),
        compiler_params=params(("arbitrary",), collective_id=5, has_side_effects=True),
        cost_estimate=pl.CostEstimate(
            flops=11_000_000_000, bytes_accessed=30_000_000, transcendentals=0
        ),
        name="combine",
    )(mid, sout, sin, g, h2, probs, place_col, eout, ein, gains, wr, full, part)


def backward_kernel(
    exps, shds,
    qkv_ref, og_ref, lse_ref, bidr_ref, bidc_ref, tok_ref, midg_ref, o_ref, midb_ref, w_ref,
    gains_ref, gain2_ref, rgrad_ref, lb_ref, part_ref,
    igrad_ref, sw_ref, sa_ref, sb_ref, st_ref,
    dk_s, dv_s, h1t_s, ot_s, grad_s, stack_s, pair_s, plane_s, r_s, zr_s, fw_s,
    la_s, qa_s, qb_s, za_s, zb_s, fa_s, fb_s, tiny_s, tpair_s, tplane_s, tz_s,
    a_send, a_recv, pair_send, pair_recv, p_send, p_recv, r_send, r_recv, f_own, f_send, f_recv,
    line_send, line_recv, last_own, last_send, last_recv, t_send, t_recv, tp_send, tp_recv,
):
    step = pl.program_id(0)
    columns, layers = others("exp", exps), others("shd", shds)
    group = lax.axis_index("grp")
    core = lax.rem(group, 2)
    partner = {"grp": lax.bitwise_xor(group, 1)}
    seq, width = tok_ref.shape
    tile = 256
    pieces = width // 128
    deep = width // exps
    early = [(j + 1) % shds for j in range(shds)]

    def chunk(j):
        return plane_copies(
            exps, lambda c: part_ref.at[c, layers[j]], la_s.at[j], a_send.at[j], a_recv.at[j]
        )

    def chunk_line(j):
        return send(
            qa_s.at[j], za_s.at[j], line_send.at[0, j], line_recv.at[0, j], {"shd": layers[j]}
        )

    def chunk_sum(j, landed):
        value = landed[0].astype(f32)
        for k in range(1, exps):
            value = value + landed[k].astype(f32)
        qa_s[j] = value.astype(bf16)
        if j:
            chunk_line(j).start()

    def line(part_s, landed_s, kind):
        return [
            send(
                part_s.at[layers[k]], landed_s.at[k],
                line_send.at[kind, k], line_recv.at[kind, k], {"shd": layers[k]},
            )
            for k in range(1, shds)
        ]

    def plane_rows(k):
        return pl.ds(pl.multiple_of(columns[k] * deep, 16), deep)

    def pair_copy(p):
        return send(stack_s.at[p], pair_s.at[p // 2], pair_send.at[p // 2], pair_recv.at[p // 2], partner)

    def plane_copy(p):
        return [
            send(
                stack_s.at[p, :, plane_rows(k), :], plane_s.at[p // 2, k],
                p_send.at[p // 2, k], p_recv.at[p // 2, k], {"exp": columns[k]},
            )
            for k in range(1, exps)
        ]

    def line_copy(p):
        return [
            send(
                r_s.at[p // 2, layers[k]], zr_s.at[p // 2, k],
                r_send.at[p // 2, k], r_recv.at[p // 2, k], {"shd": layers[k]},
            )
            for k in range(1, shds)
        ]

    def final_copy(p):
        at = sw_ref.at[:, :, pl.ds(pl.multiple_of(p * 128, 128), 128)]
        return [
            pltpu.make_async_copy(fw_s.at[p // 2], at, f_own.at[p // 2]),
            send(fw_s.at[p // 2], at, f_send.at[p // 2], f_recv.at[p // 2], partner),
        ]

    def start(copies):
        for copy in copies:
            copy.start()

    def summing(p):
        return jnp.logical_and(p >= 0, core == p % 2)

    def to_pair(p):
        @pl.when(core != p % 2)
        def _():
            pair_copy(p).start()

    def to_plane(p):
        @pl.when(summing(p))
        def _():
            pair_copy(p).wait_recv()
            for i in range(4):
                stack_s[p, i] = (stack_s[p, i].astype(f32) + pair_s[p // 2, i].astype(f32)).astype(bf16)
            start(plane_copy(p))

    def to_line(p):
        @pl.when(summing(p))
        def _():
            for copy in plane_copy(p):
                copy.wait_recv()
            for i in range(4):
                value = stack_s[p, i, plane_rows(0), :].astype(f32)
                for k in range(1, exps):
                    value = value + plane_s[p // 2, k, i].astype(f32)
                r_s[p // 2, :, i] = value.astype(bf16).reshape(shds, deep // shds, 128)
            start(line_copy(p))

    def to_final(p):
        @pl.when(summing(p))
        def _():
            for copy in line_copy(p):
                copy.wait_recv()
            value = r_s[p // 2, layers[0]].astype(f32)
            for k in range(1, shds):
                value = value + zr_s[p // 2, k].astype(f32)
            fw_s[p // 2] = value
            start(final_copy(p))

    def line_total(landed_s, part_s):
        value = part_s[layers[0]].astype(f32)
        for k in range(1, shds):
            value = value + landed_s[k].astype(f32)
        return value

    def finals(kind, part_s, out_ref):
        return [
            pltpu.make_async_copy(part_s, out_ref.at[core], last_own.at[kind]),
            send(part_s, out_ref.at[core], last_send.at[kind], last_recv.at[kind], partner),
        ]

    @pl.when(step == 0)
    def _():
        greet(
            [{"shd": layer} for layer in layers[1:]]
            + [{"exp": column} for column in columns[1:]]
            + [partner]
        )
        for z in range(shds):
            qb_s[z] = sum([lb_ref[k, z].astype(f32) for k in range(1, exps)], lb_ref[0, z].astype(f32)).astype(bf16)
        start(line(qb_s, zb_s, 1))
        for row in range(0, seq, tile):
            x = tok_ref[row : row + tile, :].astype(f32)
            r1 = lax.rsqrt(jnp.mean(x * x, axis=1, keepdims=True) + norm_eps)
            h1t_s[:, row : row + tile] = (x * r1 * gains_ref[4:5, :]).astype(bf16).T
            ot_s[:, row : row + tile] = o_ref[row : row + tile, :].T
        grad_s[...] = jnp.zeros_like(grad_s)

    for turn, j in enumerate(early):

        @pl.when(step == turn)
        def _():
            start(chunk(j))

        @pl.when(step == turn + 2)
        def _():
            for copy in chunk(j):
                copy.wait()
            chunk_sum(j, la_s.at[j])

    @pl.when(step == shds)
    def _():
        for copy in line(qb_s, zb_s, 1):
            copy.wait()
        fb_s[...] = line_total(zb_s, qb_s)
        start(finals(1, fb_s, sb_ref))

    qs = qkv_ref[0] * jnp.asarray(0.125, bf16)
    k = qkv_ref[1]
    v = qkv_ref[2]
    kt = k.T
    og = og_ref[...]
    lane = lax.broadcasted_iota(jnp.int32, (tile, 128), 1)
    dk_s[...] = jnp.zeros_like(dk_s)
    dv_s[...] = jnp.zeros_like(dv_s)
    dqs = []
    for q0 in range(0, seq, tile):
        kl = min(seq, q0 + 2 * tile)
        qt, ot = qs[q0 : q0 + tile], og[q0 : q0 + tile]
        allowed = bidc_ref[q0:kl, :] <= bidr_ref[0:1, q0 : q0 + tile]
        parts = []
        for head in range(2):
            own = (lane // 64) == head
            qm = jnp.where(own, qt, jnp.zeros_like(qt))
            om = jnp.where(own, ot, jnp.zeros_like(ot))
            lse = lse_ref[0, head : head + 1, q0 : q0 + tile]
            spans = ([(0, q0)] if q0 else []) + [(q0, kl)]
            kept = []
            delta = jnp.zeros((1, tile), f32)
            for low, high in spans:
                s = mm_nt(k[low:high], qm)
                if low == q0:
                    s = jnp.where(allowed, s, masked_score)
                p = jnp.exp(s - lse)
                dp = mm_nt(v[low:high], om)
                delta = delta + jnp.sum(p * dp, axis=0, keepdims=True)
                kept.append((low, high, p, dp))
            dq = jnp.zeros((64, tile), f32)
            for low, high, p, dp in kept:
                ds = (p * (dp - delta)).astype(bf16)
                dv_s[low:high, :] += mm(p.astype(bf16), om)
                dk_s[low:high, :] += mm(ds, qm)
                dq = dq + mm(kt[64 * head : 64 * head + 64, low:high], ds)
            parts.append(dq)
        dqs.append((jnp.concatenate(parts, axis=0).T * 0.125).astype(bf16))
        if q0 == tile:
            to_plane(step - 1)
    dqkv = [jnp.concatenate(dqs, axis=0), dk_s[...].astype(bf16), dv_s[...].astype(bf16)]
    to_final(step - 4)
    to_line(step - 3)
    wide = mm(h1t_s[...], jnp.concatenate(dqkv, axis=1)).astype(bf16)
    for i in range(3):
        stack_s[step, i] = wide[:, 128 * i : 128 * i + 128]
    stack_s[step, 3] = mm(ot_s[...], midb_ref[...]).astype(bf16)
    to_pair(step)
    for row in range(0, seq, tile):
        rows = slice(row, row + tile)
        grad_s[rows, :] += (
            mm_nt(dqkv[0][rows], w_ref[0]) + mm_nt(dqkv[1][rows], w_ref[1]) + mm_nt(dqkv[2][rows], w_ref[2])
        )

    @pl.when(step == pieces - 1)
    def _():
        to_line(pieces - 3)
        to_final(pieces - 4)
        to_plane(pieces - 1)
        gain = jnp.zeros((1, width), f32)
        for row in range(0, seq, tile):
            rows = slice(row, row + tile)
            x = tok_ref[rows, :].astype(f32)
            r1 = lax.rsqrt(jnp.mean(x * x, axis=1, keepdims=True) + norm_eps)
            n1 = x * r1
            grad = grad_s[rows, :]
            gain = gain + jnp.sum(grad * n1, axis=0, keepdims=True)
            d1 = grad * gains_ref[4:5, :]
            igrad_ref[rows, :] = midg_ref[rows, :] + r1 * (d1 - n1 * jnp.mean(d1 * n1, axis=1, keepdims=True))
        spot = lax.broadcasted_iota(jnp.int32, (8, width), 0)
        small = jnp.where(spot < 4, rgrad_ref[...], jnp.where(spot == 4, gain, gain2_ref[0:1, :]))
        tiny_s[...] = small
        tswap = send(tiny_s, tpair_s, t_send, t_recv, partner)
        tswap.start()
        to_line(pieces - 2)
        to_final(pieces - 3)
        to_line(pieces - 1)
        tswap.wait()
        tpair_s[...] += tiny_s[...]
        tplane = [
            send(tpair_s, tplane_s.at[k], tp_send.at[k], tp_recv.at[k], {"exp": columns[k]})
            for k in range(1, exps)
        ]
        start(tplane)
        to_final(pieces - 2)
        for copy in tplane:
            copy.wait()
        value = qa_s[0].astype(f32)
        for j in range(1, shds):
            chunk_line(j).wait()
            value = value + za_s[j].astype(f32)
        fa_s[...] = value
        start(finals(0, fa_s, sa_ref))
        tz_s[0] = sum([tplane_s[k] for k in range(1, exps)], tpair_s[...])
        tline = [
            send(
                tz_s.at[0], tz_s.at[k], line_send.at[2, k], line_recv.at[2, k], {"shd": layers[k]}
            )
            for k in range(1, shds)
        ]
        start(tline)
        to_final(pieces - 1)
        for copy in tline:
            copy.wait()
        st_ref[...] = sum([tz_s[k] for k in range(1, shds)], tz_s[0])
        for p in range(pieces):

            @pl.when(core == p % 2)
            def _():
                for copy in plane_copy(p) + line_copy(p) + final_copy(p)[1:]:
                    copy.wait_send()
                final_copy(p)[0].wait()

            @pl.when(core != p % 2)
            def _():
                pair_copy(p).wait_send()
                final_copy(p)[1].wait_recv()

        for copy in finals(1, fb_s, sb_ref) + finals(0, fa_s, sa_ref):
            copy.wait()


def attention_backward(qkv, og, lse, bid_row, bid_col, tokens, midg, o, midb, full, gains, gain2, rgrad, lb, part):
    exps, shds = part.shape[:2]
    seq, width = tokens.shape
    rows = part.shape[2]
    pairs = width // 128
    half = pairs // 2
    big = lambda *shape: pltpu.VMEM(shape, bf16)
    wide = lambda *shape: pltpu.VMEM(shape, f32)
    sems = lambda *n: pltpu.SemaphoreType.DMA(n)
    a, b = part.shape[2:], lb.shape[2:]
    return pl.pallas_call(
        functools.partial(backward_kernel, exps, shds),
        grid=(pairs,),
        in_specs=[
            pl.BlockSpec((3, seq, 128), lambda i: (0, 0, i)),
            pl.BlockSpec((seq, 128), lambda i: (0, i)),
            pl.BlockSpec((1, 8, seq), lambda i: (i, 0, 0)),
            once(bid_row.shape),
            once(bid_col.shape),
            once(tokens.shape),
            once(midg.shape),
            once(o.shape),
            pl.BlockSpec((seq, 128), lambda i: (0, i)),
            pl.BlockSpec((3, width, 128), lambda i: (0, 0, i)),
            once(gains.shape),
            once(gain2.shape),
            once(rgrad.shape),
            once(lb.shape),
            ANY,
        ],
        out_specs=[once((seq, width)), ANY, ANY, ANY, once((8, width))],
        out_shape=[
            jax.ShapeDtypeStruct((seq, width), f32),
            jax.ShapeDtypeStruct((4, rows, width), f32),
            jax.ShapeDtypeStruct((2,) + a, f32),
            jax.ShapeDtypeStruct((2,) + b, f32),
            jax.ShapeDtypeStruct((8, width), f32),
        ],
        scratch_shapes=[
            wide(seq, 128),
            wide(seq, 128),
            big(width, seq),
            big(width, seq),
            wide(seq, width),
            big(pairs, 4, width, 128),
            big(half, 4, width, 128),
            big(half, exps, 4, width // exps, 128),
            big(half, shds, 4, rows, 128),
            big(half, shds, 4, rows, 128),
            wide(half, 4, rows, 128),
            big(shds, exps, *a),
            big(shds, *a),
            big(shds, *b),
            big(shds, *a),
            big(shds, *b),
            wide(*a),
            wide(*b),
            wide(8, width),
            wide(8, width),
            wide(exps, 8, width),
            wide(shds, 8, width),
            sems(shds, exps), sems(shds, exps), sems(half), sems(half),
            sems(half, exps), sems(half, exps), sems(half, shds), sems(half, shds),
            sems(half), sems(half), sems(half),
            sems(3, shds), sems(3, shds), sems(2), sems(2), sems(2),
            pltpu.SemaphoreType.DMA, pltpu.SemaphoreType.DMA, sems(exps), sems(exps),
        ],
        compiler_params=params(("arbitrary",), collective_id=6, has_side_effects=True),
        cost_estimate=pl.CostEstimate(
            flops=80_000_000_000, bytes_accessed=30_000_000, transcendentals=12_000_000
        ),
        name="attention_backward",
    )(
        qkv, og, lse, bid_row, bid_col, tokens, midg, o, midb, full,
        gains, gain2, rgrad, lb, part,
    )


def adam_update(weight, moment, square, gradient, step_rate, shrink_rate):
    moment_next = beta_one * moment + (1.0 - beta_one) * gradient
    square_next = beta_two * square + (1.0 - beta_two) * gradient * gradient
    direction = moment_next / first_fix / (jnp.sqrt(square_next / second_fix) + adam_eps)
    return (weight - step_rate * (direction + shrink_rate * weight), moment_next, square_next)


def adam_kernel(rates, w_ref, m_ref, v_ref, g_ref, wo_ref, mo_ref, vo_ref):
    shape = w_ref.shape
    high = shape[-2]
    gradient = g_ref[0].astype(f32)
    parts = [gradient[i : i + high] for i in range(0, gradient.shape[0], high)]
    gradient = jnp.concatenate(parts, axis=1).reshape(shape)
    wo_ref[...], mo_ref[...], vo_ref[...] = adam_update(
        w_ref[...], m_ref[...], v_ref[...], gradient, *rates
    )


def adam_blocks(kind, state, sums, grid, spec, sums_spec):
    return pl.pallas_call(
        functools.partial(adam_kernel, (learning_rates[kind], decay_rates[kind])),
        grid=grid,
        in_specs=[spec] * 3 + [sums_spec],
        out_specs=[spec] * 3,
        out_shape=[jax.ShapeDtypeStruct(state[0].shape, f32)] * 3,
        compiler_params=params(("arbitrary",) * len(grid)),
        cost_estimate=pl.CostEstimate(
            flops=20 * state[0].size, bytes_accessed=26 * state[0].size, transcendentals=0
        ),
        name="adam_blocks",
    )(*state, sums)


def pick(array, axis, index):
    return lax.dynamic_index_in_dim(array, index, axis, keepdims=False)


def share(part, groups, core):
    swap = [(i, i ^ 1) for i in range(groups)]
    both = jnp.zeros((2,) + part.shape, part.dtype)
    both = lax.dynamic_update_index_in_dim(both, part, core, 0)
    if groups > 2:
        return lax.psum(both, "grp")
    return lax.dynamic_update_index_in_dim(both, lax.ppermute(part, "grp", swap), 1 - core, 0)


def on_device(
    tokens_in, cotangent, block_ids, expert_ids,
    scales, moment_scales, square_scales, attend, moment_attend, square_attend,
    output, moment_output, square_output, router, moment_router, square_router,
    widener, moment_widener, square_widener, reducer, moment_reducer, square_reducer,
    experts, moment_experts, square_experts, narrower, moment_narrower, square_narrower,
):
    groups, exps, shds = (lax.axis_size(a) for a in ("grp", "exp", "shd"))
    spread = exps * shds
    core = lax.rem(lax.axis_index("grp"), 2)
    _, seq, width = tokens_in.shape
    hidden = reducer.shape[0] * spread
    experts_all = exps * experts.shape[0]
    rows, tall = output.shape[0], reducer.shape[0] // 2
    deep = width // shds
    tokens, g = tokens_in.reshape(seq, width), cotangent.reshape(seq, width)

    def packed(wide, narrow):
        wide = pick(wide.astype(bf16), 0, core)
        narrow = pick(narrow.astype(bf16).reshape(2, -1, width), 0, core)
        blocks = [
            a.reshape(a.shape[0], -1, 256).transpose(1, 0, 2).reshape(-1, 256) for a in (wide, narrow)
        ]
        return jnp.concatenate(blocks, axis=0)

    def gather(part, axes):
        wide = lax.all_gather(part, ("grp",) + axes, axis=0, tiled=False)
        return wide.reshape((groups, -1) + part.shape)[:2]

    mine = jnp.where(
        core == 0,
        attend[:2].astype(bf16),
        jnp.stack([attend[2].astype(bf16), output.astype(bf16)]),
    )
    tiny = jnp.concatenate([router, scales.T], axis=1).astype(bf16)
    tiny = jnp.pad(tiny, ((0, 0), (0, 128 - tiny.shape[1])))
    expert_weights = gather(packed(experts[0], narrower[0]), ("shd",))
    shared_weights = gather(packed(widener, reducer), ("exp", "shd"))

    ids = expert_ids.reshape(seq, 2)
    every = jnp.arange(128, dtype=jnp.int32)[None, :]
    hot = (ids[:, 0:1] == every) | (ids[:, 1:2] == every)
    order = jnp.arange(seq, dtype=jnp.int32)
    before = (order[:, None] > order[None, :]).astype(bf16)
    placed = mm(before, hot.astype(bf16)).astype(jnp.int32)
    place_col = jnp.where(hot, placed, -1)
    place_row = place_col[:, :16].T
    bid = block_ids.reshape(1, seq)
    bid_row = jnp.broadcast_to(bid, (8, seq))
    bid_col = jnp.broadcast_to(bid.reshape(seq, 1), (seq, 256))

    lanes = -(-CAP // 128) * 128
    full, wr, g_slots = gather_first(mine, tiny, g, place_row, exps, shds, experts_all, CAP)
    qkv, lse, o, mid, h2, probs, probst, gains, g_landed = attention_forward(
        tokens, bid_row, bid_col, full, wr, g_slots
    )
    slot_rows, chosen = dispatch(h2, place_row, probst, experts_all, CAP, lanes)
    eout, back, part = routed(slot_rows, chosen, g_landed, expert_weights, hidden)
    part = lax.psum_scatter(part, "shd", scatter_dimension=0, tiled=False)
    sout, sin, part_a, part_b, ein = ffn(
        h2, g, shared_weights, back, hidden, f32, 256, "shared"
    )
    part_a = part_a.reshape(exps, shds, rows, hidden)
    part_b = part_b.reshape(exps, shds, tall, width)
    block_out, mid_grad, midb, og, gain_two, rgrad, landed_b = combine(
        mid, sout, sin, g, h2, probs, place_col, eout, ein, gains, wr, full, part_b
    )
    input_grad, sum_w, sum_a, sum_b, sum_t = attention_backward(
        qkv, og, lse, bid_row, bid_col, tokens, mid_grad, o, midb, full,
        gains, gain_two, rgrad, landed_b, part_a,
    )
    if groups > 2:
        sum_w, sum_a, sum_b, sum_t = (
            0.5 * lax.psum(v, "grp") for v in (sum_w, sum_a, sum_b, sum_t)
        )
    expert_sums = share(part, groups, core)
    wide_state = [v[0] for v in (experts, moment_experts, square_experts)]
    new_experts = adam_blocks(
        6, wide_state, expert_sums, (2, hidden // 512),
        pl.BlockSpec((1, deep, 512), lambda c, b: (c, 0, b)),
        pl.BlockSpec((1, 2 * deep, 256), lambda c, b: (c, b, 0)),
    )
    narrow_state = [v[0] for v in (narrower, moment_narrower, square_narrower)]
    high = narrower.shape[1] // 2
    across = width // 256
    skip = hidden // 256 * deep // (across * high)
    new_narrower = adam_blocks(
        7, narrow_state, expert_sums, (2, 1),
        pl.BlockSpec((high, width), lambda c, b: (c, b)),
        pl.BlockSpec((1, across * high, 256), lambda c, b: (c, skip + b, 0)),
    )
    shard = lax.axis_index("exp") * shds + lax.axis_index("shd")
    sum_t = lax.dynamic_slice_in_dim(sum_t, shard * rows, rows, 1)
    grads = (
        sum_t[4:6],
        sum_w[:3],
        sum_w[3],
        sum_t[:experts_all].T,
        sum_a,
        sum_b.reshape(reducer.shape),
    )
    masters = (scales, attend, output, router, widener, reducer)
    moments = (
        moment_scales, moment_attend, moment_output, moment_router,
        moment_widener, moment_reducer,
    )
    squares = (
        square_scales, square_attend, square_output, square_router,
        square_widener, square_reducer,
    )
    results = [block_out.reshape(tokens_in.shape), input_grad.reshape(tokens_in.shape)]
    for kind in range(6):
        results.extend(
            adam_update(
                masters[kind], moments[kind], squares[kind], grads[kind],
                learning_rates[kind], decay_rates[kind],
            )
        )
    results.extend(v[None] for v in new_experts)
    results.extend(v[None] for v in new_narrower)
    return tuple(results)


def solution(mesh):
    tokens = P(("grp", "exp", "shd"), None, None)
    both = ("exp", "shd")
    kinds = (
        P(None, both), P(None, both, None), P(both, None), P(both, None),
        P(None, both, None), P(both, None), P("exp", None, "shd", None), P("exp", "shd", None),
    )
    thrice = tuple(kind for kind in kinds for _ in range(3))
    return jax.shard_map(
        on_device,
        mesh=mesh,
        in_specs=(tokens, tokens, P(("grp", "exp", "shd"), None), tokens) + thrice,
        out_specs=(tokens, tokens) + thrice,
        check_vma=False,
    )
```

```python
import functools

import jax
import jax.numpy as jnp
from jax import lax
from jax.experimental import pallas as pl
from jax.experimental.pallas import tpu as pltpu
from jax.sharding import PartitionSpec as P

HEADS = 12
CAP = 576
VMEM_LIMIT = 60 * 1024 * 1024

norm_eps = 1e-06
adam_eps = 1e-08
beta_one = 0.9
beta_two = 0.95
first_fix = 1.0 - 0.9**10
second_fix = 1.0 - 0.95**10
learning_rates = (0.3, 0.02, 0.15, 0.02, 0.02, 0.012, 0.02, 0.012)
decay_rates = (0.0, 0.1, 0.1, 0.1, 0.1, 0.1, 0.1, 0.1)
masked_score = -1e30
bf16 = jnp.bfloat16
f32 = jnp.float32


def mm(a, b):
    return jnp.dot(a, b, preferred_element_type=f32)


def mm_nt(a, b):
    return lax.dot_general(a, b, (((1,), (1,)), ((), ())), preferred_element_type=f32)


def mm_tn(a, b):
    return lax.dot_general(a, b, (((0,), (0,)), ((), ())), preferred_element_type=f32)


def params(semantics=None, **more):
    return pltpu.CompilerParams(
        dimension_semantics=semantics, vmem_limit_bytes=VMEM_LIMIT, **more
    )


def whole_spec(shape, **more):
    zeros = (0,) * len(shape)
    return pl.BlockSpec(shape, lambda *_: zeros, **more)


def once(shape):
    return whole_spec(shape, pipeline_mode=pl.Buffered(1))


MESH = pl.DeviceIdType.MESH
ANY = pl.BlockSpec(memory_space=pl.ANY)


def greet(targets):
    barrier = pltpu.get_barrier_semaphore()
    for target in targets:
        pl.semaphore_signal(barrier, inc=1, device_id=target, device_id_type=MESH)
    pl.semaphore_wait(barrier, len(targets))


def send(src, dst, send_sem, recv_sem, target):
    return pltpu.make_async_remote_copy(
        src_ref=src, dst_ref=dst, send_sem=send_sem, recv_sem=recv_sem,
        device_id=target, device_id_type=MESH,
    )


def pair_sems(count):
    return [pltpu.SemaphoreType.DMA((count,)), pltpu.SemaphoreType.DMA((count,))]


def others(axis, count):
    me = lax.axis_index(axis)
    return [lax.bitwise_xor(me, k) for k in range(count)]


def gather_kernel(
    exps, shds,
    mine_ref, tiny_ref, pack_ref, g_ref, ids_ref,
    full_ref, every_ref, packs_ref, slots_ref, row_ref, col_ref,
    own_sem, z_send, z_recv, p_send, p_recv, c_send, c_recv, k_send, k_recv,
):
    columns, layers = others("exp", exps), others("shd", shds)
    group = lax.axis_index("grp")
    core = lax.rem(group, 2)
    partner = {"grp": lax.bitwise_xor(group, 1)}
    rows = mine_ref.shape[1]
    relay = exps == 4
    direct = range(1, 3 if relay else exps)

    def spots(kz, kx):
        at = pl.ds(pl.multiple_of((columns[kx] * shds + layers[kz]) * rows, 16), rows)
        return full_ref.at[pl.ds(2 * core, 2), at, :], every_ref.at[at, :]

    greet(
        [{"shd": layer} for layer in layers[1:]]
        + [{"exp": column} for column in columns[1:]]
        + [partner]
    )
    started = []

    def begin(copies):
        for copy in copies:
            copy.start()
        started.extend(copies)
        return copies

    def both(sources, kz, kx, sem, far, index, target):
        return [
            send(a, b, sem.at[index + (i,)], far.at[index + (i,)], target)
            for i, (a, b) in enumerate(zip(sources, spots(kz, kx)))
        ]

    mine = (mine_ref, tiny_ref)
    local = [
        pltpu.make_async_copy(a, b, own_sem.at[i])
        for i, (a, b) in enumerate(zip(mine, spots(0, 0)))
    ]
    for copy in local:
        copy.start()
    down = [both(mine, 0, 0, z_send, z_recv, (k,), {"shd": layers[k]}) for k in range(1, shds)]
    for copies in down:
        begin(copies)
    across = {}
    for kx in direct:
        across[0, kx] = begin(both(mine, 0, 0, p_send, p_recv, (0, kx), {"exp": columns[kx]}))
    packs = [pltpu.make_async_copy(pack_ref, packs_ref.at[columns[0]], k_send.at[0])]
    for kx in direct:
        packs.append(
            send(pack_ref, packs_ref.at[columns[0]], k_send.at[kx], k_recv.at[kx], {"exp": columns[kx]})
        )
    for copy in packs:
        copy.start()
    swaps = [send(mine_ref, spots(0, 0)[0], c_send.at[0, 0], c_recv.at[0, 0], partner)]
    swaps[0].start()
    seq = g_ref.shape[0]
    expert = lax.broadcasted_iota(jnp.int32, (16, seq), 0)
    named = (ids_ref[0:1, :] == expert) | (ids_ref[1:2, :] == expert)
    earlier = lax.broadcasted_iota(jnp.int32, (seq, seq), 0) < lax.broadcasted_iota(jnp.int32, (seq, seq), 1)
    count = mm(named.astype(f32).astype(bf16), earlier.astype(f32).astype(bf16))
    place = jnp.where(named, count, -1.0)
    row_ref[...] = place.astype(jnp.int32)
    col_ref[...] = jnp.concatenate([place, jnp.full((112, seq), -1.0, f32)], axis=0).T.astype(jnp.int32)

    def fill(e):
        hot = slots_of(row_ref[e : e + 1, :], slots_ref.shape[1])
        slots_ref[e] = mm(hot, g_ref[...]).astype(bf16)

    def swap(kz, kx):
        here = spots(kz, kx)[0]
        copy = send(here, here, c_send.at[kz, kx], c_recv.at[kz, kx], partner)
        copy.start()
        swaps.append(copy)

    for kz in range(1, shds):
        for copy in down[kz - 1]:
            copy.wait_recv()
        for kx in direct:
            across[kz, kx] = begin(both(spots(kz, 0), kz, 0, p_send, p_recv, (kz, kx), {"exp": columns[kx]}))
        swap(kz, 0)
        if kz <= slots_ref.shape[0]:
            fill(kz - 1)
    for e in range(shds - 1, slots_ref.shape[0]):
        fill(e)
    if relay:
        half = pack_ref.shape[0] // 2
        for kx in direct:
            packs[kx].wait_recv()
            spot = packs_ref.at[columns[kx], pl.ds(half * (kx - 1), half), :]
            copy = send(spot, spot, k_send.at[2 + kx], k_recv.at[2 + kx], {"exp": columns[3 - kx]})
            copy.start()
            packs.append(copy)
    for kz in range(shds):
        via = 1 + kz % 2
        for kx in direct:
            for copy in across[kz, kx]:
                copy.wait_recv()
            if relay and kx == via:
                across[kz, 3] = begin(
                    both(spots(kz, kx), kz, kx, p_send, p_recv, (kz, 3), {"exp": columns[3 - via]})
                )
            swap(kz, kx)
    if relay:
        for kz in range(shds):
            for copy in across[kz, 3]:
                copy.wait_recv()
            swap(kz, 3)
    for copy in started:
        copy.wait_send()
    if relay:
        for kx in direct:
            packs[kx].wait_send()
        packs = packs[:1] + packs[3:]
    for copy in swaps + local + packs:
        copy.wait()


def gather_first(mine, tiny, pack, g, ids, exps, shds, experts_all, cap):
    _, rows, width = mine.shape
    tall = exps * shds * rows
    sems = lambda *shape: pltpu.SemaphoreType.DMA(shape)
    return pl.pallas_call(
        functools.partial(gather_kernel, exps, shds),
        in_specs=[ANY, ANY, ANY] + [pl.BlockSpec(memory_space=pltpu.VMEM)] * 2,
        out_specs=[ANY, ANY, ANY] + [pl.BlockSpec(memory_space=pltpu.VMEM)] * 3,
        out_shape=[
            jax.ShapeDtypeStruct((4, tall, width), bf16),
            jax.ShapeDtypeStruct((tall, 128), bf16),
            jax.ShapeDtypeStruct((exps,) + pack.shape, bf16),
            jax.ShapeDtypeStruct((experts_all, cap, width), bf16),
            jax.ShapeDtypeStruct((16, g.shape[0]), jnp.int32),
            jax.ShapeDtypeStruct((g.shape[0], 128), jnp.int32),
        ],
        scratch_shapes=[
            sems(2), sems(shds, 2), sems(shds, 2), sems(shds, exps, 2), sems(shds, exps, 2),
            sems(shds, exps), sems(shds, exps), sems(exps + 1), sems(exps + 1),
        ],
        compiler_params=params(collective_id=4, has_side_effects=True),
        cost_estimate=pl.CostEstimate(
            flops=40_000_000_000, bytes_accessed=10_000_000, transcendentals=0
        ),
        name="gather_first",
    )(mine, tiny, pack, g, ids)


def forward_kernel(
    exps,
    tok_ref, bidr_ref, bidc_ref, wa_ref, wo_ref, wr_ref, slots_ref,
    qkv_ref, lse_ref, o_ref, mid_ref, h2_ref, probs_ref, probst_ref, gains_ref, landed_ref, h1_ref,
    send_sem, recv_sem,
):
    pair = pl.program_id(0)
    me = lax.axis_index("exp")

    def copies():
        made = [pltpu.make_async_copy(slots_ref.at[me], landed_ref.at[0], send_sem.at[0])]
        for k in range(1, exps):
            peer = lax.bitwise_xor(me, k)
            made.append(
                send(slots_ref.at[peer], landed_ref.at[k], send_sem.at[k], recv_sem.at[k], {"exp": peer})
            )
        return made

    @pl.when(pair == 0)
    def _():
        greet([{"exp": lax.bitwise_xor(me, k)} for k in range(1, exps)])
        for copy in copies():
            copy.start()
    seq, width = tok_ref.shape
    tile = 256

    @pl.when(pair == 0)
    def _():
        gains_ref[...] = wr_ref[...].astype(f32).T[:8]
        for row in range(0, seq, tile):
            x = tok_ref[pl.ds(row, tile), :].astype(f32)
            r1 = lax.rsqrt(jnp.mean(x * x, axis=1, keepdims=True) + norm_eps)
            h1_ref[pl.ds(row, tile), :] = (x * r1 * gains_ref[4:5, :]).astype(bf16)

    h1 = h1_ref[...]
    for i in range(3):
        qkv_ref[i] = mm(h1, wa_ref[i]).astype(bf16)
    qs = qkv_ref[0] * jnp.asarray(0.125, bf16)
    k = qkv_ref[1]
    vt = qkv_ref[2].T
    lane = lax.broadcasted_iota(jnp.int32, (tile, 128), 1)
    for q0 in range(0, seq, tile):
        kl = min(seq, q0 + 2 * tile)
        qt = qs[q0 : q0 + tile]
        allowed = bidc_ref[q0:kl, :] <= bidr_ref[0:1, q0 : q0 + tile]
        parts = []
        for head in range(2):
            qm = jnp.where((lane // 64) == head, qt, jnp.zeros_like(qt))
            tail = jnp.where(allowed, mm_nt(k[q0:kl], qm), masked_score)
            top = jnp.max(tail, axis=0, keepdims=True)
            if q0:
                lead = mm_nt(k[:q0], qm)
                top = jnp.maximum(top, jnp.max(lead, axis=0, keepdims=True))
                lead = jnp.exp(lead - top)
            tail = jnp.exp(tail - top)
            total = jnp.sum(tail, axis=0, keepdims=True)
            if q0:
                total = total + jnp.sum(lead, axis=0, keepdims=True)
            inverse = 1.0 / total
            vh = vt[64 * head : 64 * head + 64]
            ot = mm(vh[:, q0:kl], (tail * inverse).astype(bf16))
            if q0:
                ot = ot + mm(vh[:, :q0], (lead * inverse).astype(bf16))
            lse_ref[0, head : head + 1, q0 : q0 + tile] = top + jnp.log(total)
            parts.append(ot)
        out = jnp.concatenate(parts, axis=0).T.astype(bf16)
        o_ref[q0 : q0 + tile, pl.ds(pl.multiple_of(pair * 128, 128), 128)] = out

    @pl.when(pair == pl.num_programs(0) - 1)
    def _():
        for row in range(0, seq, tile):
            rows = pl.ds(row, tile)
            mid = tok_ref[rows, :].astype(f32) + mm(o_ref[rows, :], wo_ref[0])
            mid_ref[rows, :] = mid
            r2 = lax.rsqrt(jnp.mean(mid * mid, axis=1, keepdims=True) + norm_eps)
            h2 = (mid * r2 * gains_ref[5:6, :]).astype(bf16)
            h2_ref[rows, :] = h2
            logits = mm(h2, wr_ref[...])
            spot = lax.broadcasted_iota(jnp.int32, logits.shape, 1)
            logits = jnp.where(spot < 4, logits, masked_score)
            e = jnp.exp(logits - jnp.max(logits, axis=1, keepdims=True))
            probs_ref[rows, :] = e / jnp.sum(e, axis=1, keepdims=True)
        routers = gains_ref[...].astype(bf16)
        logits = mm_nt(jnp.concatenate([routers, routers], axis=0), h2_ref[...])
        spot = lax.broadcasted_iota(jnp.int32, logits.shape, 0)
        logits = jnp.where(spot < 4, logits, masked_score)
        e = jnp.exp(logits - jnp.max(logits, axis=0, keepdims=True))
        probst_ref[...] = e / jnp.sum(e, axis=0, keepdims=True)
        for copy in copies():
            copy.wait()


def attention_forward(tokens, bid_row, bid_col, full, wr, slots):
    exps = slots.shape[0]
    seq, width = tokens.shape
    pairs = width // 128
    return pl.pallas_call(
        functools.partial(forward_kernel, exps),
        grid=(pairs,),
        in_specs=[
            once((seq, width)),
            once(bid_row.shape),
            once(bid_col.shape),
            pl.BlockSpec((3, width, 128), lambda i: (0, 0, i)),
            pl.BlockSpec((1, width, width), lambda i: (3, 0, 0), pipeline_mode=pl.Buffered(1)),
            once(wr.shape),
            ANY,
        ],
        out_specs=[
            pl.BlockSpec((3, seq, 128), lambda i: (0, 0, i)),
            pl.BlockSpec((1, 8, seq), lambda i: (i, 0, 0)),
            whole_spec((seq, width)),
            whole_spec((seq, width)),
            whole_spec((seq, width)),
            whole_spec((seq, 128)),
            whole_spec((16, seq)),
            whole_spec((8, width)),
            ANY,
        ],
        out_shape=[
            jax.ShapeDtypeStruct((3, seq, width), bf16),
            jax.ShapeDtypeStruct((pairs, 8, seq), f32),
            jax.ShapeDtypeStruct((seq, width), bf16),
            jax.ShapeDtypeStruct((seq, width), f32),
            jax.ShapeDtypeStruct((seq, width), bf16),
            jax.ShapeDtypeStruct((seq, 128), f32),
            jax.ShapeDtypeStruct((16, seq), f32),
            jax.ShapeDtypeStruct((8, width), f32),
            jax.ShapeDtypeStruct(slots.shape, bf16),
        ],
        scratch_shapes=[pltpu.VMEM((seq, width), bf16)] + pair_sems(exps),
        compiler_params=params(("arbitrary",), collective_id=1, has_side_effects=True),
        cost_estimate=pl.CostEstimate(
            flops=30_000_000_000, bytes_accessed=20_000_000, transcendentals=12_000_000
        ),
        name="attention_forward",
    )(tokens, bid_row, bid_col, full, full, wr, slots)


def slots_of(place_row, cap):
    slot = lax.broadcasted_iota(jnp.int32, (cap, place_row.shape[1]), 0)
    return (slot == place_row).astype(f32).astype(bf16)


def dispatch_kernel(h2_ref, place_ref, probst_ref, rows_ref, chosen_ref):
    expert = pl.program_id(0)
    cap = rows_ref.shape[1]
    lanes = chosen_ref.shape[2]
    row = place_ref[pl.ds(expert, 1), :]
    rows_ref[0] = mm(slots_of(row, cap), h2_ref[...]).astype(bf16)
    value = probst_ref[pl.ds(expert, 1), :]
    high = value.astype(bf16)
    rest = value - high.astype(f32)
    middle = rest.astype(bf16)
    low = (rest - middle.astype(f32)).astype(bf16)
    spot = lax.broadcasted_iota(jnp.int32, (16, row.shape[1]), 0)
    pieces = jnp.where(
        spot == 0, high.astype(f32), jnp.where(spot == 1, middle.astype(f32), jnp.where(spot == 2, low.astype(f32), 0.0))
    )
    chosen = jnp.sum(mm_nt(pieces.astype(bf16), slots_of(row, lanes)), axis=0, keepdims=True)
    chosen_ref[0] = jnp.broadcast_to(chosen, chosen_ref.shape[1:])


def dispatch(h2, place_row, probst, experts_all, cap, lanes):
    seq, width = h2.shape
    return pl.pallas_call(
        dispatch_kernel,
        grid=(experts_all,),
        in_specs=[once(h2.shape), once(place_row.shape), once(probst.shape)],
        out_specs=[
            pl.BlockSpec((1, cap, width), lambda e: (e, 0, 0)),
            pl.BlockSpec((1, 8, lanes), lambda e: (e, 0, 0)),
        ],
        out_shape=[
            jax.ShapeDtypeStruct((experts_all, cap, width), bf16),
            jax.ShapeDtypeStruct((experts_all, 8, lanes), f32),
        ],
        compiler_params=params(("arbitrary",)),
        cost_estimate=pl.CostEstimate(
            flops=5_000_000_000, bytes_accessed=6_000_000, transcendentals=0
        ),
        name="dispatch",
    )(h2, place_row, probst)


def gated(x, g, wg, wu, wn):
    gate, up = mm(x, wg), mm(x, wu)
    hgrad = mm_nt(g, wn)
    sig = lax.logistic(gate)
    active = gate * sig
    slope = sig * (1.0 + gate * (1.0 - sig))
    hidden = (active * up).astype(bf16)
    return hidden, (hgrad * up * slope).astype(bf16), (hgrad * active).astype(bf16)


def routed_kernel(
    exps, shds,
    rows_ref, chosen_ref, grads_ref, packed_ref,
    eout_ref, gin_ref, sum_ref,
    x_s, g_s, c_s, w_s, n_s, hid_s, gg_s, ug_s, out_s, gin_s, wide_l, narrow_l,
    load_sem, x_send, x_recv, c_send, c_recv, o_send, o_recv, i_send, w_sem, s_send, s_recv,
):
    me = lax.axis_index("exp")
    _, cap, width = x_s.shape
    hidden = hid_s.shape[1]
    rows_all = exps * cap
    peers = [lax.bitwise_xor(me, k) for k in range(exps)]
    group = lax.axis_index("grp")
    core = lax.rem(group, 2)
    partner = {"grp": lax.bitwise_xor(group, 1)}
    greet([{"exp": peer} for peer in peers[1:]] + [partner])
    deep, tall = w_s.shape[2], n_s.shape[2]
    base = hidden // 256 * deep
    wide_at = lambda b: pl.ds(pl.multiple_of(b * deep, 16), deep)
    narrow_at = lambda b: pl.ds(base + b * tall, tall)
    lanes_at = lambda b: pl.ds(pl.multiple_of(256 * b, 256), 256)

    chosen, arriving = [], []
    for k in range(1, exps):
        target = {"exp": peers[k]}
        chosen.append(send(chosen_ref.at[peers[k]], c_s.at[k], c_send.at[k], c_recv.at[k], target))
        arriving.append(send(rows_ref.at[peers[k]], x_s.at[k], x_send.at[k], x_recv.at[k], target))
    for copy in chosen + arriving[:2]:
        copy.start()
    loads = [
        pltpu.make_async_copy(rows_ref.at[me], x_s.at[0], load_sem.at[0]),
        pltpu.make_async_copy(chosen_ref.at[me], c_s.at[0], load_sem.at[1]),
        pltpu.make_async_copy(grads_ref, g_s, load_sem.at[2]),
    ]
    for c in range(2):
        for b in range(hidden // 256):
            loads.append(
                pltpu.make_async_copy(
                    packed_ref.at[c, :, wide_at(b), :], w_s.at[c, :, :, lanes_at(b)], load_sem.at[len(loads)]
                )
            )
        for b in range(width // 256):
            loads.append(
                pltpu.make_async_copy(
                    packed_ref.at[c, :, narrow_at(b), :], n_s.at[:, c, :, lanes_at(b)], load_sem.at[len(loads)]
                )
            )
    for copy in loads:
        copy.start()
    for copy in loads:
        copy.wait()

    ft = 512
    returns, kept = [], []
    for k in range(exps):
        if k:
            chosen[k - 1].wait()
            arriving[k - 1].wait()
        scale = c_s[k].T[:cap, 0:1]
        g_s[k] = (g_s[k].astype(f32) * scale).astype(bf16)

        @pl.loop(0, hidden // ft)
        def _(f):
            columns = pl.ds(pl.multiple_of(f * ft, ft), ft)
            wg = w_s[0, :, :, columns].reshape(width, ft)
            wu = w_s[1, :, :, columns].reshape(width, ft)
            hid, gg, ug = gated(x_s[k], g_s[k], wg, wu, n_s[f].reshape(ft, width))
            hid_s[pl.ds(k * cap, cap), columns] = hid
            gg_s[pl.ds(k * cap, cap), columns] = gg
            ug_s[pl.ds(k * cap, cap), columns] = ug

        mine = pl.ds(k * cap, cap)
        if k >= 2:
            kept[k - 2].wait()
        for b in range(width // 256):
            part = slice(256 * b, 256 * b + 256)
            out_s[k, :, part] = mm(hid_s[mine, :], n_s[:, :, :, part].reshape(hidden, 256)).astype(bf16)
            wg = w_s[0].reshape(width, hidden)[part]
            wu = w_s[1].reshape(width, hidden)[part]
            gin_s[k % 2, :, part] = (mm_nt(gg_s[mine, :], wg) + mm_nt(ug_s[mine, :], wu)).astype(bf16)

        if k:
            back = send(
                out_s.at[k], eout_ref.at[me], o_send.at[k], o_recv.at[k], {"exp": peers[k]}
            )
        else:
            back = pltpu.make_async_copy(out_s.at[0], eout_ref.at[me], o_send.at[0])
            for copy in arriving[2:]:
                copy.start()
        kept.append(pltpu.make_async_copy(gin_s.at[k % 2], gin_ref.at[peers[k]], i_send.at[k]))
        for copy in (back, kept[k]):
            copy.start()
        returns.append(back)

    wide = hidden // shds
    per = wide // 256

    across = lambda f: pl.ds(pl.multiple_of(f * wide, wide), wide)

    def swaps(f):
        return [
            send(w_s.at[1 - core, :, :, across(f)], wide_l.at[f], s_send.at[f, 0], s_recv.at[f, 0], partner),
            send(n_s.at[f, 1 - core], narrow_l.at[f], s_send.at[f, 1], s_recv.at[f, 1], partner),
        ]

    def stores(f):
        made = []
        for b in range(per):
            block = per * f + b
            made.append((w_s.at[core, :, :, lanes_at(block)], sum_ref.at[:, wide_at(block), :]))
        for b in range(width // 256):
            made.append((n_s.at[f, core, :, lanes_at(b)], sum_ref.at[f, narrow_at(b), :]))
        return [pltpu.make_async_copy(a, b, w_sem.at[f, i]) for i, (a, b) in enumerate(made)]

    def add(f):
        for copy in swaps(f):
            copy.wait_recv()
        for z in range(shds):
            own = w_s[core, z, :, across(f)].astype(f32)
            w_s[core, z, :, across(f)] = (own + wide_l[f, z].astype(f32)).astype(bf16)
        n_s[f, core] = (n_s[f, core].astype(f32) + narrow_l[f].astype(f32)).astype(bf16)
        for copy in stores(f):
            copy.start()

    @pl.loop(0, shds)
    def _(f):
        columns = pl.ds(pl.multiple_of(f * wide, wide), wide)
        x = x_s[...].reshape(rows_all, width)
        g = g_s[...].reshape(rows_all, width)
        part = w_s.shape[1:3] + (wide,)
        w_s[0, :, :, columns] = mm_tn(x, gg_s[:, columns]).astype(bf16).reshape(part)
        w_s[1, :, :, columns] = mm_tn(x, ug_s[:, columns]).astype(bf16).reshape(part)
        n_s[f] = mm_tn(hid_s[:, columns], g).astype(bf16).reshape(n_s.shape[1:])
        for copy in swaps(f):
            copy.start()

        @pl.when(f > 0)
        def _():
            add(f - 1)

    add(shds - 1)
    for copy in returns + kept[-2:]:
        copy.wait()

    @pl.loop(0, shds)
    def _(f):
        for copy in swaps(f):
            copy.wait_send()
        for copy in stores(f):
            copy.wait()


def routed(slot_rows, chosen, grads, packed, hidden):
    exps, cap, width = slot_rows.shape
    shds, height = packed.shape[1:3]
    deep, tall = width // shds, hidden // shds // 2
    pieces = hidden // shds // 256 + width // 256
    big = lambda *shape: pltpu.VMEM(shape, bf16)
    sems = lambda *n: pltpu.SemaphoreType.DMA(n)
    return pl.pallas_call(
        functools.partial(routed_kernel, exps, shds),
        in_specs=[ANY] * 4,
        out_specs=[ANY] * 3,
        out_shape=[
            jax.ShapeDtypeStruct((exps, cap, width), bf16),
            jax.ShapeDtypeStruct((exps, cap, width), bf16),
            jax.ShapeDtypeStruct((shds, height, 256), bf16),
        ],
        scratch_shapes=[
            big(exps, cap, width),
            big(exps, cap, width),
            pltpu.VMEM(chosen.shape, f32),
            big(2, shds, deep, hidden),
            big(shds, 2, tall, width),
            big(exps * cap, hidden),
            big(exps * cap, hidden),
            big(exps * cap, hidden),
            big(exps, cap, width),
            big(2, cap, width),
            big(shds, shds, deep, hidden // shds),
            big(shds, tall, width),
            sems(3 + 2 * (hidden // 256 + width // 256)),
            sems(exps), sems(exps), sems(exps), sems(exps), sems(exps), sems(exps), sems(exps),
            sems(shds, pieces), sems(shds, 2), sems(shds, 2),
        ],
        compiler_params=params(collective_id=2, has_side_effects=True),
        cost_estimate=pl.CostEstimate(
            flops=18 * exps * cap * width * hidden,
            bytes_accessed=40_000_000,
            transcendentals=exps * cap * hidden,
        ),
        name="routed",
    )(slot_rows, chosen, grads, packed)


def ffn_kernel(
    x_ref, g_ref, wg_ref, wu_ref, wn_ref, back_ref,
    out_ref, gin_ref, part_a, part_b, ein_ref,
    acc_out, acc_gin, hid_s, gg_s, ug_s, wide_s, narrow_s, wide_l, narrow_l,
    own_sem, send_sem, recv_sem, b_send, b_recv,
    *, tile,
):
    f = pl.program_id(0)
    last = pl.num_programs(0) - 1
    rows_all, width = x_ref.shape
    group = lax.axis_index("grp")
    core = lax.rem(group, 2)
    partner = {"grp": lax.bitwise_xor(group, 1)}
    ft = wide_s.shape[3]
    shards, tall = narrow_s.shape[2:4]

    def swaps(step):
        return [
            send(a.at[step, b], c.at[step], send_sem.at[step, i], recv_sem.at[step, i], partner)
            for i, (a, b, c) in enumerate(
                [(wide_s, 1 - core, wide_l), (narrow_s, 1 - core, narrow_l)]
            )
        ]

    def stores(step):
        columns = pl.ds(pl.multiple_of(step * ft, ft), ft)
        at = pl.ds(step * shards, shards)
        return [
            pltpu.make_async_copy(wide_s.at[step, core], part_a.at[:, columns], own_sem.at[step, 0]),
            pltpu.make_async_copy(narrow_s.at[step, core], part_b.at[at], own_sem.at[step, 1]),
        ]

    def add(step):
        for copy in swaps(step):
            copy.wait_recv()
        wide_s[step, core] = (wide_s[step, core].astype(f32) + wide_l[step].astype(f32)).astype(bf16)
        narrow_s[step, core] = (narrow_s[step, core].astype(f32) + narrow_l[step].astype(f32)).astype(bf16)
        for copy in stores(step):
            copy.start()

    exps = back_ref.shape[0]
    columns = others("exp", exps)

    def returns():
        me = columns[0]
        made = [pltpu.make_async_copy(back_ref.at[me], ein_ref.at[me], b_send.at[0])]
        for k in range(1, exps):
            made.append(
                send(
                    back_ref.at[columns[k]], ein_ref.at[me],
                    b_send.at[k], b_recv.at[k], {"exp": columns[k]},
                )
            )
        return made

    @pl.when(f == 0)
    def _():
        greet([{"exp": column} for column in columns[1:]] + [partner])
        for copy in returns():
            copy.start()
        acc_out[...] = jnp.zeros_like(acc_out)
        acc_gin[...] = jnp.zeros_like(acc_gin)

    deep = wg_ref.shape[3] // 2
    order = [(z, e) for e in range(wg_ref.shape[2]) for z in range(wg_ref.shape[1])]

    def wide(ref):
        blocks = [
            jnp.concatenate([ref[0, z, e, deep * b : deep * (b + 1)] for z, e in order], axis=0)
            for b in range(2)
        ]
        return jnp.concatenate(blocks, axis=1)

    wg, wu = wide(wg_ref), wide(wu_ref)
    narrow = [
        jnp.concatenate([wn_ref[c, z, e, tall * b : tall * (b + 1)] for b in range(width // 256)], axis=1)
        for e in range(wn_ref.shape[2])
        for z in range(wn_ref.shape[1])
        for c in range(2)
    ]
    wn = jnp.concatenate(narrow, axis=0)
    for row in range(0, rows_all, tile):
        rows = pl.ds(row, tile)
        x, g = x_ref[rows, :], g_ref[rows, :]
        hidden, gg, ug = gated(x, g, wg, wu, wn)
        hid_s[rows, :], gg_s[rows, :], ug_s[rows, :] = hidden, gg, ug
        acc_out[rows, :] += mm(hidden, wn)
        acc_gin[rows, :] += mm_nt(gg, wg) + mm_nt(ug, wu)
    wide_s[f, 0] = mm_tn(x_ref[...], gg_s[...]).astype(bf16)
    wide_s[f, 1] = mm_tn(x_ref[...], ug_s[...]).astype(bf16)
    narrow = mm_tn(hid_s[...], g_ref[...]).astype(bf16).reshape(shards, 2, tall, width)
    for c in range(2):
        narrow_s[f, c] = narrow[:, c]
    for copy in swaps(f):
        copy.start()

    @pl.when(f > 0)
    def _():
        add(f - 1)

    @pl.when(f == last)
    def _():
        out_ref[...] = acc_out[...].astype(out_ref.dtype)
        gin_ref[...] = acc_gin[...].astype(gin_ref.dtype)

        add(last)

        @pl.loop(0, pl.num_programs(0))
        def _(step):
            for copy in swaps(step):
                copy.wait_send()
            for copy in stores(step):
                copy.wait()

        for copy in returns():
            copy.wait()


def ffn(x, g, packed, back, hidden, out_type, tile, name):
    rows, width = x.shape
    _, shds, exps, height, _ = packed.shape
    spread = shds * exps
    ft = 512
    steps = hidden // ft
    deep, tall = width // spread, hidden // spread // 2
    shards = spread // steps
    base = hidden // 256 * deep
    narrow_high = height - base
    sems = pltpu.SemaphoreType.DMA((steps, 2))
    return pl.pallas_call(
        functools.partial(ffn_kernel, tile=tile),
        grid=(steps,),
        in_specs=[
            once((rows, width)),
            once((rows, width)),
            pl.BlockSpec((1, shds, exps, 2 * deep, 256), lambda f: (0, 0, 0, f, 0)),
            pl.BlockSpec((1, shds, exps, 2 * deep, 256), lambda f: (1, 0, 0, f, 0)),
            pl.BlockSpec((2, shds, shards // shds, narrow_high, 256), lambda f: (0, 0, f, base // narrow_high, 0)),
            ANY,
        ],
        out_specs=[once((rows, width)), once((rows, width)), ANY, ANY, ANY],
        out_shape=[
            jax.ShapeDtypeStruct((rows, width), out_type),
            jax.ShapeDtypeStruct((rows, width), out_type),
            jax.ShapeDtypeStruct((width, hidden), bf16),
            jax.ShapeDtypeStruct((spread, tall, width), bf16),
            jax.ShapeDtypeStruct(back.shape, bf16),
        ],
        scratch_shapes=[
            pltpu.VMEM((rows, width), f32),
            pltpu.VMEM((rows, width), f32),
            pltpu.VMEM((rows, ft), bf16),
            pltpu.VMEM((rows, ft), bf16),
            pltpu.VMEM((rows, ft), bf16),
            pltpu.VMEM((steps, 2, width, ft), bf16),
            pltpu.VMEM((steps, 2, shards, tall, width), bf16),
            pltpu.VMEM((steps, width, ft), bf16),
            pltpu.VMEM((steps, shards, tall, width), bf16),
            sems, sems, sems,
        ]
        + pair_sems(back.shape[0]),
        compiler_params=params(("arbitrary",), collective_id=3, has_side_effects=True),
        cost_estimate=pl.CostEstimate(
            flops=18 * rows * width * hidden,
            bytes_accessed=12 * width * hidden + 8 * rows * width,
            transcendentals=rows * hidden,
        ),
        name=name,
    )(x, g, packed, packed, packed, back)


def plane_copies(exps, block_for, landed_ref, send_sem, recv_sem):
    columns = others("exp", exps)
    made = [pltpu.make_async_copy(block_for(columns[0]), landed_ref.at[0], send_sem.at[0])]
    for k in range(1, exps):
        made.append(
            send(
                block_for(columns[k]), landed_ref.at[k],
                send_sem.at[k], recv_sem.at[k], {"exp": columns[k]},
            )
        )
    return made


def combine_kernel(
    mid_ref, sout_ref, sin_ref, g_ref, h2_ref, probs_ref, place_ref, eout_ref, ein_ref,
    gains_ref, wr_ref, wo_ref, part_ref,
    block_ref, midg_ref, midb_ref, og_ref, gain_ref, rgrad_ref, landed_ref,
    send_sem, recv_sem,
):
    step = pl.program_id(0)
    exps = part_ref.shape[0]
    exchange = lambda: plane_copies(exps, lambda c: part_ref.at[c], landed_ref, send_sem, recv_sem)

    @pl.when(step == 0)
    def _():
        greet([{"exp": column} for column in others("exp", exps)[1:]])
        for copy in exchange():
            copy.start()

    tile, width = mid_ref.shape
    experts_all, cap = eout_ref.shape[0], eout_ref.shape[1]
    slot = lax.broadcasted_iota(jnp.int32, (tile, cap), 1)
    g = g_ref[...].astype(f32)
    probs = probs_ref[...]
    spot = lax.broadcasted_iota(jnp.int32, probs.shape, 1)
    mixture = jnp.zeros((tile, width), f32)
    moe_in = jnp.zeros((tile, width), f32)
    pgrad = jnp.zeros(probs.shape, f32)
    for e in range(experts_all):
        hot = (slot == place_ref[:, e : e + 1]).astype(f32).astype(bf16)
        pair_out = mm(hot, eout_ref[e])
        mixture += probs[:, e : e + 1] * pair_out
        grad = jnp.sum(g * pair_out, axis=1, keepdims=True)
        pgrad = jnp.where(spot == e, grad, pgrad)
        moe_in += mm(hot, ein_ref[e])
    mid = mid_ref[...]
    block_ref[...] = (mid + sout_ref[...] + mixture).astype(bf16)
    inner = jnp.sum(pgrad * probs, axis=1, keepdims=True)
    lgrad = (probs * (pgrad - inner)).astype(bf16)
    h2_grad = moe_in + mm_nt(lgrad, wr_ref[...]) + sin_ref[...]
    r2 = lax.rsqrt(jnp.mean(mid * mid, axis=1, keepdims=True) + norm_eps)
    n2 = mid * r2
    d2 = h2_grad * gains_ref[5:6, :]
    mid_grad = g + r2 * (d2 - n2 * jnp.mean(d2 * n2, axis=1, keepdims=True))
    midb = mid_grad.astype(bf16)
    midg_ref[...] = mid_grad
    midb_ref[...] = midb
    og_ref[...] = mm_nt(midb, wo_ref[0]).astype(bf16)
    gsum = jnp.sum(h2_grad * n2, axis=0, keepdims=True)
    rsum = mm_tn(lgrad, h2_ref[...])[:8]

    @pl.when(step == 0)
    def _():
        gain_ref[...] = jnp.zeros_like(gain_ref)
        rgrad_ref[...] = jnp.zeros_like(rgrad_ref)

    gain_ref[0:1, :] += gsum
    rgrad_ref[...] += rsum

    @pl.when(step == pl.num_programs(0) - 1)
    def _():
        for copy in exchange():
            copy.wait()


def combine(mid, sout, sin, g, h2, probs, place_col, eout, ein, gains, wr, full, part):
    seq, width = mid.shape
    tile = 256
    by_rows = pl.BlockSpec((tile, width), lambda i: (i, 0))
    lanes = pl.BlockSpec((tile, 128), lambda i: (i, 0))
    return pl.pallas_call(
        combine_kernel,
        grid=(seq // tile,),
        in_specs=[
            by_rows, by_rows, by_rows, by_rows, by_rows, lanes, lanes,
            once(eout.shape), once(ein.shape), once(gains.shape), once(wr.shape),
            pl.BlockSpec((1, width, width), lambda i: (3, 0, 0), pipeline_mode=pl.Buffered(1)),
            ANY,
        ],
        out_specs=[
            by_rows, by_rows, by_rows, by_rows, whole_spec((8, width)), whole_spec((8, width)), ANY,
        ],
        out_shape=[
            jax.ShapeDtypeStruct((seq, width), bf16),
            jax.ShapeDtypeStruct((seq, width), f32),
            jax.ShapeDtypeStruct((seq, width), bf16),
            jax.ShapeDtypeStruct((seq, width), bf16),
            jax.ShapeDtypeStruct((8, width), f32),
            jax.ShapeDtypeStruct((8, width), f32),
            jax.ShapeDtypeStruct(part.shape, bf16),
        ],
        scratch_shapes=pair_sems(part.shape[0]),
        compiler_params=params(("arbitrary",), collective_id=5, has_side_effects=True),
        cost_estimate=pl.CostEstimate(
            flops=11_000_000_000, bytes_accessed=30_000_000, transcendentals=0
        ),
        name="combine",
    )(mid, sout, sin, g, h2, probs, place_col, eout, ein, gains, wr, full, part)


def backward_kernel(
    exps, shds,
    qkv_ref, og_ref, lse_ref, bidr_ref, bidc_ref, tok_ref, midg_ref, o_ref, midb_ref, w_ref,
    gains_ref, gain2_ref, rgrad_ref, lb_ref, part_ref,
    igrad_ref, sw_ref, sa_ref, sb_ref, st_ref,
    dk_s, dv_s, h1t_s, ot_s, grad_s, stack_s, pair_s, plane_s, r_s, zr_s, fw_s,
    la_s, qa_s, qb_s, za_s, zb_s, fa_s, fb_s, tiny_s, tpair_s, tplane_s, tz_s,
    a_send, a_recv, pair_send, pair_recv, p_send, p_recv, r_send, r_recv, f_own, f_send, f_recv,
    line_send, line_recv, last_own, last_send, last_recv, t_send, t_recv, tp_send, tp_recv,
):
    step = pl.program_id(0)
    columns, layers = others("exp", exps), others("shd", shds)
    group = lax.axis_index("grp")
    core = lax.rem(group, 2)
    partner = {"grp": lax.bitwise_xor(group, 1)}
    seq, width = tok_ref.shape
    tile = 256
    pieces = width // 128
    deep = width // exps
    early = [(j + 1) % shds for j in range(shds)]

    def chunk(j):
        return plane_copies(
            exps, lambda c: part_ref.at[c, layers[j]], la_s.at[j], a_send.at[j], a_recv.at[j]
        )

    def chunk_line(j):
        return send(
            qa_s.at[j], za_s.at[j], line_send.at[0, j], line_recv.at[0, j], {"shd": layers[j]}
        )

    def chunk_sum(j, landed):
        value = landed[0].astype(f32)
        for k in range(1, exps):
            value = value + landed[k].astype(f32)
        qa_s[j] = value.astype(bf16)
        if j:
            chunk_line(j).start()

    def line(part_s, landed_s, kind):
        return [
            send(
                part_s.at[layers[k]], landed_s.at[k],
                line_send.at[kind, k], line_recv.at[kind, k], {"shd": layers[k]},
            )
            for k in range(1, shds)
        ]

    def plane_rows(k):
        return pl.ds(pl.multiple_of(columns[k] * deep, 16), deep)

    def pair_copy(p):
        return send(stack_s.at[p], pair_s.at[p // 2], pair_send.at[p // 2], pair_recv.at[p // 2], partner)

    def plane_copy(p):
        return [
            send(
                stack_s.at[p, :, plane_rows(k), :], plane_s.at[p // 2, k],
                p_send.at[p // 2, k], p_recv.at[p // 2, k], {"exp": columns[k]},
            )
            for k in range(1, exps)
        ]

    def line_copy(p):
        return [
            send(
                r_s.at[p // 2, layers[k]], zr_s.at[p // 2, k],
                r_send.at[p // 2, k], r_recv.at[p // 2, k], {"shd": layers[k]},
            )
            for k in range(1, shds)
        ]

    def final_copy(p):
        at = sw_ref.at[:, :, pl.ds(pl.multiple_of(p * 128, 128), 128)]
        return [
            pltpu.make_async_copy(fw_s.at[p // 2], at, f_own.at[p // 2]),
            send(fw_s.at[p // 2], at, f_send.at[p // 2], f_recv.at[p // 2], partner),
        ]

    def start(copies):
        for copy in copies:
            copy.start()

    def summing(p):
        return jnp.logical_and(p >= 0, core == p % 2)

    def to_pair(p):
        @pl.when(core != p % 2)
        def _():
            pair_copy(p).start()

    def to_plane(p):
        @pl.when(summing(p))
        def _():
            pair_copy(p).wait_recv()
            for i in range(4):
                stack_s[p, i] = (stack_s[p, i].astype(f32) + pair_s[p // 2, i].astype(f32)).astype(bf16)
            start(plane_copy(p))

    def to_line(p):
        @pl.when(summing(p))
        def _():
            for copy in plane_copy(p):
                copy.wait_recv()
            for i in range(4):
                value = stack_s[p, i, plane_rows(0), :].astype(f32)
                for k in range(1, exps):
                    value = value + plane_s[p // 2, k, i].astype(f32)
                r_s[p // 2, :, i] = value.astype(bf16).reshape(shds, deep // shds, 128)
            start(line_copy(p))

    def to_final(p):
        @pl.when(summing(p))
        def _():
            for copy in line_copy(p):
                copy.wait_recv()
            value = r_s[p // 2, layers[0]].astype(f32)
            for k in range(1, shds):
                value = value + zr_s[p // 2, k].astype(f32)
            fw_s[p // 2] = value
            start(final_copy(p))

    def line_total(landed_s, part_s):
        value = part_s[layers[0]].astype(f32)
        for k in range(1, shds):
            value = value + landed_s[k].astype(f32)
        return value

    def finals(kind, part_s, out_ref):
        return [
            pltpu.make_async_copy(part_s, out_ref.at[core], last_own.at[kind]),
            send(part_s, out_ref.at[core], last_send.at[kind], last_recv.at[kind], partner),
        ]

    @pl.when(step == 0)
    def _():
        greet(
            [{"shd": layer} for layer in layers[1:]]
            + [{"exp": column} for column in columns[1:]]
            + [partner]
        )
        for z in range(shds):
            qb_s[z] = sum([lb_ref[k, z].astype(f32) for k in range(1, exps)], lb_ref[0, z].astype(f32)).astype(bf16)
        start(line(qb_s, zb_s, 1))
        for row in range(0, seq, tile):
            x = tok_ref[row : row + tile, :].astype(f32)
            r1 = lax.rsqrt(jnp.mean(x * x, axis=1, keepdims=True) + norm_eps)
            h1t_s[:, row : row + tile] = (x * r1 * gains_ref[4:5, :]).astype(bf16).T
            ot_s[:, row : row + tile] = o_ref[row : row + tile, :].T
        grad_s[...] = jnp.zeros_like(grad_s)

    for turn, j in enumerate(early):

        @pl.when(step == turn)
        def _():
            start(chunk(j))

        @pl.when(step == turn + 2)
        def _():
            for copy in chunk(j):
                copy.wait()
            chunk_sum(j, la_s.at[j])

    @pl.when(step == shds)
    def _():
        for copy in line(qb_s, zb_s, 1):
            copy.wait()
        fb_s[...] = line_total(zb_s, qb_s)
        start(finals(1, fb_s, sb_ref))

    qs = qkv_ref[0] * jnp.asarray(0.125, bf16)
    k = qkv_ref[1]
    v = qkv_ref[2]
    kt = k.T
    og = og_ref[...]
    lane = lax.broadcasted_iota(jnp.int32, (tile, 128), 1)
    dk_s[...] = jnp.zeros_like(dk_s)
    dv_s[...] = jnp.zeros_like(dv_s)
    dqs = []
    for q0 in range(0, seq, tile):
        kl = min(seq, q0 + 2 * tile)
        qt, ot = qs[q0 : q0 + tile], og[q0 : q0 + tile]
        allowed = bidc_ref[q0:kl, :] <= bidr_ref[0:1, q0 : q0 + tile]
        parts = []
        for head in range(2):
            own = (lane // 64) == head
            qm = jnp.where(own, qt, jnp.zeros_like(qt))
            om = jnp.where(own, ot, jnp.zeros_like(ot))
            lse = lse_ref[0, head : head + 1, q0 : q0 + tile]
            spans = ([(0, q0)] if q0 else []) + [(q0, kl)]
            kept = []
            delta = jnp.zeros((1, tile), f32)
            for low, high in spans:
                s = mm_nt(k[low:high], qm)
                if low == q0:
                    s = jnp.where(allowed, s, masked_score)
                p = jnp.exp(s - lse)
                dp = mm_nt(v[low:high], om)
                delta = delta + jnp.sum(p * dp, axis=0, keepdims=True)
                kept.append((low, high, p, dp))
            dq = jnp.zeros((64, tile), f32)
            for low, high, p, dp in kept:
                ds = (p * (dp - delta)).astype(bf16)
                dv_s[low:high, :] += mm(p.astype(bf16), om)
                dk_s[low:high, :] += mm(ds, qm)
                dq = dq + mm(kt[64 * head : 64 * head + 64, low:high], ds)
            parts.append(dq)
        dqs.append((jnp.concatenate(parts, axis=0).T * 0.125).astype(bf16))
        if q0 == tile:
            to_plane(step - 1)
    dqkv = [jnp.concatenate(dqs, axis=0), dk_s[...].astype(bf16), dv_s[...].astype(bf16)]
    to_final(step - 4)
    to_line(step - 3)
    wide = mm(h1t_s[...], jnp.concatenate(dqkv, axis=1)).astype(bf16)
    for i in range(3):
        stack_s[step, i] = wide[:, 128 * i : 128 * i + 128]
    stack_s[step, 3] = mm(ot_s[...], midb_ref[...]).astype(bf16)
    to_pair(step)
    for row in range(0, seq, tile):
        rows = slice(row, row + tile)
        grad_s[rows, :] += (
            mm_nt(dqkv[0][rows], w_ref[0]) + mm_nt(dqkv[1][rows], w_ref[1]) + mm_nt(dqkv[2][rows], w_ref[2])
        )

    @pl.when(step == pieces - 1)
    def _():
        to_line(pieces - 3)
        to_final(pieces - 4)
        to_plane(pieces - 1)
        gain = jnp.zeros((1, width), f32)
        for row in range(0, seq, tile):
            rows = slice(row, row + tile)
            x = tok_ref[rows, :].astype(f32)
            r1 = lax.rsqrt(jnp.mean(x * x, axis=1, keepdims=True) + norm_eps)
            n1 = x * r1
            grad = grad_s[rows, :]
            gain = gain + jnp.sum(grad * n1, axis=0, keepdims=True)
            d1 = grad * gains_ref[4:5, :]
            igrad_ref[rows, :] = midg_ref[rows, :] + r1 * (d1 - n1 * jnp.mean(d1 * n1, axis=1, keepdims=True))
        spot = lax.broadcasted_iota(jnp.int32, (8, width), 0)
        small = jnp.where(spot < 4, rgrad_ref[...], jnp.where(spot == 4, gain, gain2_ref[0:1, :]))
        tiny_s[...] = small
        tswap = send(tiny_s, tpair_s, t_send, t_recv, partner)
        tswap.start()
        to_line(pieces - 2)
        to_final(pieces - 3)
        to_line(pieces - 1)
        tswap.wait()
        tpair_s[...] += tiny_s[...]
        tplane = [
            send(tpair_s, tplane_s.at[k], tp_send.at[k], tp_recv.at[k], {"exp": columns[k]})
            for k in range(1, exps)
        ]
        start(tplane)
        to_final(pieces - 2)
        for copy in tplane:
            copy.wait()
        value = qa_s[0].astype(f32)
        for j in range(1, shds):
            chunk_line(j).wait()
            value = value + za_s[j].astype(f32)
        fa_s[...] = value
        start(finals(0, fa_s, sa_ref))
        tz_s[0] = sum([tplane_s[k] for k in range(1, exps)], tpair_s[...])
        tline = [
            send(
                tz_s.at[0], tz_s.at[k], line_send.at[2, k], line_recv.at[2, k], {"shd": layers[k]}
            )
            for k in range(1, shds)
        ]
        start(tline)
        to_final(pieces - 1)
        for copy in tline:
            copy.wait()
        st_ref[...] = sum([tz_s[k] for k in range(1, shds)], tz_s[0])
        for p in range(pieces):

            @pl.when(core == p % 2)
            def _():
                for copy in plane_copy(p) + line_copy(p) + final_copy(p)[1:]:
                    copy.wait_send()
                final_copy(p)[0].wait()

            @pl.when(core != p % 2)
            def _():
                pair_copy(p).wait_send()
                final_copy(p)[1].wait_recv()

        for copy in finals(1, fb_s, sb_ref) + finals(0, fa_s, sa_ref):
            copy.wait()


def attention_backward(qkv, og, lse, bid_row, bid_col, tokens, midg, o, midb, full, gains, gain2, rgrad, lb, part):
    exps, shds = part.shape[:2]
    seq, width = tokens.shape
    rows = part.shape[2]
    pairs = width // 128
    half = pairs // 2
    big = lambda *shape: pltpu.VMEM(shape, bf16)
    wide = lambda *shape: pltpu.VMEM(shape, f32)
    sems = lambda *n: pltpu.SemaphoreType.DMA(n)
    a, b = part.shape[2:], lb.shape[2:]
    return pl.pallas_call(
        functools.partial(backward_kernel, exps, shds),
        grid=(pairs,),
        in_specs=[
            pl.BlockSpec((3, seq, 128), lambda i: (0, 0, i)),
            pl.BlockSpec((seq, 128), lambda i: (0, i)),
            pl.BlockSpec((1, 8, seq), lambda i: (i, 0, 0)),
            once(bid_row.shape),
            once(bid_col.shape),
            once(tokens.shape),
            once(midg.shape),
            once(o.shape),
            pl.BlockSpec((seq, 128), lambda i: (0, i)),
            pl.BlockSpec((3, width, 128), lambda i: (0, 0, i)),
            once(gains.shape),
            once(gain2.shape),
            once(rgrad.shape),
            once(lb.shape),
            ANY,
        ],
        out_specs=[once((seq, width)), ANY, ANY, ANY, once((8, width))],
        out_shape=[
            jax.ShapeDtypeStruct((seq, width), f32),
            jax.ShapeDtypeStruct((4, rows, width), f32),
            jax.ShapeDtypeStruct((2,) + a, f32),
            jax.ShapeDtypeStruct((2,) + b, f32),
            jax.ShapeDtypeStruct((8, width), f32),
        ],
        scratch_shapes=[
            wide(seq, 128),
            wide(seq, 128),
            big(width, seq),
            big(width, seq),
            wide(seq, width),
            big(pairs, 4, width, 128),
            big(half, 4, width, 128),
            big(half, exps, 4, width // exps, 128),
            big(half, shds, 4, rows, 128),
            big(half, shds, 4, rows, 128),
            wide(half, 4, rows, 128),
            big(shds, exps, *a),
            big(shds, *a),
            big(shds, *b),
            big(shds, *a),
            big(shds, *b),
            wide(*a),
            wide(*b),
            wide(8, width),
            wide(8, width),
            wide(exps, 8, width),
            wide(shds, 8, width),
            sems(shds, exps), sems(shds, exps), sems(half), sems(half),
            sems(half, exps), sems(half, exps), sems(half, shds), sems(half, shds),
            sems(half), sems(half), sems(half),
            sems(3, shds), sems(3, shds), sems(2), sems(2), sems(2),
            pltpu.SemaphoreType.DMA, pltpu.SemaphoreType.DMA, sems(exps), sems(exps),
        ],
        compiler_params=params(("arbitrary",), collective_id=6, has_side_effects=True),
        cost_estimate=pl.CostEstimate(
            flops=80_000_000_000, bytes_accessed=30_000_000, transcendentals=12_000_000
        ),
        name="attention_backward",
    )(
        qkv, og, lse, bid_row, bid_col, tokens, midg, o, midb, full,
        gains, gain2, rgrad, lb, part,
    )


def adam_update(weight, moment, square, gradient, step_rate, shrink_rate):
    moment_next = beta_one * moment + (1.0 - beta_one) * gradient
    square_next = beta_two * square + (1.0 - beta_two) * gradient * gradient
    direction = moment_next / first_fix / (jnp.sqrt(square_next / second_fix) + adam_eps)
    return (weight - step_rate * (direction + shrink_rate * weight), moment_next, square_next)


def adam_kernel(rates, core_ref, w_ref, m_ref, v_ref, own_ref, other_ref, wo_ref, mo_ref, vo_ref):
    shape = w_ref.shape
    high = shape[-2]
    mine = jnp.full(own_ref.shape, core_ref[0], jnp.int32) == pl.program_id(0)
    gradient = jnp.where(mine, own_ref[...].astype(f32), other_ref[...].astype(f32))
    parts = [gradient[i : i + high] for i in range(0, gradient.shape[0], high)]
    gradient = jnp.concatenate(parts, axis=1).reshape(shape)
    wo_ref[...], mo_ref[...], vo_ref[...] = adam_update(
        w_ref[...], m_ref[...], v_ref[...], gradient, *rates
    )


def adam_blocks(kind, state, sums, core, grid, spec, sums_spec):
    return pl.pallas_call(
        functools.partial(adam_kernel, (learning_rates[kind], decay_rates[kind])),
        grid=grid,
        in_specs=[pl.BlockSpec(memory_space=pltpu.SMEM)] + [spec] * 3 + [sums_spec] * 2,
        out_specs=[spec] * 3,
        out_shape=[jax.ShapeDtypeStruct(state[0].shape, f32)] * 3,
        compiler_params=params(("arbitrary",) * len(grid)),
        cost_estimate=pl.CostEstimate(
            flops=20 * state[0].size, bytes_accessed=26 * state[0].size, transcendentals=0
        ),
        name="adam_blocks",
    )(core.reshape(1), *state, *sums)


def pick(array, axis, index):
    return lax.dynamic_index_in_dim(array, index, axis, keepdims=False)


def share(part, groups, core):
    if groups > 2:
        both = jnp.zeros((2,) + part.shape, f32)
        both = lax.dynamic_update_index_in_dim(both, part.astype(f32), core, 0)
        both = lax.psum(both, "grp")
        return pick(both, 0, core), pick(both, 0, 1 - core)
    return part, lax.ppermute(part, "grp", [(i, i ^ 1) for i in range(groups)])


def on_device(
    tokens_in, cotangent, block_ids, expert_ids,
    scales, moment_scales, square_scales, attend, moment_attend, square_attend,
    output, moment_output, square_output, router, moment_router, square_router,
    widener, moment_widener, square_widener, reducer, moment_reducer, square_reducer,
    experts, moment_experts, square_experts, narrower, moment_narrower, square_narrower,
):
    groups, exps, shds = (lax.axis_size(a) for a in ("grp", "exp", "shd"))
    spread = exps * shds
    core = lax.rem(lax.axis_index("grp"), 2)
    _, seq, width = tokens_in.shape
    hidden = reducer.shape[0] * spread
    experts_all = exps * experts.shape[0]
    rows, tall = output.shape[0], reducer.shape[0] // 2
    deep = width // shds
    tokens, g = tokens_in.reshape(seq, width), cotangent.reshape(seq, width)

    def packed(wide, narrow):
        wide = pick(wide.astype(bf16), 0, core)
        narrow = pick(narrow.astype(bf16).reshape(2, -1, width), 0, core)
        blocks = [
            a.reshape(a.shape[0], -1, 256).transpose(1, 0, 2).reshape(-1, 256) for a in (wide, narrow)
        ]
        return jnp.concatenate(blocks, axis=0)

    def gather(part, axes):
        wide = lax.all_gather(part, ("grp",) + axes, axis=0, tiled=False)
        return wide.reshape((groups, -1) + part.shape)[:2]

    mine = jnp.where(
        core == 0,
        attend[:2].astype(bf16),
        jnp.stack([attend[2].astype(bf16), output.astype(bf16)]),
    )
    tiny = jnp.concatenate([router, scales.T], axis=1).astype(bf16)
    tiny = jnp.pad(tiny, ((0, 0), (0, 128 - tiny.shape[1])))
    expert_weights = gather(packed(experts[0], narrower[0]), ("shd",))
    shared_pack = packed(widener, reducer)

    ids = jnp.pad(expert_ids.reshape(seq, 2).T, ((0, 6), (0, 0)), constant_values=-1)
    bid = block_ids.reshape(1, seq)
    bid_row = jnp.broadcast_to(bid, (8, seq))
    bid_col = jnp.broadcast_to(bid.reshape(seq, 1), (seq, 256))

    lanes = -(-CAP // 128) * 128
    full, wr, packs, g_slots, place_row, place_col = gather_first(
        mine, tiny, shared_pack, g, ids, exps, shds, experts_all, CAP
    )
    qkv, lse, o, mid, h2, probs, probst, gains, g_landed = attention_forward(
        tokens, bid_row, bid_col, full, wr, g_slots
    )
    shared_weights = gather(packs, ("shd",)).reshape((2, shds) + packs.shape)
    slot_rows, chosen = dispatch(h2, place_row, probst, experts_all, CAP, lanes)
    eout, back, part = routed(slot_rows, chosen, g_landed, expert_weights, hidden)
    part = lax.psum_scatter(part, "shd", scatter_dimension=0, tiled=False)
    sout, sin, part_a, part_b, ein = ffn(
        h2, g, shared_weights, back, hidden, f32, 256, "shared"
    )
    part_a = part_a.reshape(exps, shds, rows, hidden)
    part_b = part_b.reshape(exps, shds, tall, width)
    block_out, mid_grad, midb, og, gain_two, rgrad, landed_b = combine(
        mid, sout, sin, g, h2, probs, place_col, eout, ein, gains, wr, full, part_b
    )
    input_grad, sum_w, sum_a, sum_b, sum_t = attention_backward(
        qkv, og, lse, bid_row, bid_col, tokens, mid_grad, o, midb, full,
        gains, gain_two, rgrad, landed_b, part_a,
    )
    if groups > 2:
        sum_w, sum_a, sum_b, sum_t = (
            0.5 * lax.psum(v, "grp") for v in (sum_w, sum_a, sum_b, sum_t)
        )
    expert_sums = share(part, groups, core)
    wide_state = [v[0] for v in (experts, moment_experts, square_experts)]
    new_experts = adam_blocks(
        6, wide_state, expert_sums, core, (2, hidden // 512),
        pl.BlockSpec((1, deep, 512), lambda c, b: (c, 0, b)),
        pl.BlockSpec((2 * deep, 256), lambda c, b: (b, 0)),
    )
    narrow_state = [v[0] for v in (narrower, moment_narrower, square_narrower)]
    high = narrower.shape[1] // 2
    across = width // 256
    skip = hidden // 256 * deep // (across * high)
    new_narrower = adam_blocks(
        7, narrow_state, expert_sums, core, (2, 1),
        pl.BlockSpec((high, width), lambda c, b: (c, b)),
        pl.BlockSpec((across * high, 256), lambda c, b: (skip + b, 0)),
    )
    shard = lax.axis_index("exp") * shds + lax.axis_index("shd")
    sum_t = lax.dynamic_slice_in_dim(sum_t, shard * rows, rows, 1)
    grads = (
        sum_t[4:6],
        sum_w[:3],
        sum_w[3],
        sum_t[:experts_all].T,
        sum_a,
        sum_b.reshape(reducer.shape),
    )
    masters = (scales, attend, output, router, widener, reducer)
    moments = (
        moment_scales, moment_attend, moment_output, moment_router,
        moment_widener, moment_reducer,
    )
    squares = (
        square_scales, square_attend, square_output, square_router,
        square_widener, square_reducer,
    )
    results = [block_out.reshape(tokens_in.shape), input_grad.reshape(tokens_in.shape)]
    for kind in range(6):
        results.extend(
            adam_update(
                masters[kind], moments[kind], squares[kind], grads[kind],
                learning_rates[kind], decay_rates[kind],
            )
        )
    results.extend(v[None] for v in new_experts)
    results.extend(v[None] for v in new_narrower)
    return tuple(results)


def solution(mesh):
    tokens = P(("grp", "exp", "shd"), None, None)
    both = ("exp", "shd")
    kinds = (
        P(None, both), P(None, both, None), P(both, None), P(both, None),
        P(None, both, None), P(both, None), P("exp", None, "shd", None), P("exp", "shd", None),
    )
    thrice = tuple(kind for kind in kinds for _ in range(3))
    return jax.shard_map(
        on_device,
        mesh=mesh,
        in_specs=(tokens, tokens, P(("grp", "exp", "shd"), None), tokens) + thrice,
        out_specs=(tokens, tokens) + thrice,
        check_vma=False,
    )
```

```python
import functools

import jax
import jax.numpy as jnp
from jax import lax
from jax.experimental import pallas as pl
from jax.experimental.pallas import tpu as pltpu
from jax.sharding import PartitionSpec as P

HEADS = 12
CAP = 576
VMEM_LIMIT = 60 * 1024 * 1024

norm_eps = 1e-06
adam_eps = 1e-08
beta_one = 0.9
beta_two = 0.95
first_fix = 1.0 - 0.9**10
second_fix = 1.0 - 0.95**10
learning_rates = (0.3, 0.02, 0.15, 0.02, 0.02, 0.012, 0.02, 0.012)
decay_rates = (0.0, 0.1, 0.1, 0.1, 0.1, 0.1, 0.1, 0.1)
masked_score = -1e30
bf16 = jnp.bfloat16
f32 = jnp.float32


def mm(a, b):
    return jnp.dot(a, b, preferred_element_type=f32)


def mm_nt(a, b):
    return lax.dot_general(a, b, (((1,), (1,)), ((), ())), preferred_element_type=f32)


def mm_tn(a, b):
    return lax.dot_general(a, b, (((0,), (0,)), ((), ())), preferred_element_type=f32)


def params(semantics=None, **more):
    return pltpu.CompilerParams(
        dimension_semantics=semantics, vmem_limit_bytes=VMEM_LIMIT, **more
    )


def whole_spec(shape, **more):
    zeros = (0,) * len(shape)
    return pl.BlockSpec(shape, lambda *_: zeros, **more)


def once(shape):
    return whole_spec(shape, pipeline_mode=pl.Buffered(1))


MESH = pl.DeviceIdType.MESH
ANY = pl.BlockSpec(memory_space=pl.ANY)


def greet(targets):
    barrier = pltpu.get_barrier_semaphore()
    for target in targets:
        pl.semaphore_signal(barrier, inc=1, device_id=target, device_id_type=MESH)
    pl.semaphore_wait(barrier, len(targets))


def send(src, dst, send_sem, recv_sem, target):
    return pltpu.make_async_remote_copy(
        src_ref=src, dst_ref=dst, send_sem=send_sem, recv_sem=recv_sem,
        device_id=target, device_id_type=MESH,
    )


def pair_sems(count):
    return [pltpu.SemaphoreType.DMA((count,)), pltpu.SemaphoreType.DMA((count,))]


def others(axis, count):
    me = lax.axis_index(axis)
    return [lax.bitwise_xor(me, k) for k in range(count)]


def gather_kernel(
    exps, shds,
    mine_ref, tiny_ref, pack_ref, g_ref, ids_ref, bid_ref,
    full_ref, every_ref, packs_ref, slots_ref, row_ref, col_ref, bidc_ref,
    own_sem, z_send, z_recv, p_send, p_recv, c_send, c_recv, k_send, k_recv,
):
    columns, layers = others("exp", exps), others("shd", shds)
    group = lax.axis_index("grp")
    core = lax.rem(group, 2)
    partner = {"grp": lax.bitwise_xor(group, 1)}
    rows = mine_ref.shape[1]
    relay = exps == 4
    direct = range(1, 3 if relay else exps)

    def spots(kz, kx):
        at = pl.ds(pl.multiple_of((columns[kx] * shds + layers[kz]) * rows, 16), rows)
        return full_ref.at[pl.ds(2 * core, 2), at, :], every_ref.at[at, :]

    greet(
        [{"shd": layer} for layer in layers[1:]]
        + [{"exp": column} for column in columns[1:]]
        + [partner]
    )
    started = []

    def begin(copies):
        for copy in copies:
            copy.start()
        started.extend(copies)
        return copies

    def both(sources, kz, kx, sem, far, index, target):
        return [
            send(a, b, sem.at[index + (i,)], far.at[index + (i,)], target)
            for i, (a, b) in enumerate(zip(sources, spots(kz, kx)))
        ]

    mine = (mine_ref, tiny_ref)
    local = [
        pltpu.make_async_copy(a, b, own_sem.at[i])
        for i, (a, b) in enumerate(zip(mine, spots(0, 0)))
    ]
    for copy in local:
        copy.start()
    down = [both(mine, 0, 0, z_send, z_recv, (k,), {"shd": layers[k]}) for k in range(1, shds)]
    for copies in down:
        begin(copies)
    across = {}
    for kx in direct:
        across[0, kx] = begin(both(mine, 0, 0, p_send, p_recv, (0, kx), {"exp": columns[kx]}))
    packs = [pltpu.make_async_copy(pack_ref, packs_ref.at[columns[0]], k_send.at[0])]
    for kx in direct:
        packs.append(
            send(pack_ref, packs_ref.at[columns[0]], k_send.at[kx], k_recv.at[kx], {"exp": columns[kx]})
        )
    for copy in packs:
        copy.start()
    swaps = [send(mine_ref, spots(0, 0)[0], c_send.at[0, 0], c_recv.at[0, 0], partner)]
    swaps[0].start()
    seq = g_ref.shape[0]
    blocks = bid_ref[...].astype(f32).T[:, 0:1]
    bidc_ref[...] = jnp.broadcast_to(blocks, bidc_ref.shape).astype(jnp.int32)
    expert = lax.broadcasted_iota(jnp.int32, (16, seq), 0)
    named = (ids_ref[0:1, :] == expert) | (ids_ref[1:2, :] == expert)
    earlier = lax.broadcasted_iota(jnp.int32, (seq, seq), 0) < lax.broadcasted_iota(jnp.int32, (seq, seq), 1)
    count = mm(named.astype(f32).astype(bf16), earlier.astype(f32).astype(bf16))
    place = jnp.where(named, count, -1.0)
    row_ref[...] = place.astype(jnp.int32)
    col_ref[...] = jnp.concatenate([place, jnp.full((112, seq), -1.0, f32)], axis=0).T.astype(jnp.int32)

    def fill(e):
        hot = slots_of(row_ref[e : e + 1, :], slots_ref.shape[1])
        slots_ref[e] = mm(hot, g_ref[...]).astype(bf16)

    def swap(kz, kx):
        here = spots(kz, kx)[0]
        copy = send(here, here, c_send.at[kz, kx], c_recv.at[kz, kx], partner)
        copy.start()
        swaps.append(copy)

    for kz in range(1, shds):
        for copy in down[kz - 1]:
            copy.wait_recv()
        for kx in direct:
            across[kz, kx] = begin(both(spots(kz, 0), kz, 0, p_send, p_recv, (kz, kx), {"exp": columns[kx]}))
        swap(kz, 0)
        if kz <= slots_ref.shape[0]:
            fill(kz - 1)
    for e in range(shds - 1, slots_ref.shape[0]):
        fill(e)
    if relay:
        half = pack_ref.shape[0] // 2
        for kx in direct:
            packs[kx].wait_recv()
            spot = packs_ref.at[columns[kx], pl.ds(half * (kx - 1), half), :]
            copy = send(spot, spot, k_send.at[2 + kx], k_recv.at[2 + kx], {"exp": columns[3 - kx]})
            copy.start()
            packs.append(copy)
    for kz in range(shds):
        via = 1 + kz % 2
        for kx in direct:
            for copy in across[kz, kx]:
                copy.wait_recv()
            if relay and kx == via:
                across[kz, 3] = begin(
                    both(spots(kz, kx), kz, kx, p_send, p_recv, (kz, 3), {"exp": columns[3 - via]})
                )
            swap(kz, kx)
    if relay:
        for kz in range(shds):
            for copy in across[kz, 3]:
                copy.wait_recv()
            swap(kz, 3)
    for copy in started:
        copy.wait_send()
    if relay:
        for kx in direct:
            packs[kx].wait_send()
        packs = packs[:1] + packs[3:]
    for copy in swaps + local + packs:
        copy.wait()


def gather_first(mine, tiny, pack, g, ids, bids, exps, shds, experts_all, cap):
    _, rows, width = mine.shape
    tall = exps * shds * rows
    sems = lambda *shape: pltpu.SemaphoreType.DMA(shape)
    return pl.pallas_call(
        functools.partial(gather_kernel, exps, shds),
        in_specs=[ANY, ANY, ANY] + [pl.BlockSpec(memory_space=pltpu.VMEM)] * 3,
        out_specs=[ANY, ANY, ANY] + [pl.BlockSpec(memory_space=pltpu.VMEM)] * 4,
        out_shape=[
            jax.ShapeDtypeStruct((4, tall, width), bf16),
            jax.ShapeDtypeStruct((tall, 128), bf16),
            jax.ShapeDtypeStruct((exps,) + pack.shape, bf16),
            jax.ShapeDtypeStruct((experts_all, cap, width), bf16),
            jax.ShapeDtypeStruct((16, g.shape[0]), jnp.int32),
            jax.ShapeDtypeStruct((g.shape[0], 128), jnp.int32),
            jax.ShapeDtypeStruct((g.shape[0], 256), jnp.int32),
        ],
        scratch_shapes=[
            sems(2), sems(shds, 2), sems(shds, 2), sems(shds, exps, 2), sems(shds, exps, 2),
            sems(shds, exps), sems(shds, exps), sems(exps + 1), sems(exps + 1),
        ],
        compiler_params=params(collective_id=4, has_side_effects=True),
        cost_estimate=pl.CostEstimate(
            flops=40_000_000_000, bytes_accessed=10_000_000, transcendentals=0
        ),
        name="gather_first",
    )(mine, tiny, pack, g, ids, bids)


def forward_kernel(
    exps,
    tok_ref, bidr_ref, bidc_ref, wa_ref, wo_ref, wr_ref, slots_ref,
    qkv_ref, lse_ref, o_ref, mid_ref, h2_ref, probs_ref, probst_ref, gains_ref, landed_ref, h1_ref,
    send_sem, recv_sem,
):
    pair = pl.program_id(0)
    me = lax.axis_index("exp")

    def copies():
        made = [pltpu.make_async_copy(slots_ref.at[me], landed_ref.at[0], send_sem.at[0])]
        for k in range(1, exps):
            peer = lax.bitwise_xor(me, k)
            made.append(
                send(slots_ref.at[peer], landed_ref.at[k], send_sem.at[k], recv_sem.at[k], {"exp": peer})
            )
        return made

    @pl.when(pair == 0)
    def _():
        greet([{"exp": lax.bitwise_xor(me, k)} for k in range(1, exps)])
        for copy in copies():
            copy.start()
    seq, width = tok_ref.shape
    tile = 256

    @pl.when(pair == 0)
    def _():
        gains_ref[...] = wr_ref[...].astype(f32).T[:8]
        for row in range(0, seq, tile):
            x = tok_ref[pl.ds(row, tile), :].astype(f32)
            r1 = lax.rsqrt(jnp.mean(x * x, axis=1, keepdims=True) + norm_eps)
            h1_ref[pl.ds(row, tile), :] = (x * r1 * gains_ref[4:5, :]).astype(bf16)

    h1 = h1_ref[...]
    for i in range(3):
        qkv_ref[i] = mm(h1, wa_ref[i]).astype(bf16)
    qs = qkv_ref[0] * jnp.asarray(0.125, bf16)
    k = qkv_ref[1]
    vt = qkv_ref[2].T
    lane = lax.broadcasted_iota(jnp.int32, (tile, 128), 1)
    for q0 in range(0, seq, tile):
        kl = min(seq, q0 + 2 * tile)
        qt = qs[q0 : q0 + tile]
        allowed = bidc_ref[q0:kl, :] <= bidr_ref[0:1, q0 : q0 + tile]
        parts = []
        for head in range(2):
            qm = jnp.where((lane // 64) == head, qt, jnp.zeros_like(qt))
            tail = jnp.where(allowed, mm_nt(k[q0:kl], qm), masked_score)
            top = jnp.max(tail, axis=0, keepdims=True)
            if q0:
                lead = mm_nt(k[:q0], qm)
                top = jnp.maximum(top, jnp.max(lead, axis=0, keepdims=True))
                lead = jnp.exp(lead - top)
            tail = jnp.exp(tail - top)
            total = jnp.sum(tail, axis=0, keepdims=True)
            if q0:
                total = total + jnp.sum(lead, axis=0, keepdims=True)
            inverse = 1.0 / total
            vh = vt[64 * head : 64 * head + 64]
            ot = mm(vh[:, q0:kl], (tail * inverse).astype(bf16))
            if q0:
                ot = ot + mm(vh[:, :q0], (lead * inverse).astype(bf16))
            lse_ref[0, head : head + 1, q0 : q0 + tile] = top + jnp.log(total)
            parts.append(ot)
        out = jnp.concatenate(parts, axis=0).T.astype(bf16)
        o_ref[q0 : q0 + tile, pl.ds(pl.multiple_of(pair * 128, 128), 128)] = out

    @pl.when(pair == pl.num_programs(0) - 1)
    def _():
        for row in range(0, seq, tile):
            rows = pl.ds(row, tile)
            mid = tok_ref[rows, :].astype(f32) + mm(o_ref[rows, :], wo_ref[0])
            mid_ref[rows, :] = mid
            r2 = lax.rsqrt(jnp.mean(mid * mid, axis=1, keepdims=True) + norm_eps)
            h2 = (mid * r2 * gains_ref[5:6, :]).astype(bf16)
            h2_ref[rows, :] = h2
            logits = mm(h2, wr_ref[...])
            spot = lax.broadcasted_iota(jnp.int32, logits.shape, 1)
            logits = jnp.where(spot < 4, logits, masked_score)
            e = jnp.exp(logits - jnp.max(logits, axis=1, keepdims=True))
            probs_ref[rows, :] = e / jnp.sum(e, axis=1, keepdims=True)
        routers = gains_ref[...].astype(bf16)
        logits = mm_nt(jnp.concatenate([routers, routers], axis=0), h2_ref[...])
        spot = lax.broadcasted_iota(jnp.int32, logits.shape, 0)
        logits = jnp.where(spot < 4, logits, masked_score)
        e = jnp.exp(logits - jnp.max(logits, axis=0, keepdims=True))
        probst_ref[...] = e / jnp.sum(e, axis=0, keepdims=True)
        for copy in copies():
            copy.wait()


def attention_forward(tokens, bid_row, bid_col, full, wr, slots):
    exps = slots.shape[0]
    seq, width = tokens.shape
    pairs = width // 128
    return pl.pallas_call(
        functools.partial(forward_kernel, exps),
        grid=(pairs,),
        in_specs=[
            once((seq, width)),
            once(bid_row.shape),
            once(bid_col.shape),
            pl.BlockSpec((3, width, 128), lambda i: (0, 0, i)),
            pl.BlockSpec((1, width, width), lambda i: (3, 0, 0), pipeline_mode=pl.Buffered(1)),
            once(wr.shape),
            ANY,
        ],
        out_specs=[
            pl.BlockSpec((3, seq, 128), lambda i: (0, 0, i)),
            pl.BlockSpec((1, 8, seq), lambda i: (i, 0, 0)),
            whole_spec((seq, width)),
            whole_spec((seq, width)),
            whole_spec((seq, width)),
            whole_spec((seq, 128)),
            whole_spec((16, seq)),
            whole_spec((8, width)),
            ANY,
        ],
        out_shape=[
            jax.ShapeDtypeStruct((3, seq, width), bf16),
            jax.ShapeDtypeStruct((pairs, 8, seq), f32),
            jax.ShapeDtypeStruct((seq, width), bf16),
            jax.ShapeDtypeStruct((seq, width), f32),
            jax.ShapeDtypeStruct((seq, width), bf16),
            jax.ShapeDtypeStruct((seq, 128), f32),
            jax.ShapeDtypeStruct((16, seq), f32),
            jax.ShapeDtypeStruct((8, width), f32),
            jax.ShapeDtypeStruct(slots.shape, bf16),
        ],
        scratch_shapes=[pltpu.VMEM((seq, width), bf16)] + pair_sems(exps),
        compiler_params=params(("arbitrary",), collective_id=1, has_side_effects=True),
        cost_estimate=pl.CostEstimate(
            flops=30_000_000_000, bytes_accessed=20_000_000, transcendentals=12_000_000
        ),
        name="attention_forward",
    )(tokens, bid_row, bid_col, full, full, wr, slots)


def slots_of(place_row, cap):
    slot = lax.broadcasted_iota(jnp.int32, (cap, place_row.shape[1]), 0)
    return (slot == place_row).astype(f32).astype(bf16)


def dispatch_kernel(h2_ref, place_ref, probst_ref, rows_ref, chosen_ref):
    expert = pl.program_id(0)
    cap = rows_ref.shape[1]
    row = place_ref[pl.ds(expert, 1), :]
    hot = slots_of(row, cap)
    rows_ref[0] = mm(hot, h2_ref[...]).astype(bf16)
    value = probst_ref[pl.ds(expert, 1), :]
    high = value.astype(bf16)
    rest = value - high.astype(f32)
    middle = rest.astype(bf16)
    low = (rest - middle.astype(f32)).astype(bf16)
    spot = lax.broadcasted_iota(jnp.int32, (16, row.shape[1]), 0)
    pieces = jnp.where(
        spot == 0, high.astype(f32), jnp.where(spot == 1, middle.astype(f32), jnp.where(spot == 2, low.astype(f32), 0.0))
    )
    chosen = jnp.sum(mm_nt(pieces.astype(bf16), hot), axis=0, keepdims=True)
    chosen_ref[...] = jnp.zeros_like(chosen_ref)
    chosen_ref[0, :, :cap] = jnp.broadcast_to(chosen, (8, cap))


def dispatch(h2, place_row, probst, experts_all, cap, lanes):
    seq, width = h2.shape
    return pl.pallas_call(
        dispatch_kernel,
        grid=(experts_all,),
        in_specs=[once(h2.shape), once(place_row.shape), once(probst.shape)],
        out_specs=[
            pl.BlockSpec((1, cap, width), lambda e: (e, 0, 0)),
            pl.BlockSpec((1, 8, lanes), lambda e: (e, 0, 0)),
        ],
        out_shape=[
            jax.ShapeDtypeStruct((experts_all, cap, width), bf16),
            jax.ShapeDtypeStruct((experts_all, 8, lanes), f32),
        ],
        compiler_params=params(("arbitrary",)),
        cost_estimate=pl.CostEstimate(
            flops=5_000_000_000, bytes_accessed=6_000_000, transcendentals=0
        ),
        name="dispatch",
    )(h2, place_row, probst)


def gated(x, g, wg, wu, wn):
    gate, up = mm(x, wg), mm(x, wu)
    hgrad = mm_nt(g, wn)
    sig = lax.logistic(gate)
    active = gate * sig
    slope = sig * (1.0 + gate * (1.0 - sig))
    hidden = (active * up).astype(bf16)
    return hidden, (hgrad * up * slope).astype(bf16), (hgrad * active).astype(bf16)


def routed_kernel(
    exps, shds,
    rows_ref, chosen_ref, grads_ref, packed_ref,
    eout_ref, gin_ref, sum_ref,
    x_s, g_s, c_s, w_s, n_s, hid_s, gg_s, ug_s, out_s, gin_s, wide_l, narrow_l,
    load_sem, x_send, x_recv, c_send, c_recv, o_send, o_recv, i_send, w_sem, s_send, s_recv,
):
    me = lax.axis_index("exp")
    _, cap, width = x_s.shape
    hidden = hid_s.shape[1]
    rows_all = exps * cap
    peers = [lax.bitwise_xor(me, k) for k in range(exps)]
    group = lax.axis_index("grp")
    core = lax.rem(group, 2)
    partner = {"grp": lax.bitwise_xor(group, 1)}
    greet([{"exp": peer} for peer in peers[1:]] + [partner])
    deep, tall = w_s.shape[2], n_s.shape[2]
    base = hidden // 256 * deep
    wide_at = lambda b: pl.ds(pl.multiple_of(b * deep, 16), deep)
    narrow_at = lambda b: pl.ds(base + b * tall, tall)
    lanes_at = lambda b: pl.ds(pl.multiple_of(256 * b, 256), 256)

    chosen, arriving = [], []
    for k in range(1, exps):
        target = {"exp": peers[k]}
        chosen.append(send(chosen_ref.at[peers[k]], c_s.at[k], c_send.at[k], c_recv.at[k], target))
        arriving.append(send(rows_ref.at[peers[k]], x_s.at[k], x_send.at[k], x_recv.at[k], target))
    for copy in chosen + arriving[:2]:
        copy.start()
    loads = [
        pltpu.make_async_copy(rows_ref.at[me], x_s.at[0], load_sem.at[0]),
        pltpu.make_async_copy(chosen_ref.at[me], c_s.at[0], load_sem.at[1]),
        pltpu.make_async_copy(grads_ref, g_s, load_sem.at[2]),
    ]
    for c in range(2):
        for b in range(hidden // 256):
            loads.append(
                pltpu.make_async_copy(
                    packed_ref.at[c, :, wide_at(b), :], w_s.at[c, :, :, lanes_at(b)], load_sem.at[len(loads)]
                )
            )
        for b in range(width // 256):
            loads.append(
                pltpu.make_async_copy(
                    packed_ref.at[c, :, narrow_at(b), :], n_s.at[:, c, :, lanes_at(b)], load_sem.at[len(loads)]
                )
            )
    for copy in loads:
        copy.start()
    for copy in loads:
        copy.wait()

    ft = 512
    returns, kept = [], []
    for k in range(exps):
        if k:
            chosen[k - 1].wait()
            arriving[k - 1].wait()
        scale = c_s[k].T[:cap, 0:1]
        g_s[k] = (g_s[k].astype(f32) * scale).astype(bf16)

        @pl.loop(0, hidden // ft)
        def _(f):
            columns = pl.ds(pl.multiple_of(f * ft, ft), ft)
            wg = w_s[0, :, :, columns].reshape(width, ft)
            wu = w_s[1, :, :, columns].reshape(width, ft)
            hid, gg, ug = gated(x_s[k], g_s[k], wg, wu, n_s[f].reshape(ft, width))
            hid_s[pl.ds(k * cap, cap), columns] = hid
            gg_s[pl.ds(k * cap, cap), columns] = gg
            ug_s[pl.ds(k * cap, cap), columns] = ug

        mine = pl.ds(k * cap, cap)
        if k >= 2:
            kept[k - 2].wait()
        for b in range(width // 256):
            part = slice(256 * b, 256 * b + 256)
            out_s[k, :, part] = mm(hid_s[mine, :], n_s[:, :, :, part].reshape(hidden, 256)).astype(bf16)
            wg = w_s[0].reshape(width, hidden)[part]
            wu = w_s[1].reshape(width, hidden)[part]
            gin_s[k % 2, :, part] = (mm_nt(gg_s[mine, :], wg) + mm_nt(ug_s[mine, :], wu)).astype(bf16)

        if k:
            back = send(
                out_s.at[k], eout_ref.at[me], o_send.at[k], o_recv.at[k], {"exp": peers[k]}
            )
        else:
            back = pltpu.make_async_copy(out_s.at[0], eout_ref.at[me], o_send.at[0])
            for copy in arriving[2:]:
                copy.start()
        kept.append(pltpu.make_async_copy(gin_s.at[k % 2], gin_ref.at[peers[k]], i_send.at[k]))
        for copy in (back, kept[k]):
            copy.start()
        returns.append(back)

    wide = hidden // shds
    per = wide // 256

    across = lambda f: pl.ds(pl.multiple_of(f * wide, wide), wide)

    def swaps(f):
        return [
            send(w_s.at[1 - core, :, :, across(f)], wide_l.at[f], s_send.at[f, 0], s_recv.at[f, 0], partner),
            send(n_s.at[f, 1 - core], narrow_l.at[f], s_send.at[f, 1], s_recv.at[f, 1], partner),
        ]

    def stores(f):
        made = []
        for b in range(per):
            block = per * f + b
            made.append((w_s.at[core, :, :, lanes_at(block)], sum_ref.at[:, wide_at(block), :]))
        for b in range(width // 256):
            made.append((n_s.at[f, core, :, lanes_at(b)], sum_ref.at[f, narrow_at(b), :]))
        return [pltpu.make_async_copy(a, b, w_sem.at[f, i]) for i, (a, b) in enumerate(made)]

    def add(f):
        for copy in swaps(f):
            copy.wait_recv()
        for z in range(shds):
            own = w_s[core, z, :, across(f)].astype(f32)
            w_s[core, z, :, across(f)] = (own + wide_l[f, z].astype(f32)).astype(bf16)
        n_s[f, core] = (n_s[f, core].astype(f32) + narrow_l[f].astype(f32)).astype(bf16)
        for copy in stores(f):
            copy.start()

    @pl.loop(0, shds)
    def _(f):
        columns = pl.ds(pl.multiple_of(f * wide, wide), wide)
        x = x_s[...].reshape(rows_all, width)
        g = g_s[...].reshape(rows_all, width)
        part = w_s.shape[1:3] + (wide,)
        w_s[0, :, :, columns] = mm_tn(x, gg_s[:, columns]).astype(bf16).reshape(part)
        w_s[1, :, :, columns] = mm_tn(x, ug_s[:, columns]).astype(bf16).reshape(part)
        n_s[f] = mm_tn(hid_s[:, columns], g).astype(bf16).reshape(n_s.shape[1:])
        for copy in swaps(f):
            copy.start()

        @pl.when(f > 0)
        def _():
            add(f - 1)

    add(shds - 1)
    for copy in returns + kept[-2:]:
        copy.wait()

    @pl.loop(0, shds)
    def _(f):
        for copy in swaps(f):
            copy.wait_send()
        for copy in stores(f):
            copy.wait()


def routed(slot_rows, chosen, grads, packed, hidden):
    exps, cap, width = slot_rows.shape
    shds, height = packed.shape[1:3]
    deep, tall = width // shds, hidden // shds // 2
    pieces = hidden // shds // 256 + width // 256
    big = lambda *shape: pltpu.VMEM(shape, bf16)
    sems = lambda *n: pltpu.SemaphoreType.DMA(n)
    return pl.pallas_call(
        functools.partial(routed_kernel, exps, shds),
        in_specs=[ANY] * 4,
        out_specs=[ANY] * 3,
        out_shape=[
            jax.ShapeDtypeStruct((exps, cap, width), bf16),
            jax.ShapeDtypeStruct((exps, cap, width), bf16),
            jax.ShapeDtypeStruct((shds, height, 256), bf16),
        ],
        scratch_shapes=[
            big(exps, cap, width),
            big(exps, cap, width),
            pltpu.VMEM(chosen.shape, f32),
            big(2, shds, deep, hidden),
            big(shds, 2, tall, width),
            big(exps * cap, hidden),
            big(exps * cap, hidden),
            big(exps * cap, hidden),
            big(exps, cap, width),
            big(2, cap, width),
            big(shds, shds, deep, hidden // shds),
            big(shds, tall, width),
            sems(3 + 2 * (hidden // 256 + width // 256)),
            sems(exps), sems(exps), sems(exps), sems(exps), sems(exps), sems(exps), sems(exps),
            sems(shds, pieces), sems(shds, 2), sems(shds, 2),
        ],
        compiler_params=params(collective_id=2, has_side_effects=True),
        cost_estimate=pl.CostEstimate(
            flops=18 * exps * cap * width * hidden,
            bytes_accessed=40_000_000,
            transcendentals=exps * cap * hidden,
        ),
        name="routed",
    )(slot_rows, chosen, grads, packed)


def ffn_kernel(
    x_ref, g_ref, wg_ref, wu_ref, wn_ref, back_ref,
    out_ref, gin_ref, part_a, part_b, ein_ref,
    acc_out, acc_gin, hid_s, gg_s, ug_s, wide_s, narrow_s, wide_l, narrow_l,
    own_sem, send_sem, recv_sem, b_send, b_recv,
    *, tile,
):
    f = pl.program_id(0)
    last = pl.num_programs(0) - 1
    rows_all, width = x_ref.shape
    group = lax.axis_index("grp")
    core = lax.rem(group, 2)
    partner = {"grp": lax.bitwise_xor(group, 1)}
    ft = wide_s.shape[3]
    shards, tall = narrow_s.shape[2:4]

    def swaps(step):
        return [
            send(a.at[step, b], c.at[step], send_sem.at[step, i], recv_sem.at[step, i], partner)
            for i, (a, b, c) in enumerate(
                [(wide_s, 1 - core, wide_l), (narrow_s, 1 - core, narrow_l)]
            )
        ]

    def stores(step):
        columns = pl.ds(pl.multiple_of(step * ft, ft), ft)
        at = pl.ds(step * shards, shards)
        return [
            pltpu.make_async_copy(wide_s.at[step, core], part_a.at[:, columns], own_sem.at[step, 0]),
            pltpu.make_async_copy(narrow_s.at[step, core], part_b.at[at], own_sem.at[step, 1]),
        ]

    def add(step):
        for copy in swaps(step):
            copy.wait_recv()
        wide_s[step, core] = (wide_s[step, core].astype(f32) + wide_l[step].astype(f32)).astype(bf16)
        narrow_s[step, core] = (narrow_s[step, core].astype(f32) + narrow_l[step].astype(f32)).astype(bf16)
        for copy in stores(step):
            copy.start()

    exps = back_ref.shape[0]
    columns = others("exp", exps)

    def returns():
        me = columns[0]
        made = [pltpu.make_async_copy(back_ref.at[me], ein_ref.at[me], b_send.at[0])]
        for k in range(1, exps):
            made.append(
                send(
                    back_ref.at[columns[k]], ein_ref.at[me],
                    b_send.at[k], b_recv.at[k], {"exp": columns[k]},
                )
            )
        return made

    @pl.when(f == 0)
    def _():
        greet([{"exp": column} for column in columns[1:]] + [partner])
        for copy in returns():
            copy.start()
        acc_out[...] = jnp.zeros_like(acc_out)
        acc_gin[...] = jnp.zeros_like(acc_gin)

    deep = wg_ref.shape[3] // 2
    order = [(z, e) for e in range(wg_ref.shape[2]) for z in range(wg_ref.shape[1])]

    def wide(ref):
        blocks = [
            jnp.concatenate([ref[0, z, e, deep * b : deep * (b + 1)] for z, e in order], axis=0)
            for b in range(2)
        ]
        return jnp.concatenate(blocks, axis=1)

    wg, wu = wide(wg_ref), wide(wu_ref)
    narrow = [
        jnp.concatenate([wn_ref[c, z, e, tall * b : tall * (b + 1)] for b in range(width // 256)], axis=1)
        for e in range(wn_ref.shape[2])
        for z in range(wn_ref.shape[1])
        for c in range(2)
    ]
    wn = jnp.concatenate(narrow, axis=0)
    for row in range(0, rows_all, tile):
        rows = pl.ds(row, tile)
        x, g = x_ref[rows, :], g_ref[rows, :]
        hidden, gg, ug = gated(x, g, wg, wu, wn)
        hid_s[rows, :], gg_s[rows, :], ug_s[rows, :] = hidden, gg, ug
        acc_out[rows, :] += mm(hidden, wn)
        acc_gin[rows, :] += mm_nt(gg, wg) + mm_nt(ug, wu)
    wide_s[f, 0] = mm_tn(x_ref[...], gg_s[...]).astype(bf16)
    wide_s[f, 1] = mm_tn(x_ref[...], ug_s[...]).astype(bf16)
    narrow = mm_tn(hid_s[...], g_ref[...]).astype(bf16).reshape(shards, 2, tall, width)
    for c in range(2):
        narrow_s[f, c] = narrow[:, c]
    for copy in swaps(f):
        copy.start()

    @pl.when(f > 0)
    def _():
        add(f - 1)

    @pl.when(f == last)
    def _():
        out_ref[...] = acc_out[...].astype(out_ref.dtype)
        gin_ref[...] = acc_gin[...].astype(gin_ref.dtype)

        add(last)

        @pl.loop(0, pl.num_programs(0))
        def _(step):
            for copy in swaps(step):
                copy.wait_send()
            for copy in stores(step):
                copy.wait()

        for copy in returns():
            copy.wait()


def ffn(x, g, packed, back, hidden, out_type, tile, name):
    rows, width = x.shape
    _, shds, exps, height, _ = packed.shape
    spread = shds * exps
    ft = 512
    steps = hidden // ft
    deep, tall = width // spread, hidden // spread // 2
    shards = spread // steps
    base = hidden // 256 * deep
    narrow_high = height - base
    sems = pltpu.SemaphoreType.DMA((steps, 2))
    return pl.pallas_call(
        functools.partial(ffn_kernel, tile=tile),
        grid=(steps,),
        in_specs=[
            once((rows, width)),
            once((rows, width)),
            pl.BlockSpec((1, shds, exps, 2 * deep, 256), lambda f: (0, 0, 0, f, 0)),
            pl.BlockSpec((1, shds, exps, 2 * deep, 256), lambda f: (1, 0, 0, f, 0)),
            pl.BlockSpec((2, shds, shards // shds, narrow_high, 256), lambda f: (0, 0, f, base // narrow_high, 0)),
            ANY,
        ],
        out_specs=[once((rows, width)), once((rows, width)), ANY, ANY, ANY],
        out_shape=[
            jax.ShapeDtypeStruct((rows, width), out_type),
            jax.ShapeDtypeStruct((rows, width), out_type),
            jax.ShapeDtypeStruct((width, hidden), bf16),
            jax.ShapeDtypeStruct((spread, tall, width), bf16),
            jax.ShapeDtypeStruct(back.shape, bf16),
        ],
        scratch_shapes=[
            pltpu.VMEM((rows, width), f32),
            pltpu.VMEM((rows, width), f32),
            pltpu.VMEM((rows, ft), bf16),
            pltpu.VMEM((rows, ft), bf16),
            pltpu.VMEM((rows, ft), bf16),
            pltpu.VMEM((steps, 2, width, ft), bf16),
            pltpu.VMEM((steps, 2, shards, tall, width), bf16),
            pltpu.VMEM((steps, width, ft), bf16),
            pltpu.VMEM((steps, shards, tall, width), bf16),
            sems, sems, sems,
        ]
        + pair_sems(back.shape[0]),
        compiler_params=params(("arbitrary",), collective_id=3, has_side_effects=True),
        cost_estimate=pl.CostEstimate(
            flops=18 * rows * width * hidden,
            bytes_accessed=12 * width * hidden + 8 * rows * width,
            transcendentals=rows * hidden,
        ),
        name=name,
    )(x, g, packed, packed, packed, back)


def plane_copies(exps, block_for, landed_ref, send_sem, recv_sem):
    columns = others("exp", exps)
    made = [pltpu.make_async_copy(block_for(columns[0]), landed_ref.at[0], send_sem.at[0])]
    for k in range(1, exps):
        made.append(
            send(
                block_for(columns[k]), landed_ref.at[k],
                send_sem.at[k], recv_sem.at[k], {"exp": columns[k]},
            )
        )
    return made


def combine_kernel(
    mid_ref, sout_ref, sin_ref, g_ref, h2_ref, probs_ref, place_ref, eout_ref, ein_ref,
    gains_ref, wr_ref, wo_ref, part_ref,
    block_ref, midg_ref, midb_ref, og_ref, gain_ref, rgrad_ref, landed_ref,
    send_sem, recv_sem,
):
    step = pl.program_id(0)
    exps = part_ref.shape[0]
    exchange = lambda: plane_copies(exps, lambda c: part_ref.at[c], landed_ref, send_sem, recv_sem)

    @pl.when(step == 0)
    def _():
        greet([{"exp": column} for column in others("exp", exps)[1:]])
        for copy in exchange():
            copy.start()

    tile, width = mid_ref.shape
    experts_all, cap = eout_ref.shape[0], eout_ref.shape[1]
    slot = lax.broadcasted_iota(jnp.int32, (tile, cap), 1)
    g = g_ref[...].astype(f32)
    probs = probs_ref[...]
    spot = lax.broadcasted_iota(jnp.int32, probs.shape, 1)
    mixture = jnp.zeros((tile, width), f32)
    moe_in = jnp.zeros((tile, width), f32)
    pgrad = jnp.zeros(probs.shape, f32)
    for e in range(experts_all):
        hot = (slot == place_ref[:, e : e + 1]).astype(f32).astype(bf16)
        pair_out = mm(hot, eout_ref[e])
        mixture += probs[:, e : e + 1] * pair_out
        grad = jnp.sum(g * pair_out, axis=1, keepdims=True)
        pgrad = jnp.where(spot == e, grad, pgrad)
        moe_in += mm(hot, ein_ref[e])
    mid = mid_ref[...]
    block_ref[...] = (mid + sout_ref[...] + mixture).astype(bf16)
    inner = jnp.sum(pgrad * probs, axis=1, keepdims=True)
    lgrad = (probs * (pgrad - inner)).astype(bf16)
    h2_grad = moe_in + mm_nt(lgrad, wr_ref[...]) + sin_ref[...]
    r2 = lax.rsqrt(jnp.mean(mid * mid, axis=1, keepdims=True) + norm_eps)
    n2 = mid * r2
    d2 = h2_grad * gains_ref[5:6, :]
    mid_grad = g + r2 * (d2 - n2 * jnp.mean(d2 * n2, axis=1, keepdims=True))
    midb = mid_grad.astype(bf16)
    midg_ref[...] = mid_grad
    midb_ref[...] = midb
    og_ref[...] = mm_nt(midb, wo_ref[0]).astype(bf16)
    gsum = jnp.sum(h2_grad * n2, axis=0, keepdims=True)
    rsum = mm_tn(lgrad, h2_ref[...])[:8]

    @pl.when(step == 0)
    def _():
        gain_ref[...] = jnp.zeros_like(gain_ref)
        rgrad_ref[...] = jnp.zeros_like(rgrad_ref)

    gain_ref[0:1, :] += gsum
    rgrad_ref[...] += rsum

    @pl.when(step == pl.num_programs(0) - 1)
    def _():
        for copy in exchange():
            copy.wait()


def combine(mid, sout, sin, g, h2, probs, place_col, eout, ein, gains, wr, full, part):
    seq, width = mid.shape
    tile = 256
    by_rows = pl.BlockSpec((tile, width), lambda i: (i, 0))
    lanes = pl.BlockSpec((tile, 128), lambda i: (i, 0))
    return pl.pallas_call(
        combine_kernel,
        grid=(seq // tile,),
        in_specs=[
            by_rows, by_rows, by_rows, by_rows, by_rows, lanes, lanes,
            once(eout.shape), once(ein.shape), once(gains.shape), once(wr.shape),
            pl.BlockSpec((1, width, width), lambda i: (3, 0, 0), pipeline_mode=pl.Buffered(1)),
            ANY,
        ],
        out_specs=[
            by_rows, by_rows, by_rows, by_rows, whole_spec((8, width)), whole_spec((8, width)), ANY,
        ],
        out_shape=[
            jax.ShapeDtypeStruct((seq, width), bf16),
            jax.ShapeDtypeStruct((seq, width), f32),
            jax.ShapeDtypeStruct((seq, width), bf16),
            jax.ShapeDtypeStruct((seq, width), bf16),
            jax.ShapeDtypeStruct((8, width), f32),
            jax.ShapeDtypeStruct((8, width), f32),
            jax.ShapeDtypeStruct(part.shape, bf16),
        ],
        scratch_shapes=pair_sems(part.shape[0]),
        compiler_params=params(("arbitrary",), collective_id=5, has_side_effects=True),
        cost_estimate=pl.CostEstimate(
            flops=11_000_000_000, bytes_accessed=30_000_000, transcendentals=0
        ),
        name="combine",
    )(mid, sout, sin, g, h2, probs, place_col, eout, ein, gains, wr, full, part)


def backward_kernel(
    exps, shds,
    qkv_ref, og_ref, lse_ref, bidr_ref, bidc_ref, tok_ref, midg_ref, o_ref, midb_ref, w_ref,
    gains_ref, gain2_ref, rgrad_ref, lb_ref, part_ref,
    igrad_ref, sw_ref, sa_ref, sb_ref, st_ref,
    dk_s, dv_s, h1t_s, ot_s, grad_s, stack_s, pair_s, plane_s, r_s, zr_s, fw_s,
    la_s, qa_s, qb_s, za_s, zb_s, fa_s, fb_s, tiny_s, tpair_s, tplane_s, tz_s,
    a_send, a_recv, pair_send, pair_recv, p_send, p_recv, r_send, r_recv, f_own, f_send, f_recv,
    line_send, line_recv, last_own, last_send, last_recv, t_send, t_recv, tp_send, tp_recv,
):
    step = pl.program_id(0)
    columns, layers = others("exp", exps), others("shd", shds)
    group = lax.axis_index("grp")
    core = lax.rem(group, 2)
    partner = {"grp": lax.bitwise_xor(group, 1)}
    seq, width = tok_ref.shape
    tile = 256
    pieces = width // 128
    deep = width // exps
    early = [(j + 1) % shds for j in range(shds)]

    def chunk(j):
        return plane_copies(
            exps, lambda c: part_ref.at[c, layers[j]], la_s.at[j], a_send.at[j], a_recv.at[j]
        )

    def chunk_line(j):
        return send(
            qa_s.at[j], za_s.at[j], line_send.at[0, j], line_recv.at[0, j], {"shd": layers[j]}
        )

    def chunk_sum(j, landed):
        value = landed[0].astype(f32)
        for k in range(1, exps):
            value = value + landed[k].astype(f32)
        qa_s[j] = value.astype(bf16)
        if j:
            chunk_line(j).start()

    def line(part_s, landed_s, kind):
        return [
            send(
                part_s.at[layers[k]], landed_s.at[k],
                line_send.at[kind, k], line_recv.at[kind, k], {"shd": layers[k]},
            )
            for k in range(1, shds)
        ]

    def plane_rows(k):
        return pl.ds(pl.multiple_of(columns[k] * deep, 16), deep)

    def pair_copy(p):
        return send(stack_s.at[p], pair_s.at[p // 2], pair_send.at[p // 2], pair_recv.at[p // 2], partner)

    def plane_copy(p):
        return [
            send(
                stack_s.at[p, :, plane_rows(k), :], plane_s.at[p // 2, k],
                p_send.at[p // 2, k], p_recv.at[p // 2, k], {"exp": columns[k]},
            )
            for k in range(1, exps)
        ]

    def line_copy(p):
        return [
            send(
                r_s.at[p // 2, layers[k]], zr_s.at[p // 2, k],
                r_send.at[p // 2, k], r_recv.at[p // 2, k], {"shd": layers[k]},
            )
            for k in range(1, shds)
        ]

    def final_copy(p):
        at = sw_ref.at[:, :, pl.ds(pl.multiple_of(p * 128, 128), 128)]
        return [
            pltpu.make_async_copy(fw_s.at[p // 2], at, f_own.at[p // 2]),
            send(fw_s.at[p // 2], at, f_send.at[p // 2], f_recv.at[p // 2], partner),
        ]

    def start(copies):
        for copy in copies:
            copy.start()

    def summing(p):
        return jnp.logical_and(p >= 0, core == p % 2)

    def to_pair(p):
        @pl.when(core != p % 2)
        def _():
            pair_copy(p).start()

    def to_plane(p):
        @pl.when(summing(p))
        def _():
            pair_copy(p).wait_recv()
            for i in range(4):
                stack_s[p, i] = (stack_s[p, i].astype(f32) + pair_s[p // 2, i].astype(f32)).astype(bf16)
            start(plane_copy(p))

    def to_line(p):
        @pl.when(summing(p))
        def _():
            for copy in plane_copy(p):
                copy.wait_recv()
            for i in range(4):
                value = stack_s[p, i, plane_rows(0), :].astype(f32)
                for k in range(1, exps):
                    value = value + plane_s[p // 2, k, i].astype(f32)
                r_s[p // 2, :, i] = value.astype(bf16).reshape(shds, deep // shds, 128)
            start(line_copy(p))

    def to_final(p):
        @pl.when(summing(p))
        def _():
            for copy in line_copy(p):
                copy.wait_recv()
            value = r_s[p // 2, layers[0]].astype(f32)
            for k in range(1, shds):
                value = value + zr_s[p // 2, k].astype(f32)
            fw_s[p // 2] = value
            start(final_copy(p))

    def line_total(landed_s, part_s):
        value = part_s[layers[0]].astype(f32)
        for k in range(1, shds):
            value = value + landed_s[k].astype(f32)
        return value

    def finals(kind, part_s, out_ref):
        return [
            pltpu.make_async_copy(part_s, out_ref.at[core], last_own.at[kind]),
            send(part_s, out_ref.at[core], last_send.at[kind], last_recv.at[kind], partner),
        ]

    @pl.when(step == 0)
    def _():
        greet(
            [{"shd": layer} for layer in layers[1:]]
            + [{"exp": column} for column in columns[1:]]
            + [partner]
        )
        for z in range(shds):
            qb_s[z] = sum([lb_ref[k, z].astype(f32) for k in range(1, exps)], lb_ref[0, z].astype(f32)).astype(bf16)
        start(line(qb_s, zb_s, 1))
        for row in range(0, seq, tile):
            x = tok_ref[row : row + tile, :].astype(f32)
            r1 = lax.rsqrt(jnp.mean(x * x, axis=1, keepdims=True) + norm_eps)
            h1t_s[:, row : row + tile] = (x * r1 * gains_ref[4:5, :]).astype(bf16).T
            ot_s[:, row : row + tile] = o_ref[row : row + tile, :].T
        grad_s[...] = jnp.zeros_like(grad_s)

    for turn, j in enumerate(early):

        @pl.when(step == turn)
        def _():
            start(chunk(j))

        @pl.when(step == turn + 2)
        def _():
            for copy in chunk(j):
                copy.wait()
            chunk_sum(j, la_s.at[j])

    @pl.when(step == shds)
    def _():
        for copy in line(qb_s, zb_s, 1):
            copy.wait()
        fb_s[...] = line_total(zb_s, qb_s)
        start(finals(1, fb_s, sb_ref))

    qs = qkv_ref[0] * jnp.asarray(0.125, bf16)
    k = qkv_ref[1]
    v = qkv_ref[2]
    kt = k.T
    og = og_ref[...]
    lane = lax.broadcasted_iota(jnp.int32, (tile, 128), 1)
    dk_s[...] = jnp.zeros_like(dk_s)
    dv_s[...] = jnp.zeros_like(dv_s)
    dqs = []
    for q0 in range(0, seq, tile):
        kl = min(seq, q0 + 2 * tile)
        qt, ot = qs[q0 : q0 + tile], og[q0 : q0 + tile]
        allowed = bidc_ref[q0:kl, :] <= bidr_ref[0:1, q0 : q0 + tile]
        parts = []
        for head in range(2):
            own = (lane // 64) == head
            qm = jnp.where(own, qt, jnp.zeros_like(qt))
            om = jnp.where(own, ot, jnp.zeros_like(ot))
            lse = lse_ref[0, head : head + 1, q0 : q0 + tile]
            spans = ([(0, q0)] if q0 else []) + [(q0, kl)]
            kept = []
            delta = jnp.zeros((1, tile), f32)
            for low, high in spans:
                s = mm_nt(k[low:high], qm)
                if low == q0:
                    s = jnp.where(allowed, s, masked_score)
                p = jnp.exp(s - lse)
                dp = mm_nt(v[low:high], om)
                delta = delta + jnp.sum(p * dp, axis=0, keepdims=True)
                kept.append((low, high, p, dp))
            dq = jnp.zeros((64, tile), f32)
            for low, high, p, dp in kept:
                ds = (p * (dp - delta)).astype(bf16)
                dv_s[low:high, :] += mm(p.astype(bf16), om)
                dk_s[low:high, :] += mm(ds, qm)
                dq = dq + mm(kt[64 * head : 64 * head + 64, low:high], ds)
            parts.append(dq)
        dqs.append((jnp.concatenate(parts, axis=0).T * 0.125).astype(bf16))
        if q0 == tile:
            to_plane(step - 1)
    dqkv = [jnp.concatenate(dqs, axis=0), dk_s[...].astype(bf16), dv_s[...].astype(bf16)]
    to_final(step - 4)
    to_line(step - 3)
    wide = mm(h1t_s[...], jnp.concatenate(dqkv, axis=1)).astype(bf16)
    for i in range(3):
        stack_s[step, i] = wide[:, 128 * i : 128 * i + 128]
    stack_s[step, 3] = mm(ot_s[...], midb_ref[...]).astype(bf16)
    to_pair(step)
    for row in range(0, seq, tile):
        rows = slice(row, row + tile)
        grad_s[rows, :] += (
            mm_nt(dqkv[0][rows], w_ref[0]) + mm_nt(dqkv[1][rows], w_ref[1]) + mm_nt(dqkv[2][rows], w_ref[2])
        )

    @pl.when(step == pieces - 1)
    def _():
        to_line(pieces - 3)
        to_final(pieces - 4)
        to_plane(pieces - 1)
        gain = jnp.zeros((1, width), f32)
        for row in range(0, seq, tile):
            rows = slice(row, row + tile)
            x = tok_ref[rows, :].astype(f32)
            r1 = lax.rsqrt(jnp.mean(x * x, axis=1, keepdims=True) + norm_eps)
            n1 = x * r1
            grad = grad_s[rows, :]
            gain = gain + jnp.sum(grad * n1, axis=0, keepdims=True)
            d1 = grad * gains_ref[4:5, :]
            igrad_ref[rows, :] = midg_ref[rows, :] + r1 * (d1 - n1 * jnp.mean(d1 * n1, axis=1, keepdims=True))
        spot = lax.broadcasted_iota(jnp.int32, (8, width), 0)
        small = jnp.where(spot < 4, rgrad_ref[...], jnp.where(spot == 4, gain, gain2_ref[0:1, :]))
        tiny_s[...] = small
        tswap = send(tiny_s, tpair_s, t_send, t_recv, partner)
        tswap.start()
        to_line(pieces - 2)
        to_final(pieces - 3)
        to_line(pieces - 1)
        tswap.wait()
        tpair_s[...] += tiny_s[...]
        tplane = [
            send(tpair_s, tplane_s.at[k], tp_send.at[k], tp_recv.at[k], {"exp": columns[k]})
            for k in range(1, exps)
        ]
        start(tplane)
        to_final(pieces - 2)
        for copy in tplane:
            copy.wait()
        value = qa_s[0].astype(f32)
        for j in range(1, shds):
            chunk_line(j).wait()
            value = value + za_s[j].astype(f32)
        fa_s[...] = value
        start(finals(0, fa_s, sa_ref))
        tz_s[0] = sum([tplane_s[k] for k in range(1, exps)], tpair_s[...])
        tline = [
            send(
                tz_s.at[0], tz_s.at[k], line_send.at[2, k], line_recv.at[2, k], {"shd": layers[k]}
            )
            for k in range(1, shds)
        ]
        start(tline)
        to_final(pieces - 1)
        for copy in tline:
            copy.wait()
        st_ref[...] = sum([tz_s[k] for k in range(1, shds)], tz_s[0])
        for p in range(pieces):

            @pl.when(core == p % 2)
            def _():
                for copy in plane_copy(p) + line_copy(p) + final_copy(p)[1:]:
                    copy.wait_send()
                final_copy(p)[0].wait()

            @pl.when(core != p % 2)
            def _():
                pair_copy(p).wait_send()
                final_copy(p)[1].wait_recv()

        for copy in finals(1, fb_s, sb_ref) + finals(0, fa_s, sa_ref):
            copy.wait()


def attention_backward(qkv, og, lse, bid_row, bid_col, tokens, midg, o, midb, full, gains, gain2, rgrad, lb, part):
    exps, shds = part.shape[:2]
    seq, width = tokens.shape
    rows = part.shape[2]
    pairs = width // 128
    half = pairs // 2
    big = lambda *shape: pltpu.VMEM(shape, bf16)
    wide = lambda *shape: pltpu.VMEM(shape, f32)
    sems = lambda *n: pltpu.SemaphoreType.DMA(n)
    a, b = part.shape[2:], lb.shape[2:]
    return pl.pallas_call(
        functools.partial(backward_kernel, exps, shds),
        grid=(pairs,),
        in_specs=[
            pl.BlockSpec((3, seq, 128), lambda i: (0, 0, i)),
            pl.BlockSpec((seq, 128), lambda i: (0, i)),
            pl.BlockSpec((1, 8, seq), lambda i: (i, 0, 0)),
            once(bid_row.shape),
            once(bid_col.shape),
            once(tokens.shape),
            once(midg.shape),
            once(o.shape),
            pl.BlockSpec((seq, 128), lambda i: (0, i)),
            pl.BlockSpec((3, width, 128), lambda i: (0, 0, i)),
            once(gains.shape),
            once(gain2.shape),
            once(rgrad.shape),
            once(lb.shape),
            ANY,
        ],
        out_specs=[once((seq, width)), ANY, ANY, ANY, once((8, width))],
        out_shape=[
            jax.ShapeDtypeStruct((seq, width), f32),
            jax.ShapeDtypeStruct((4, rows, width), f32),
            jax.ShapeDtypeStruct((2,) + a, f32),
            jax.ShapeDtypeStruct((2,) + b, f32),
            jax.ShapeDtypeStruct((8, width), f32),
        ],
        scratch_shapes=[
            wide(seq, 128),
            wide(seq, 128),
            big(width, seq),
            big(width, seq),
            wide(seq, width),
            big(pairs, 4, width, 128),
            big(half, 4, width, 128),
            big(half, exps, 4, width // exps, 128),
            big(half, shds, 4, rows, 128),
            big(half, shds, 4, rows, 128),
            wide(half, 4, rows, 128),
            big(shds, exps, *a),
            big(shds, *a),
            big(shds, *b),
            big(shds, *a),
            big(shds, *b),
            wide(*a),
            wide(*b),
            wide(8, width),
            wide(8, width),
            wide(exps, 8, width),
            wide(shds, 8, width),
            sems(shds, exps), sems(shds, exps), sems(half), sems(half),
            sems(half, exps), sems(half, exps), sems(half, shds), sems(half, shds),
            sems(half), sems(half), sems(half),
            sems(3, shds), sems(3, shds), sems(2), sems(2), sems(2),
            pltpu.SemaphoreType.DMA, pltpu.SemaphoreType.DMA, sems(exps), sems(exps),
        ],
        compiler_params=params(("arbitrary",), collective_id=6, has_side_effects=True),
        cost_estimate=pl.CostEstimate(
            flops=80_000_000_000, bytes_accessed=30_000_000, transcendentals=12_000_000
        ),
        name="attention_backward",
    )(
        qkv, og, lse, bid_row, bid_col, tokens, midg, o, midb, full,
        gains, gain2, rgrad, lb, part,
    )


def adam_update(weight, moment, square, gradient, step_rate, shrink_rate):
    moment_next = beta_one * moment + (1.0 - beta_one) * gradient
    square_next = beta_two * square + (1.0 - beta_two) * gradient * gradient
    direction = moment_next / first_fix / (jnp.sqrt(square_next / second_fix) + adam_eps)
    return (weight - step_rate * (direction + shrink_rate * weight), moment_next, square_next)


def adam_kernel(rates, core_ref, w_ref, m_ref, v_ref, own_ref, other_ref, wo_ref, mo_ref, vo_ref):
    shape = w_ref.shape
    high = shape[-2]
    mine = jnp.full(own_ref.shape, core_ref[0], jnp.int32) == pl.program_id(0)
    gradient = jnp.where(mine, own_ref[...].astype(f32), other_ref[...].astype(f32))
    parts = [gradient[i : i + high] for i in range(0, gradient.shape[0], high)]
    gradient = jnp.concatenate(parts, axis=1).reshape(shape)
    wo_ref[...], mo_ref[...], vo_ref[...] = adam_update(
        w_ref[...], m_ref[...], v_ref[...], gradient, *rates
    )


def adam_blocks(kind, state, sums, core, grid, spec, sums_spec):
    return pl.pallas_call(
        functools.partial(adam_kernel, (learning_rates[kind], decay_rates[kind])),
        grid=grid,
        in_specs=[pl.BlockSpec(memory_space=pltpu.SMEM)] + [spec] * 3 + [sums_spec] * 2,
        out_specs=[spec] * 3,
        out_shape=[jax.ShapeDtypeStruct(state[0].shape, f32)] * 3,
        compiler_params=params(("arbitrary",) * len(grid)),
        cost_estimate=pl.CostEstimate(
            flops=20 * state[0].size, bytes_accessed=26 * state[0].size, transcendentals=0
        ),
        name="adam_blocks",
    )(core.reshape(1), *state, *sums)


def pick(array, axis, index):
    return lax.dynamic_index_in_dim(array, index, axis, keepdims=False)


def share(part, groups, core):
    if groups > 2:
        both = jnp.zeros((2,) + part.shape, f32)
        both = lax.dynamic_update_index_in_dim(both, part.astype(f32), core, 0)
        both = lax.psum(both, "grp")
        return pick(both, 0, core), pick(both, 0, 1 - core)
    return part, lax.ppermute(part, "grp", [(i, i ^ 1) for i in range(groups)])


def on_device(
    tokens_in, cotangent, block_ids, expert_ids,
    scales, moment_scales, square_scales, attend, moment_attend, square_attend,
    output, moment_output, square_output, router, moment_router, square_router,
    widener, moment_widener, square_widener, reducer, moment_reducer, square_reducer,
    experts, moment_experts, square_experts, narrower, moment_narrower, square_narrower,
):
    groups, exps, shds = (lax.axis_size(a) for a in ("grp", "exp", "shd"))
    spread = exps * shds
    core = lax.rem(lax.axis_index("grp"), 2)
    _, seq, width = tokens_in.shape
    hidden = reducer.shape[0] * spread
    experts_all = exps * experts.shape[0]
    rows, tall = output.shape[0], reducer.shape[0] // 2
    deep = width // shds
    tokens, g = tokens_in.reshape(seq, width), cotangent.reshape(seq, width)

    def packed(wide, narrow):
        wide = pick(wide.astype(bf16), 0, core)
        narrow = pick(narrow.astype(bf16).reshape(2, -1, width), 0, core)
        blocks = [
            a.reshape(a.shape[0], -1, 256).transpose(1, 0, 2).reshape(-1, 256) for a in (wide, narrow)
        ]
        return jnp.concatenate(blocks, axis=0)

    def gather(part, axes):
        wide = lax.all_gather(part, ("grp",) + axes, axis=0, tiled=False)
        return wide.reshape((groups, -1) + part.shape)[:2]

    mine = jnp.where(
        core == 0,
        attend[:2].astype(bf16),
        jnp.stack([attend[2].astype(bf16), output.astype(bf16)]),
    )
    tiny = jnp.concatenate([router, scales.T], axis=1).astype(bf16)
    tiny = jnp.pad(tiny, ((0, 0), (0, 128 - tiny.shape[1])))
    expert_weights = gather(packed(experts[0], narrower[0]), ("shd",))
    shared_pack = packed(widener, reducer)

    ids = jnp.pad(expert_ids.reshape(seq, 2).T, ((0, 6), (0, 0)), constant_values=-1)
    bid = block_ids.reshape(1, seq)
    bid_row = jnp.broadcast_to(bid, (8, seq))

    lanes = -(-CAP // 128) * 128
    full, wr, packs, g_slots, place_row, place_col, bid_col = gather_first(
        mine, tiny, shared_pack, g, ids, bid_row, exps, shds, experts_all, CAP
    )
    qkv, lse, o, mid, h2, probs, probst, gains, g_landed = attention_forward(
        tokens, bid_row, bid_col, full, wr, g_slots
    )
    shared_weights = gather(packs, ("shd",)).reshape((2, shds) + packs.shape)
    slot_rows, chosen = dispatch(h2, place_row, probst, experts_all, CAP, lanes)
    eout, back, part = routed(slot_rows, chosen, g_landed, expert_weights, hidden)
    part = lax.psum_scatter(part, "shd", scatter_dimension=0, tiled=False)
    sout, sin, part_a, part_b, ein = ffn(
        h2, g, shared_weights, back, hidden, f32, 256, "shared"
    )
    part_a = part_a.reshape(exps, shds, rows, hidden)
    part_b = part_b.reshape(exps, shds, tall, width)
    block_out, mid_grad, midb, og, gain_two, rgrad, landed_b = combine(
        mid, sout, sin, g, h2, probs, place_col, eout, ein, gains, wr, full, part_b
    )
    input_grad, sum_w, sum_a, sum_b, sum_t = attention_backward(
        qkv, og, lse, bid_row, bid_col, tokens, mid_grad, o, midb, full,
        gains, gain_two, rgrad, landed_b, part_a,
    )
    if groups > 2:
        sum_w, sum_a, sum_b, sum_t = (
            0.5 * lax.psum(v, "grp") for v in (sum_w, sum_a, sum_b, sum_t)
        )
    expert_sums = share(part, groups, core)
    wide_state = [v[0] for v in (experts, moment_experts, square_experts)]
    new_experts = adam_blocks(
        6, wide_state, expert_sums, core, (2, hidden // 512),
        pl.BlockSpec((1, deep, 512), lambda c, b: (c, 0, b)),
        pl.BlockSpec((2 * deep, 256), lambda c, b: (b, 0)),
    )
    narrow_state = [v[0] for v in (narrower, moment_narrower, square_narrower)]
    high = narrower.shape[1] // 2
    across = width // 256
    skip = hidden // 256 * deep // (across * high)
    new_narrower = adam_blocks(
        7, narrow_state, expert_sums, core, (2, 1),
        pl.BlockSpec((high, width), lambda c, b: (c, b)),
        pl.BlockSpec((across * high, 256), lambda c, b: (skip + b, 0)),
    )
    shard = lax.axis_index("exp") * shds + lax.axis_index("shd")
    sum_t = lax.dynamic_slice_in_dim(sum_t, shard * rows, rows, 1)
    grads = (
        sum_t[4:6],
        sum_w[:3],
        sum_w[3],
        sum_t[:experts_all].T,
        sum_a,
        sum_b.reshape(reducer.shape),
    )
    masters = (scales, attend, output, router, widener, reducer)
    moments = (
        moment_scales, moment_attend, moment_output, moment_router,
        moment_widener, moment_reducer,
    )
    squares = (
        square_scales, square_attend, square_output, square_router,
        square_widener, square_reducer,
    )
    results = [block_out.reshape(tokens_in.shape), input_grad.reshape(tokens_in.shape)]
    for kind in range(6):
        results.extend(
            adam_update(
                masters[kind], moments[kind], squares[kind], grads[kind],
                learning_rates[kind], decay_rates[kind],
            )
        )
    results.extend(v[None] for v in new_experts)
    results.extend(v[None] for v in new_narrower)
    return tuple(results)


def solution(mesh):
    tokens = P(("grp", "exp", "shd"), None, None)
    both = ("exp", "shd")
    kinds = (
        P(None, both), P(None, both, None), P(both, None), P(both, None),
        P(None, both, None), P(both, None), P("exp", None, "shd", None), P("exp", "shd", None),
    )
    thrice = tuple(kind for kind in kinds for _ in range(3))
    return jax.shard_map(
        on_device,
        mesh=mesh,
        in_specs=(tokens, tokens, P(("grp", "exp", "shd"), None), tokens) + thrice,
        out_specs=(tokens, tokens) + thrice,
        check_vma=False,
    )
```
